32 devices in a mesh: frames: 2 (over x), slab: 16 (over z, y, core).
Axes of the slice: x: 2, y: 2, z: 4, core: 2. Of those that a mesh axis runs over, the one named last changes fastest.
Arguments:
- x_image: float32 [2, 384, 128, 384], P(None, 'slab', 'frames'), parts along dimension 2, may hold values from -6 to 6
- residual: float32 [2, 384, 128, 384], P(None, 'slab', 'frames'), parts along dimension 2, may hold values from -6 to 6
- direction: float32 [2, 384, 128, 384], P(None, 'slab', 'frames'), parts along dimension 2, may hold values from -6 to 6
- sensitivity: float32 [2, 2, 384, 64, 384], P(None, None, 'slab'), may hold values from -5 to 5
- tile_block: int32 [256], P('slab'), may hold values from 0 to 1799
- tile_count: int32 [256], P('slab'), may hold values from 1 to 128
- tile_weight: bfloat16 [256, 128, 512], P('slab'), may hold values from -1 to 1
Outputs:
- x_next: float32 [2, 384, 128, 384], P(None, 'slab', 'frames'), parts along dimension 2
- residual_next: float32 [2, 384, 128, 384], P(None, 'slab', 'frames'), parts along dimension 2
- direction_next: float32 [2, 384, 128, 384], P(None, 'slab', 'frames'), parts along dimension 2
The draws below stay inside these ranges and needn't reach their ends.
There are 2 independent parts, one for each index of `frames`. The reference program is written for one: setup_inputs(seed, part) draws one part's arguments, and reference() takes and returns one part's arrays. A program takes and returns all parts, laid end to end along the dimension named above; an argument that names none is the same for every part. Nothing has to cross between parts.
Inputs may be any that keep to these rules, and one draw needn't show every extreme that they name: `tile_block`: tile t belongs to slab t // 16 and names a block of that slab; several tiles may name one block. `tile_count`: samples of a tile at and beyond its count are unused.
All inputs are finite; a program needn't handle non-finite values.
Results may differ from the reference program's by a relative error of at most 0.00065.
The reference program's roundings to bfloat16 on the way (of `picked` and `samples`) count: a program that leaves them out, or rounds other values in their place, can miss the bound.
Values sent between devices are 32-bit elements; how exact they have to be, the bound alone decides.
No kernel may reach another device: no remote copies, remote signals or barrier semaphores. Data moves between devices by JAX's collectives and lax.ppermute only.
A program may use at most 192 MiB of HBM per device.

```python
import math
import jax
import jax.numpy as jnp
from jax import lax

NX = 384
NY = 384
GX = 480
GY = 480
PLANES = 64
COILS = 2
TS = 128
TC = 512
TILES_DEV = 16
LINES = 1920
BLOCKS = 1800
TILES = 256
N_SLAB = 16


def with_ends(array, key, low, largest):
    dims = array.shape
    place = [jax.random.randint(jax.random.fold_in(key, axis), (), 0, dims[axis]) for axis in range(len(dims))]
    array = array.at[tuple(place)].set(low)
    longest = dims.index(max(dims))
    place[longest] = (place[longest] + 1) % dims[longest]
    return array.at[tuple(place)].set(largest)


def block_scale(stream_key, extent, pieces, low, high):
    gain, own = 1.0, jax.random.fold_in(stream_key, 6)
    for position, parts in pieces:
        draws = jnp.exp(jax.random.uniform(jax.random.fold_in(own, position), (parts,), jnp.float32, low / len(pieces), high / len(pieces)))
        gain = gain * jnp.repeat(draws, extent[position] // parts).reshape([-1 if axis == position else 1 for axis in range(len(extent))])
    return gain


def noise(key, shape, scale, limit, split=(), held_as=jnp.bfloat16):
    gain = block_scale(key, shape, split, -0.22, 0.18) if split else 1.0
    result = jax.random.normal(key, shape, jnp.float32) * scale * gain
    return jnp.minimum(jnp.maximum(result, -limit), limit).astype(held_as)


def setup_inputs(seed: int = 0, part: int = 0) -> dict:
    key_list = jax.random.split(jax.random.key(seed), 8)
    part_keys = jax.random.split(jax.random.fold_in(key_list[7], part), 8)
    x_image = noise(part_keys[0], (2, NX, PLANES, NY), 1.0, 6.0, ((1, 16),), jnp.float32)
    residual = noise(part_keys[1], (2, NX, PLANES, NY), 1.0, 6.0, ((1, 16),), jnp.float32)
    direction = noise(part_keys[2], (2, NX, PLANES, NY), 1.0, 6.0, ((1, 16),), jnp.float32)
    sensitivity = noise(key_list[3], (2, COILS, NX, PLANES, NY), 0.7, 5.0, ((2, 16),), jnp.float32)
    tile_block = with_ends(jax.random.randint(key_list[4], (TILES,), 0, BLOCKS), jax.random.fold_in(key_list[4], 1), 0, BLOCKS - 1).astype(jnp.int32)
    tile_count = with_ends(jax.random.randint(key_list[5], (TILES,), 1, TS + 1), jax.random.fold_in(key_list[5], 1), 1, TS).astype(jnp.int32)
    tile_weight = noise(key_list[6], (TILES, TS, TC), (TS // 4) ** -0.5, 1.0, ((0, 16),))
    return {"x_image": x_image, "residual": residual, "direction": direction, "sensitivity": sensitivity, "tile_block": tile_block, "tile_count": tile_count, "tile_weight": tile_weight}


DAMPING = 0.1
HIGHEST = lax.Precision.HIGHEST

def dft_table(size_in, size_out):
    out_index = jnp.arange(size_out, dtype=jnp.int32)[:, None]
    in_index = jnp.arange(size_in, dtype=jnp.int32)[None, :]
    phase_angle = (out_index * in_index % size_out).astype(jnp.float32) * (2.0 * math.pi / size_out)
    scaling = 1.0 / math.sqrt(size_out)
    cosine = jnp.cos(phase_angle) * scaling
    sine_part = jnp.sin(phase_angle) * scaling
    upper_rows = jnp.stack([cosine, sine_part], axis=1)
    lower_rows = jnp.stack([-sine_part, cosine], axis=1)
    return jnp.stack([upper_rows, lower_rows], axis=0)

def grid_tiles(cell_rows, block_ids, sample_count, weights):
    block_total = cell_rows.shape[1]
    samples_tile = weights.shape[1]
    picked = jnp.take(cell_rows, block_ids, axis=1).astype(jnp.bfloat16)
    samples = jnp.einsum('tsc,ktc->kts', weights.astype(jnp.float32), picked.astype(jnp.float32), precision=HIGHEST)
    live_mask = jnp.arange(samples_tile, dtype=jnp.int32)[None, :] < sample_count[:, None]
    samples = jnp.where(live_mask[None], samples, 0.0).astype(jnp.bfloat16)
    spread_back = jnp.einsum('tsc,kts->ktc', weights.astype(jnp.float32), samples.astype(jnp.float32), precision=HIGHEST)
    block_hit = (block_ids[:, None] == jnp.arange(block_total, dtype=jnp.int32)[None, :]).astype(jnp.float32)
    return jnp.einsum('tb,ktc->kbc', block_hit, spread_back, precision=HIGHEST)

def reference(x_image, residual, direction, sensitivity, tile_block, tile_count, tile_weight):
    y_table = dft_table(NY, GY)
    x_table = dft_table(NX, GX)
    sens_re, sens_im = (sensitivity[0], sensitivity[1])
    dir_re, dir_im = (direction[0][None], direction[1][None])
    coil_image = jnp.stack([sens_re * dir_re - sens_im * dir_im, sens_re * dir_im + sens_im * dir_re])
    y_done = jnp.einsum('agbn,bcxpn->acxpg', y_table, coil_image, precision=HIGHEST)
    line_data = y_done.reshape(2, COILS, NX, PLANES * GY)
    grid_data = jnp.einsum('agbn,bcnl->acgl', x_table, line_data, precision=HIGHEST)
    slab_cells = grid_data.reshape(2 * COILS, GX, N_SLAB, LINES).transpose(2, 0, 1, 3)
    slab_cells = slab_cells.reshape(N_SLAB, 2 * COILS, BLOCKS, TC)
    block_all = tile_block.reshape(N_SLAB, TILES_DEV)
    count_all = tile_count.reshape(N_SLAB, TILES_DEV)
    weight_all = tile_weight.reshape(N_SLAB, TILES_DEV, TS, TC)

    def one_slab(operands):
        return grid_tiles(operands[0], operands[1], operands[2], operands[3])
    spread = lax.map(one_slab, (slab_cells, block_all, count_all, weight_all))
    spread = spread.reshape(N_SLAB, 2 * COILS, GX, LINES).transpose(1, 2, 0, 3)
    spread = spread.reshape(2, COILS, GX, PLANES * GY)
    x_adjoint = jnp.einsum('agbn,acgl->bcnl', x_table, spread, precision=HIGHEST)
    x_adjoint = x_adjoint.reshape(2, COILS, NX, PLANES, GY)
    back = jnp.einsum('agbn,acxpg->bcxpn', y_table, x_adjoint, precision=HIGHEST)
    val_re, val_im = (back[0], back[1])
    comb_re = lax.optimization_barrier(jnp.sum(sens_re * val_re + sens_im * val_im, axis=0))
    comb_im = lax.optimization_barrier(jnp.sum(sens_re * val_im - sens_im * val_re, axis=0))
    image_ap = jnp.stack([comb_re, comb_im]) + DAMPING * direction
    norm_old = jnp.sum(residual * residual)
    curvature = jnp.sum(direction * image_ap)
    step_size = norm_old / curvature
    x_next = x_image + step_size * direction
    residual_next = residual - step_size * image_ap
    norm_new = jnp.sum(residual_next * residual_next)
    direction_next = residual_next + norm_new / norm_old * direction
    return (x_next, residual_next, direction_next)
```

```python
import math

import jax
import jax.numpy as jnp
import ml_dtypes
import numpy as np
from jax import lax
from jax.experimental import pallas as pl
from jax.experimental.pallas import tpu as pltpu
from jax.sharding import PartitionSpec as P

GX = 480
GY = 480
DAMPING = 0.1
HIGHEST = lax.Precision.HIGHEST
F32 = jnp.float32
BF16 = jnp.bfloat16
VMEM_LIMIT = 56 * 1024 * 1024
FIELDS = 8


def dft(out_index, in_index, size, scaled=True):
    angle = (out_index[:, None] * in_index[None, :] % size) * (2.0 * math.pi / size)
    scale = 1.0 / math.sqrt(size) if scaled else 1.0
    return np.cos(angle) * scale, np.sin(angle) * scale


def table_parts(table, count):
    parts = []
    for _ in range(count):
        part = table.astype(ml_dtypes.bfloat16)
        parts.append(part)
        table = table - part.astype(np.float64)
    return np.stack(parts)


def split(value, count):
    parts = []
    for step in range(count):
        part = value.astype(BF16)
        parts.append(part)
        if step + 1 < count:
            value = value - part.astype(F32)
    return parts


def dot(a, b):
    return lax.dot_general(a, b, (((1,), (0,)), ((), ())), preferred_element_type=F32)


def six_products(lhs, rhs):
    rows = lhs[0].shape[0]
    first = dot(jnp.concatenate(lhs, axis=0), rhs[0])
    second = dot(jnp.concatenate(lhs[:2], axis=0), rhs[1])
    third = dot(lhs[0], rhs[2])
    small = first[2 * rows :] + second[rows:] + third
    return first[:rows] + (first[rows : 2 * rows] + second[:rows] + small)


def params():
    return pltpu.CompilerParams(vmem_limit_bytes=VMEM_LIMIT)


def coil_kernel(sens_ref, dir_ref, res_ref, out_ref, sums_ref):
    coils, rows, planes, width = sens_ref.shape[1:]
    half = rows * planes
    chunk = max(16 // planes, 1)

    @pl.when(pl.program_id(0) == 0)
    def _():
        sums_ref[...] = jnp.zeros(sums_ref.shape, F32)

    def step(index, carry):
        at = pl.ds(index * chunk, chunk)
        to = index * chunk * planes
        d_re, d_im = dir_ref[0, at], dir_ref[1, at]
        r_re, r_im = res_ref[0, at], res_ref[1, at]
        sums_ref[0] += jnp.sum(r_re * r_re + r_im * r_im, axis=0)
        sums_ref[1] += jnp.sum(d_re * d_re + d_im * d_im, axis=0)
        for coil in range(coils):
            s_re, s_im = sens_ref[0, coil, at], sens_ref[1, coil, at]
            pair = (s_re * d_re - s_im * d_im, s_re * d_im + s_im * d_re)
            for ri, value in enumerate(pair):
                value = value.reshape(chunk * planes, width)
                where = pl.ds(pl.multiple_of(ri * half + to, 16), chunk * planes)
                for number, part in enumerate(split(value, 3)):
                    out_ref[0, number, where, coil * width : (coil + 1) * width] = part
        return carry

    lax.fori_loop(0, rows // chunk, step, 0)


def coil_images(sens, direction, residual, planes):
    _, coils, rows, total, width = sens.shape
    groups = total // planes
    depth = 2 * rows * planes
    return pl.pallas_call(
        coil_kernel,
        grid=(groups,),
        in_specs=[
            pl.BlockSpec((2, coils, rows, planes, width), lambda i: (0, 0, 0, i, 0)),
            pl.BlockSpec((2, rows, planes, width), lambda i: (0, 0, i, 0)),
            pl.BlockSpec((2, rows, planes, width), lambda i: (0, 0, i, 0)),
        ],
        out_specs=[
            pl.BlockSpec((1, 3, depth, coils * width), lambda i: (i, 0, 0, 0)),
            pl.BlockSpec((2, planes, width), lambda i: (0, 0, 0)),
        ],
        out_shape=[
            jax.ShapeDtypeStruct((groups, 3, depth, coils * width), BF16),
            jax.ShapeDtypeStruct((2, planes, width), F32),
        ],
        compiler_params=params(),
        name="coil_images",
    )(sens, direction, residual)


def row_matrix(info, table_ref, planes, parts):
    rows = info.shape[0]
    half = rows // 2
    depth = table_ref.shape[3]
    hot = lax.broadcasted_iota(jnp.int32, (rows, GX), 1) == info[:, 0:1]
    hot = jnp.where(hot, 1.0, 0.0)
    hot_low = hot.astype(BF16)
    live = lax.broadcasted_iota(jnp.int32, (rows, depth), 1) % planes == info[:, 1:2]
    matrix = []
    for part in range(parts):
        upper = jnp.where(live, dot(hot_low, table_ref[part, 0]), 0.0)
        lower = jnp.where(live, dot(hot_low, table_ref[part, 1]), 0.0)
        stack = [upper[:half], lower[:half], upper[half:], lower[half:]]
        matrix.append(jnp.concatenate(stack, axis=0).astype(BF16))
    return matrix, hot


def rows_kernel(planes, me_ref, info_ref, image_ref, table_ref, turn_ref, keep_ref, send_ref):
    count = info_ref.shape[2]
    info = info_ref[0].reshape(2 * count, FIELDS)
    matrix, hot = row_matrix(info, table_ref, planes, 3)
    turn = jnp.dot(hot, turn_ref[...], precision=HIGHEST, preferred_element_type=F32)
    cos, sin = turn[:, 0:1], turn[:, 1:2]
    out = six_products(matrix, [image_ref[0, part] for part in range(3)])
    for slab, ref in enumerate((keep_ref, send_ref)):
        re = out[2 * slab * count : (2 * slab + 1) * count]
        im = out[(2 * slab + 1) * count : (2 * slab + 2) * count]
        c = cos[slab * count : (slab + 1) * count]
        s = sin[slab * count : (slab + 1) * count]
        ref[0, :count] = c * re + s * im
        ref[0, count:] = c * im - s * re


def partial_rows(me, info, images, table, turn, planes, slabs_group):
    pairs, _, count, _ = info.shape
    _, _, depth, width = images.shape
    whole = jax.ShapeDtypeStruct((pairs, 2 * count, width), F32)
    block = pl.BlockSpec((1, 2 * count, width), lambda q, me: (q, 0, 0))
    return pl.pallas_call(
        lambda *refs: rows_kernel(planes, *refs),
        grid_spec=pltpu.PrefetchScalarGridSpec(
            num_scalar_prefetch=1,
            grid=(pairs,),
            in_specs=[
                pl.BlockSpec((1, 2, count, FIELDS), lambda q, me: (q, 0, 0, 0)),
                pl.BlockSpec(
                    (1, 3, depth, width),
                    lambda q, me: (lax.bitwise_xor(2 * q, me[0]) // slabs_group, 0, 0, 0),
                ),
                pl.BlockSpec(table.shape, lambda q, me: (0, 0, 0, 0)),
                pl.BlockSpec(turn.shape, lambda q, me: (0, 0)),
            ],
            out_specs=[block, block],
        ),
        out_shape=[whole, whole],
        compiler_params=params(),
        name="partial_rows",
    )(me, info, images, table, turn)


def start_turn(info_ref, start_ref):
    pairs, _, count, _ = info_ref.shape
    info = info_ref[...].reshape(pairs * count, FIELDS)
    starts = start_ref.shape[0]
    hot = lax.broadcasted_iota(jnp.int32, (pairs * count, starts), 1) == info[:, 2:3]
    turn = jnp.dot(
        jnp.where(hot, 1.0, 0.0), start_ref[...], precision=HIGHEST, preferred_element_type=F32
    )
    width = turn.shape[1] // 2
    return info, turn[:, :width], turn[:, width:]


def segment_mask(info, cells, segment):
    at = lax.broadcasted_iota(jnp.int32, (info.shape[0], 2 * cells), 1) % cells
    return (at >= info[:, 3:4]) & (at < info[:, 3:4] + segment)


def cells_kernel(tiles, segment, keep_ref, got_ref, info_ref, start_ref, table_ref, *out_refs):
    pairs, count, _ = keep_ref.shape
    count = count // 2
    cells = out_refs[0].shape[2] // 2
    info, cos, sin = start_turn(info_ref, start_ref)
    width = cos.shape[1]
    values = []
    for coil in range(len(out_refs)):
        lanes = slice(coil * width, (coil + 1) * width)
        both = keep_ref[:, :, lanes] + got_ref[:, :, lanes]
        re = both[:, :count].reshape(pairs * count, width)
        im = both[:, count:].reshape(pairs * count, width)
        values.append(jnp.concatenate([cos * re + sin * im, cos * im - sin * re], axis=1))
    value = split(jnp.concatenate(values, axis=0), 3)
    out = six_products(value, [table_ref[part] for part in range(3)])
    mask = segment_mask(info, cells, segment)
    for coil, ref in enumerate(out_refs):
        mine = jnp.where(mask, out[coil * pairs * count : (coil + 1) * pairs * count], 0.0)
        mine = mine.reshape(pairs, count // tiles, tiles, 2 * cells)
        ref[...] = jnp.sum(mine, axis=1)


def row_cells(keep, got, info, start, table, tiles, segment, coils, chunk):
    pairs, double, width = keep.shape
    lines = table.shape[2]
    rows = pl.BlockSpec((chunk, double, width), lambda i: (i, 0, 0))
    whole = jax.ShapeDtypeStruct((pairs, tiles, lines), F32)
    return pl.pallas_call(
        lambda *refs: cells_kernel(tiles, segment, *refs),
        grid=(pairs // chunk,),
        in_specs=[
            rows,
            rows,
            pl.BlockSpec((chunk, 1, double // 2, FIELDS), lambda i: (i, 0, 0, 0)),
            pl.BlockSpec(start.shape, lambda i: (0, 0)),
            pl.BlockSpec(table.shape, lambda i: (0, 0, 0), pipeline_mode=pl.Buffered(1)),
        ],
        out_specs=[pl.BlockSpec((chunk, tiles, lines), lambda i: (i, 0, 0))] * coils,
        out_shape=[whole] * coils,
        compiler_params=params(),
        name="row_cells",
    )(keep, got, info, start, table)


def adjoint_kernel(tiles, segment, coils, *refs):
    cell_refs, (info_ref, start_ref, table_ref, out_ref) = refs[:coils], refs[coils:]
    pairs, _, count, _ = info_ref.shape
    cells = cell_refs[0].shape[2] // 2
    info, cos, sin = start_turn(info_ref, start_ref)
    width = cos.shape[1]
    mask = segment_mask(info, cells, segment)
    values = []
    for ref in cell_refs:
        wide = jnp.concatenate([ref[...][:, None]] * (count // tiles), axis=1)
        values.append(jnp.where(mask, wide.reshape(pairs * count, 2 * cells), 0.0))
    rows = coils * pairs * count
    high, low = split(jnp.concatenate(values, axis=0), 2)
    first = dot(jnp.concatenate([high, low], axis=0), table_ref[0])
    out = first[:rows] + (first[rows:] + dot(high, table_ref[1]))
    for coil in range(coils):
        mine = out[coil * pairs * count : (coil + 1) * pairs * count]
        re, im = mine[:, :width], mine[:, width:]
        lanes = slice(coil * width, (coil + 1) * width)
        out_ref[:, :count, lanes] = (cos * re - sin * im).reshape(pairs, count, width)
        out_ref[:, count:, lanes] = (cos * im + sin * re).reshape(pairs, count, width)


def adjoint_rows(spread, info, start, table, tiles, segment, chunk):
    coils = len(spread)
    pairs, _, lines = spread[0].shape
    count = info.shape[2]
    width = coils * table.shape[2] // 2
    return pl.pallas_call(
        lambda *refs: adjoint_kernel(tiles, segment, coils, *refs),
        grid=(pairs // chunk,),
        in_specs=[pl.BlockSpec((chunk, tiles, lines), lambda i: (i, 0, 0))] * coils
        + [
            pl.BlockSpec((chunk, 1, count, FIELDS), lambda i: (i, 0, 0, 0)),
            pl.BlockSpec(start.shape, lambda i: (0, 0)),
            pl.BlockSpec(table.shape, lambda i: (0, 0, 0), pipeline_mode=pl.Buffered(1)),
        ],
        out_specs=pl.BlockSpec((chunk, 2 * count, width), lambda i: (i, 0, 0)),
        out_shape=jax.ShapeDtypeStruct((pairs, 2 * count, width), F32),
        compiler_params=params(),
        name="adjoint_rows",
    )(*spread, info, start, table)


def tiles_kernel(coils, *refs):
    count_ref, cell_refs = refs[0], refs[1 : 1 + coils]
    weight_ref, out_refs, dot_ref = refs[1 + coils], refs[2 + coils : 2 + 2 * coils], refs[-1]
    tiles, samples, cells = weight_ref.shape
    total = jnp.zeros((2 * coils, cells), F32)
    for tile in range(tiles):
        grid = jnp.concatenate(
            [
                ref[tile : tile + 1, ri * cells : (ri + 1) * cells]
                for ref in cell_refs
                for ri in range(2)
            ],
            axis=0,
        )
        weight = weight_ref[tile]
        found = lax.dot_general(
            grid.astype(BF16), weight, (((1,), (1,)), ((), ())), preferred_element_type=F32
        )
        live = lax.broadcasted_iota(jnp.int32, found.shape, 1) < count_ref[tile]
        found = jnp.where(live, found, 0.0).astype(BF16)
        spread = dot(found, weight)
        total += grid * spread
        for coil, ref in enumerate(out_refs):
            for ri in range(2):
                row = 2 * coil + ri
                ref[tile : tile + 1, ri * cells : (ri + 1) * cells] = spread[row : row + 1]
    dot_ref[...] = total


def run_tiles(count, cells, weight):
    coils = len(cells)
    lines = cells[0].shape[1]
    vmem = pl.BlockSpec(memory_space=pltpu.VMEM)
    whole = jax.ShapeDtypeStruct(cells[0].shape, F32)
    *spread, total = pl.pallas_call(
        lambda *refs: tiles_kernel(coils, *refs),
        in_specs=[pl.BlockSpec(memory_space=pltpu.SMEM)] + [vmem] * (coils + 1),
        out_specs=[vmem] * (coils + 1),
        out_shape=[whole] * coils + [jax.ShapeDtypeStruct((2 * coils, lines // 2), F32)],
        compiler_params=params(),
        name="tiles",
    )(count, *cells, weight)
    return spread, total


def finish_kernel(
    planes, depth_pairs, me_ref, step_ref, info_ref, mine_ref, got_ref, sens_ref, dir_ref, res_ref,
    table_ref, turn_ref, out_ref, norm_ref, *scratch,
):
    count = info_ref.shape[2]
    coils, rows, _, width = sens_ref.shape[1:]
    half = rows * planes
    group, pair = pl.program_id(0), pl.program_id(1)
    info = info_ref[0].reshape(2 * count, FIELDS)
    matrix, hot = row_matrix(info, table_ref, planes, 2)
    turn = jnp.dot(hot, turn_ref[...], precision=HIGHEST, preferred_element_type=F32)
    values = []
    for slab, ref in enumerate((mine_ref, got_ref)):
        re, im = ref[0, :count], ref[0, count:]
        c = turn[slab * count : (slab + 1) * count, 0:1]
        s = turn[slab * count : (slab + 1) * count, 1:2]
        values += [c * re - s * im, c * im + s * re]
    high, low = split(jnp.concatenate(values, axis=0), 2)
    left = jnp.concatenate([matrix[0], matrix[1], matrix[0]], axis=0)
    right = jnp.concatenate([high, high, low], axis=0)
    back = lax.dot_general(left, right, (((0,), (0,)), ((), ())), preferred_element_type=F32)

    @pl.when((group == 0) & (pair == 0))
    def _():
        norm_ref[...] = jnp.zeros(norm_ref.shape, F32)

    def combine(back):
        direction = [dir_ref[ri].reshape(half, width) for ri in range(2)]
        total = [DAMPING * direction[0], DAMPING * direction[1]]
        for coil in range(coils):
            lanes = slice(coil * width, (coil + 1) * width)
            v_re, v_im = back[:half, lanes], back[half:, lanes]
            s_re = sens_ref[0, coil].reshape(half, width)
            s_im = sens_ref[1, coil].reshape(half, width)
            total[0] += s_re * v_re + s_im * v_im
            total[1] += s_re * v_im - s_im * v_re
        squares = 0.0
        for ri in range(2):
            value = res_ref[ri].reshape(half, width) - step_ref[0] * total[ri]
            out_ref[ri] = value.reshape(rows, planes, width)
            squares = squares + jnp.sum((value * value).reshape(rows, planes, width), axis=0)
        norm_ref[...] += squares

    if depth_pairs == 1:
        combine(back)
    else:
        sum_ref = scratch[0]

        @pl.when(pair == 0)
        def _():
            sum_ref[...] = back

        @pl.when(pair > 0)
        def _():
            sum_ref[...] += back

        @pl.when(pair == depth_pairs - 1)
        def _():
            combine(sum_ref[...])


def finish(me, step, info, mine, got, sens, direction, residual, table, turn, planes, slabs_group):
    _, coils, rows, total, width = sens.shape
    pairs, _, count, _ = info.shape
    groups, deep = total // planes, slabs_group // 2
    wide = coils * width

    def place(i, j, me):
        return lax.bitwise_xor(i * slabs_group, me[0]) // slabs_group

    row_block = pl.BlockSpec((1, 2 * count, wide), lambda i, j, me: (i * deep + j, 0, 0))
    image = pl.BlockSpec((2, rows, planes, width), lambda i, j, me: (0, 0, place(i, j, me), 0))
    return pl.pallas_call(
        lambda *refs: finish_kernel(planes, deep, *refs),
        grid_spec=pltpu.PrefetchScalarGridSpec(
            num_scalar_prefetch=1,
            grid=(groups, deep),
            in_specs=[
                pl.BlockSpec(memory_space=pltpu.SMEM),
                pl.BlockSpec(
                    (1, 2, count, FIELDS), lambda i, j, me: (i * deep + j, 0, 0, 0)
                ),
                row_block,
                row_block,
                pl.BlockSpec(
                    (2, coils, rows, planes, width),
                    lambda i, j, me: (0, 0, 0, place(i, j, me), 0),
                ),
                image,
                image,
                pl.BlockSpec(table.shape, lambda i, j, me: (0, 0, 0, 0)),
                pl.BlockSpec(turn.shape, lambda i, j, me: (0, 0)),
            ],
            out_specs=[image, pl.BlockSpec((planes, width), lambda i, j, me: (0, 0))],
            scratch_shapes=[pltpu.VMEM((2 * rows * planes, wide), F32)] if deep > 1 else [],
        ),
        out_shape=[
            jax.ShapeDtypeStruct(residual.shape, F32),
            jax.ShapeDtypeStruct((planes, width), F32),
        ],
        compiler_params=params(),
        name="finish",
    )(me, step, info, mine, got, sens, direction, residual, table, turn)


def swap(value, bit, slabs):
    return lax.ppermute(value, "slab", [(i, i ^ bit) for i in range(slabs)])


def sum_scatter(value, bits, slabs):
    dims = value.shape[1:]
    value = value.reshape((2,) * len(bits) + dims)
    left = sorted(bits, reverse=True)
    for bit in bits:
        axis = left.index(bit)
        left.pop(axis)
        keep = lax.index_in_dim(value, 0, axis, keepdims=False)
        send = lax.index_in_dim(value, 1, axis, keepdims=False)
        value = keep + swap(send, bit, slabs)
    return value


def gather(value, bits, slabs):
    dims = value.shape
    have = []
    for bit in bits:
        other = swap(value, bit, slabs)
        axis = sum(1 for b in have if b > bit)
        value = jnp.stack([value, other], axis=axis)
        have.append(bit)
    return value.reshape((2 ** len(bits),) + dims)


def body(x_image, residual, direction, sensitivity, tile_block, tile_count, tile_weight):
    _, coils, rows, plane_count, ny = sensitivity.shape
    tiles, _, cells = tile_weight.shape
    slabs = lax.axis_size("slab")
    me = lax.axis_index("slab")
    lines = plane_count * GY // slabs
    segment = min(lines, GY)
    per_gx = lines // segment
    unit = math.gcd(cells, segment)
    segments = -(-(segment - unit + cells) // segment)
    planes = 8 if rows % 2 == 0 else 16
    slabs_group = planes * GY // lines
    pairs = slabs // 2
    bits = [1 << i for i in range(slabs.bit_length() - 1)]

    first = tile_block * cells
    start = first % segment
    base = (me * lines) % GY
    info = []
    for k in range(segments):
        row = jnp.minimum(first // segment + k, GX * per_gx - 1)
        plane = (me * lines + (row % per_gx) * segment) // GY
        turn = (base + start - segment * k) % GY // unit
        fields = [row // per_gx, plane % planes, turn, segment * k - start]
        info.append(jnp.stack(fields + [jnp.zeros_like(row)] * (FIELDS - len(fields)), axis=1))
    info = jnp.concatenate(info, axis=0)
    info = gather(info, bits, slabs).reshape(pairs, 2, segments * tiles, FIELDS)

    x_cos, x_sin = dft(np.arange(GX), np.repeat(np.arange(rows), planes), GX)
    x_table = np.stack([np.hstack([x_cos, x_sin]), np.hstack([-x_sin, x_cos])])
    x_table = jnp.asarray(table_parts(x_table, 3))
    y_cos, y_sin = dft(np.arange(ny), np.arange(cells), GY)
    y_table = np.vstack([np.hstack([y_cos, -y_sin]), np.hstack([y_sin, y_cos])])
    y_forward = jnp.asarray(table_parts(y_table, 3))
    y_back = jnp.asarray(table_parts(y_table.T, 2))
    start_table = np.hstack(dft(np.arange(GY // unit) * unit, np.arange(ny), GY, False))
    start_table = np.pad(start_table, ((0, -start_table.shape[0] % 8), (0, 0)))
    start_table = jnp.asarray(start_table.astype(np.float32))
    angle = (jnp.arange(GX, dtype=jnp.int32) * (me * rows) % GX).astype(F32) * (2 * math.pi / GX)
    turn = jnp.stack([jnp.cos(angle), jnp.sin(angle)], axis=1)
    turn = jnp.pad(turn, ((0, 0), (0, 126)))
    me_array = me.astype(jnp.int32)[None]

    images, sums = coil_images(sensitivity, direction, residual, planes)
    keep, send = partial_rows(me_array, info, images, x_table, turn, planes, slabs_group)
    got = swap(send, 1, slabs)
    chunk = min(pairs, 4)
    grid = row_cells(
        keep, got, info, start_table, y_forward, tiles, segment, coils, chunk
    )
    high_bits = bits[1:]
    orders = [high_bits[c % len(high_bits) :] + high_bits[: c % len(high_bits)] for c in range(coils)]
    grid = [sum_scatter(value, order, slabs) for value, order in zip(grid, orders)]

    spread, products = run_tiles(tile_count, grid, tile_weight)

    local = jnp.sum(sums, axis=(1, 2))
    scalars = jnp.stack([local[0], jnp.sum(products) + DAMPING * local[1]])
    for bit in bits:
        scalars = scalars + swap(scalars, bit, slabs)
    norm_old = scalars[0]
    step_size = norm_old / scalars[1]

    spread = [gather(value, order[::-1], slabs) for value, order in zip(spread, orders)]
    mine = adjoint_rows(spread, info, start_table, y_back, tiles, segment, chunk)
    other = swap(mine, 1, slabs)
    residual_next, squares = finish(
        me_array, step_size[None], info, mine, other, sensitivity, direction, residual, x_table, turn,
        planes, slabs_group,
    )
    norm_new = jnp.sum(squares)[None]
    for bit in bits:
        norm_new = norm_new + swap(norm_new, bit, slabs)
    x_next = x_image + step_size * direction
    direction_next = residual_next + norm_new[0] / norm_old * direction
    return (x_next, residual_next, direction_next)


def solution(mesh):
    image = P(None, "slab", "frames", None)
    placed = (image, image, image, P(None, None, "slab", None, None)) + (
        P("slab"),
        P("slab"),
        P("slab", None, None),
    )
    return jax.shard_map(
        body, mesh=mesh, in_specs=placed, out_specs=(image, image, image), check_vma=False
    )
```

```python
import math

import jax
import jax.numpy as jnp
import ml_dtypes
import numpy as np
from jax import lax
from jax.experimental import pallas as pl
from jax.experimental.pallas import tpu as pltpu
from jax.sharding import PartitionSpec as P

GX = 480
GY = 480
DAMPING = 0.1
HIGHEST = lax.Precision.HIGHEST
F32 = jnp.float32
BF16 = jnp.bfloat16
MIB = 1024 * 1024
FIELDS = 8


def dft(out_index, in_index, size, scaled=True):
    angle = (out_index[:, None] * in_index[None, :] % size) * (2.0 * math.pi / size)
    scale = 1.0 / math.sqrt(size) if scaled else 1.0
    return np.cos(angle) * scale, np.sin(angle) * scale


def table_parts(table, count):
    parts = []
    for _ in range(count):
        part = table.astype(ml_dtypes.bfloat16)
        parts.append(part)
        table = table - part.astype(np.float64)
    return np.stack(parts)


def split(value, count):
    parts = []
    for step in range(count):
        part = value.astype(BF16)
        parts.append(part)
        if step + 1 < count:
            value = value - part.astype(F32)
    return parts


def dot(a, b):
    return lax.dot_general(a, b, (((1,), (0,)), ((), ())), preferred_element_type=F32)


def six_products(lhs, rhs):
    rows = lhs[0].shape[0]
    first = dot(jnp.concatenate(lhs, axis=0), rhs[0])
    second = dot(jnp.concatenate(lhs[:2], axis=0), rhs[1])
    third = dot(lhs[0], rhs[2])
    small = first[2 * rows :] + second[rows:] + third
    return first[:rows] + (first[rows : 2 * rows] + second[:rows] + small)


def params(mib):
    return pltpu.CompilerParams(vmem_limit_bytes=mib * MIB)


def squares_kernel(value_ref, out_ref):
    @pl.when(pl.program_id(0) == 0)
    def _():
        out_ref[...] = jnp.zeros(out_ref.shape, F32)

    value = value_ref[...]
    out_ref[...] += jnp.sum(value * value, axis=0)


def squares(value):
    value = value.reshape((-1,) + value.shape[2:])
    rows, planes, width = value.shape
    step = math.gcd(rows, 8)
    return pl.pallas_call(
        squares_kernel,
        grid=(rows // step,),
        in_specs=[pl.BlockSpec((step, planes, width), lambda i: (i, 0, 0))],
        out_specs=pl.BlockSpec((planes, width), lambda i: (0, 0)),
        out_shape=jax.ShapeDtypeStruct((planes, width), F32),
        compiler_params=params(48),
        name="squares",
    )(value)


def x_kernel(sums_ref, x_ref, dir_ref, *refs):
    step = sums_ref[0:1, 0:1] / sums_ref[1:2, 0:1]
    refs[-1][...] = x_ref[...] + step * dir_ref[...]


def x_update(sums, x_image, direction, piece, pieces, before):
    dims = x_image.shape
    flat = (-1,) + dims[2:]
    rows = dims[0] * dims[1] // pieces
    step = math.gcd(rows, 4)
    given = [] if before is None else [before.reshape(flat)]
    block = pl.BlockSpec((step,) + dims[2:], lambda i: (piece * (rows // step) + i, 0, 0))
    out = pl.pallas_call(
        x_kernel,
        grid=(rows // step,),
        in_specs=[pl.BlockSpec(sums.shape, lambda i: (0, 0)), block, block]
        + [pl.BlockSpec(memory_space=pl.ANY)] * len(given),
        out_specs=block,
        out_shape=jax.ShapeDtypeStruct((dims[0] * dims[1],) + dims[2:], F32),
        input_output_aliases={3: 0} if given else {},
        compiler_params=params(48),
        name="x_update",
    )(sums, x_image.reshape(flat), direction.reshape(flat), *given)
    return out.reshape(dims)


def direction_kernel(sums_ref, one_ref, two_ref, res_ref, dir_ref, out_ref):
    ratio = (one_ref[0:1, 0:1] + two_ref[0:1, 0:1]) / sums_ref[0:1, 0:1]
    out_ref[...] = res_ref[...] + ratio * dir_ref[...]


def direction_update(sums, one, two, residual, direction):
    dims = residual.shape
    flat = (-1,) + dims[2:]
    rows = dims[0] * dims[1]
    step = math.gcd(rows, 4)
    block = pl.BlockSpec((step,) + dims[2:], lambda i: (i, 0, 0))
    small = pl.BlockSpec(sums.shape, lambda i: (0, 0))
    out = pl.pallas_call(
        direction_kernel,
        grid=(rows // step,),
        in_specs=[small, small, small, block, block],
        out_specs=block,
        out_shape=jax.ShapeDtypeStruct((rows,) + dims[2:], F32),
        compiler_params=params(32),
        name="direction_update",
    )(sums, one, two, residual.reshape(flat), direction.reshape(flat))
    return out.reshape(dims)


def row_matrix(info, table_ref, planes, parts):
    pairs, count, _ = info.shape
    half = count // 2
    info = info.reshape(pairs * count, FIELDS)
    depth = table_ref.shape[3]
    hot = lax.broadcasted_iota(jnp.int32, (pairs * count, GX), 1) == info[:, 0:1]
    hot = jnp.where(hot, 1.0, 0.0).astype(BF16)
    live = lax.broadcasted_iota(jnp.int32, (pairs * count, depth), 1) % planes == info[:, 1:2]
    matrix = []
    for part in range(parts):
        sides = [
            jnp.where(live, dot(hot, table_ref[part, side]), 0.0)
            .astype(BF16)
            .reshape(pairs, 2, 1, half, depth)
            for side in range(2)
        ]
        matrix.append(jnp.concatenate(sides, axis=2).reshape(pairs, 2 * count, depth))
    return matrix


def coil_parts(sens_ref, dir_ref, out_ref):
    coils, rows, planes, width = sens_ref.shape[1:]
    half = rows * planes
    chunk = max(16 // planes, 1)
    for index in range(0, rows, chunk):
        at = slice(index, index + chunk)
        to = index * planes
        d_re, d_im = dir_ref[0, at], dir_ref[1, at]
        for coil in range(coils):
            s_re, s_im = sens_ref[0, coil, at], sens_ref[1, coil, at]
            pair = (s_re * d_re - s_im * d_im, s_re * d_im + s_im * d_re)
            for ri, value in enumerate(pair):
                value = value.reshape(chunk * planes, width)
                where = slice(ri * half + to, ri * half + to + chunk * planes)
                for number, part in enumerate(split(value, 3)):
                    out_ref[number, where, coil * width : (coil + 1) * width] = part


def rows_kernel(
    planes, per_step, per_group, me_ref, info_ref, sens_ref, dir_ref, table_ref, keep_ref, send_ref,
    matrix_ref, all_ref, image_ref,
):
    pair = pl.program_id(0)
    count = info_ref.shape[2]

    @pl.when(pair % per_step == 0)
    def _():
        info = info_ref[...].reshape(per_step, 2 * count, FIELDS)
        for part, value in enumerate(row_matrix(info, table_ref, planes, 3)):
            all_ref[:, part] = value

    if per_group == 1:
        coil_parts(sens_ref, dir_ref, image_ref)
    else:

        @pl.when(pair % per_group == 0)
        def _():
            coil_parts(sens_ref, dir_ref, image_ref)

    matrix = [all_ref[pair % per_step, part] for part in range(3)]
    out = six_products(matrix, [image_ref[part] for part in range(3)])
    for slab, ref in enumerate((keep_ref, send_ref)):
        ref[0] = out[2 * slab * count : 2 * (slab + 1) * count]
    for part in range(2):
        matrix_ref[0, part] = matrix[part]


def partial_rows(me, info, sens, direction, table, planes, slabs_group):
    pairs, _, count, _ = info.shape
    _, coils, rows, _, width = sens.shape
    depth = 2 * rows * planes
    per_step = min(pairs, 8)
    whole = jax.ShapeDtypeStruct((pairs, 2 * count, coils * width), F32)
    block = pl.BlockSpec((1, 2 * count, coils * width), lambda q, me: (q, 0, 0))

    def place(q, me):
        return lax.bitwise_xor(2 * q, me[0]) // slabs_group

    return pl.pallas_call(
        lambda *refs: rows_kernel(planes, per_step, slabs_group // 2, *refs),
        grid_spec=pltpu.PrefetchScalarGridSpec(
            num_scalar_prefetch=1,
            grid=(pairs,),
            in_specs=[
                pl.BlockSpec((per_step, 2, count, FIELDS), lambda q, me: (q // per_step, 0, 0, 0)),
                pl.BlockSpec(
                    (2, coils, rows, planes, width), lambda q, me: (0, 0, 0, place(q, me), 0)
                ),
                pl.BlockSpec((2, rows, planes, width), lambda q, me: (0, 0, place(q, me), 0)),
                pl.BlockSpec(table.shape, lambda q, me: (0, 0, 0, 0)),
            ],
            out_specs=[
                block,
                block,
                pl.BlockSpec((1, 2, 4 * count, depth), lambda q, me: (q, 0, 0, 0)),
            ],
            scratch_shapes=[
                pltpu.VMEM((per_step, 3, 4 * count, depth), BF16),
                pltpu.VMEM((3, depth, coils * width), BF16),
            ],
        ),
        out_shape=[whole, whole, jax.ShapeDtypeStruct((pairs, 2, 4 * count, depth), BF16)],
        compiler_params=params(48),
        name="partial_rows",
    )(me, info, sens, direction, table)


def start_turn(info_ref, start_ref):
    chunk, _, count, _ = info_ref.shape
    info = info_ref[...].reshape(chunk * count, FIELDS)
    starts = start_ref.shape[0]
    hot = lax.broadcasted_iota(jnp.int32, (chunk * count, starts), 1) == info[:, 2:3]
    turn = jnp.dot(
        jnp.where(hot, 1.0, 0.0), start_ref[...], precision=HIGHEST, preferred_element_type=F32
    )
    width = turn.shape[1] // 2
    return info, turn[:, :width], turn[:, width:]


def segment_mask(info, cells, segment):
    at = lax.broadcasted_iota(jnp.int32, (info.shape[0], cells), 1)
    return (at >= info[:, 3:4]) & (at < info[:, 3:4] + segment)


def side_of(value, bit):
    step = 2**bit
    return value // step % 2, value // (2 * step) * step + value % step


def cells_kernel(tiles, segment, keep_ref, got_ref, info_ref, start_ref, table_ref, *out_refs):
    pairs, count, _ = keep_ref.shape
    count = count // 2
    cells = out_refs[0].shape[2] // 2
    coils = len(out_refs) // 2
    info, cos, sin = start_turn(info_ref, start_ref)
    width = cos.shape[1]
    values = []
    for coil in range(coils):
        lanes = slice(coil * width, (coil + 1) * width)
        both = keep_ref[:, :, lanes] + got_ref[:, :, lanes]
        re = both[:, :count].reshape(pairs * count, width)
        im = both[:, count:].reshape(pairs * count, width)
        re, im = cos * re + sin * im, cos * im - sin * re
        values.append(jnp.concatenate([re, im], axis=1))
        values.append(jnp.concatenate([im, -re], axis=1))
    value = split(jnp.concatenate(values, axis=0), 3)
    out = six_products(value, [table_ref[part] for part in range(3)])
    rows = pairs * count
    mask = segment_mask(info, cells, segment)
    for coil in range(coils):
        for ri in range(2):
            mine = out[(2 * coil + ri) * rows : (2 * coil + ri + 1) * rows]
            mine = jnp.where(mask, mine, 0.0).reshape(pairs, count // tiles, tiles, cells)
            mine = jnp.sum(mine, axis=1)
            for pair in range(pairs):
                side, place = side_of(pair, coil % 2)
                out_refs[2 * coil + side][place, :, ri * cells : (ri + 1) * cells] = mine[pair]


def row_cells(keep, got, info, start, table, tiles, segment, coils, chunk):
    pairs, double, width = keep.shape
    lines = 2 * table.shape[2]
    rows = pl.BlockSpec((chunk, double, width), lambda i: (i, 0, 0))
    half = jax.ShapeDtypeStruct((pairs // 2, tiles, lines), F32)
    return pl.pallas_call(
        lambda *refs: cells_kernel(tiles, segment, *refs),
        grid=(pairs // chunk,),
        in_specs=[
            rows,
            rows,
            pl.BlockSpec((chunk, 1, double // 2, FIELDS), lambda i: (i, 0, 0, 0)),
            pl.BlockSpec(start.shape, lambda i: (0, 0)),
            pl.BlockSpec(table.shape, lambda i: (0, 0, 0), pipeline_mode=pl.Buffered(1)),
        ],
        out_specs=[pl.BlockSpec((chunk // 2, tiles, lines), lambda i: (i, 0, 0))] * (2 * coils),
        out_shape=[half] * (2 * coils),
        compiler_params=params(40),
        name="row_cells",
    )(keep, got, info, start, table)


def adjoint_kernel(segment, coils, chunk, *refs):
    cell_refs, (info_ref, start_ref, table_ref, out_ref) = refs[: 2 * coils], refs[2 * coils :]
    count = info_ref.shape[2]
    _, tiles, cells = cell_refs[0].shape
    cells = cells // 2
    info, cos, sin = start_turn(info_ref, start_ref)
    width = cos.shape[1]
    mask = segment_mask(info, cells, segment)
    values = []
    for coil in range(coils):
        both = []
        for ri in range(2):
            wide = []
            for pair in range(chunk):
                side, place = side_of(pair, coil % 2)
                value = cell_refs[2 * coil + side][place, :, ri * cells : (ri + 1) * cells]
                wide += [value] * (count // tiles)
            both.append(jnp.where(mask, jnp.concatenate(wide, axis=0), 0.0))
        re, im = both
        values.append(jnp.concatenate([re, -im], axis=1))
        values.append(jnp.concatenate([im, re], axis=1))
    rows = chunk * count
    high, low = split(jnp.concatenate(values, axis=0), 2)
    first = dot(jnp.concatenate([high, low], axis=0), table_ref[0])
    total = high.shape[0]
    out = first[:total] + (first[total:] + dot(high, table_ref[1]))
    for coil in range(coils):
        re = out[2 * coil * rows : (2 * coil + 1) * rows]
        im = out[(2 * coil + 1) * rows : (2 * coil + 2) * rows]
        lanes = slice(coil * width, (coil + 1) * width)
        out_ref[:, :count, lanes] = (cos * re - sin * im).reshape(chunk, count, width)
        out_ref[:, count:, lanes] = (cos * im + sin * re).reshape(chunk, count, width)


def adjoint_rows(spread, info, start, table, segment, chunk):
    coils = len(spread) // 2
    half, tiles, lines = spread[0].shape
    pairs, _, count, _ = info.shape
    width = coils * table.shape[2]
    return pl.pallas_call(
        lambda *refs: adjoint_kernel(segment, coils, chunk, *refs),
        grid=(pairs // chunk,),
        in_specs=[pl.BlockSpec((chunk // 2, tiles, lines), lambda i: (i, 0, 0))] * (2 * coils)
        + [
            pl.BlockSpec((chunk, 1, count, FIELDS), lambda i: (i, 0, 0, 0)),
            pl.BlockSpec(start.shape, lambda i: (0, 0)),
            pl.BlockSpec(table.shape, lambda i: (0, 0, 0), pipeline_mode=pl.Buffered(1)),
        ],
        out_specs=pl.BlockSpec((chunk, 2 * count, width), lambda i: (i, 0, 0)),
        out_shape=jax.ShapeDtypeStruct((pairs, 2 * count, width), F32),
        compiler_params=params(32),
        name="adjoint_rows",
    )(*spread, info, start, table)


def tiles_kernel(coils, *refs):
    count_ref, res_ref, dir_ref, *refs = refs
    cell_refs, weight_ref = refs[: 2 * coils], refs[2 * coils]
    out_refs, sums_ref = refs[2 * coils + 1 : -1], refs[-1]
    tiles, samples, cells = weight_ref.shape
    rows = [
        ref[:, ri * cells : (ri + 1) * cells] + got[:, ri * cells : (ri + 1) * cells]
        for ref, got in zip(cell_refs[::2], cell_refs[1::2])
        for ri in range(2)
    ]
    found = []
    for tile in range(tiles):
        grid = jnp.concatenate([row[tile : tile + 1] for row in rows], axis=0)
        found.append(
            lax.dot_general(
                grid.astype(BF16),
                weight_ref[tile],
                (((1,), (1,)), ((), ())),
                preferred_element_type=F32,
            )
        )
    spread = []
    for tile in range(tiles):
        live = lax.broadcasted_iota(jnp.int32, found[tile].shape, 1) < count_ref[tile]
        spread.append(dot(jnp.where(live, found[tile], 0.0).astype(BF16), weight_ref[tile]))
    total = 0.0
    for number, row in enumerate(rows):
        value = jnp.concatenate([piece[number : number + 1] for piece in spread], axis=0)
        total = total + row * value
        ri = number % 2
        out_refs[number // 2][:, ri * cells : (ri + 1) * cells] = value
    norm = jnp.sum(res_ref[...], keepdims=True)
    curvature = jnp.sum(total, keepdims=True) + DAMPING * jnp.sum(dir_ref[...], keepdims=True)
    first = lax.broadcasted_iota(jnp.int32, sums_ref.shape, 0) == 0
    sums_ref[...] = jnp.where(first, norm, curvature)


def run_tiles(count, norms, cells, weight):
    coils = len(cells) // 2
    vmem = pl.BlockSpec(memory_space=pltpu.VMEM)
    whole = jax.ShapeDtypeStruct(cells[0].shape, F32)
    *spread, sums = pl.pallas_call(
        lambda *refs: tiles_kernel(coils, *refs),
        in_specs=[pl.BlockSpec(memory_space=pltpu.SMEM)] + [vmem] * (2 * coils + 3),
        out_specs=[vmem] * (coils + 1),
        out_shape=[whole] * coils + [jax.ShapeDtypeStruct((8, 128), F32)],
        compiler_params=params(16),
        name="tiles",
    )(count, *norms, *cells, weight)
    return spread, sums


def turn_kernel(matrix_ref, out_ref):
    for part in range(matrix_ref.shape[1]):
        out_ref[0, part] = jnp.transpose(matrix_ref[0, part].astype(F32)).astype(BF16)


def transposed(matrix):
    pairs, parts, rows, depth = matrix.shape
    return pl.pallas_call(
        turn_kernel,
        grid=(pairs,),
        in_specs=[pl.BlockSpec((1, parts, rows, depth), lambda q: (q, 0, 0, 0))],
        out_specs=pl.BlockSpec((1, parts, depth, rows), lambda q: (q, 0, 0, 0)),
        out_shape=jax.ShapeDtypeStruct((pairs, parts, depth, rows), BF16),
        compiler_params=params(8),
        name="transposed",
    )(matrix)


def finish_kernel(
    planes, depth_pairs, me_ref, sums_ref, mine_ref, got_ref, sens_ref, dir_ref, res_ref, matrix_ref,
    out_ref, norm_ref, squares_ref, *scratch,
):
    coils, rows, _, width = sens_ref.shape[1:]
    half = rows * planes
    group, pair = pl.program_id(0), pl.program_id(1)
    high, low = split(jnp.concatenate([mine_ref[0], got_ref[0]], axis=0), 2)
    left = jnp.concatenate([matrix_ref[0, 0], matrix_ref[0, 1], matrix_ref[0, 0]], axis=1)
    back = dot(left, jnp.concatenate([high, high, low], axis=0))

    @pl.when((group == 0) & (pair == 0))
    def _():
        squares_ref[...] = jnp.zeros(squares_ref.shape, F32)

    def combine(back):
        direction = [dir_ref[ri].reshape(half, width) for ri in range(2)]
        total = [DAMPING * direction[0], DAMPING * direction[1]]
        for coil in range(coils):
            lanes = slice(coil * width, (coil + 1) * width)
            v_re, v_im = back[:half, lanes], back[half:, lanes]
            s_re = sens_ref[0, coil].reshape(half, width)
            s_im = sens_ref[1, coil].reshape(half, width)
            total[0] += s_re * v_re + s_im * v_im
            total[1] += s_re * v_im - s_im * v_re
        squares = 0.0
        step = sums_ref[0:1, 0:1] / sums_ref[1:2, 0:1]
        for ri in range(2):
            value = res_ref[ri].reshape(half, width) - step * total[ri]
            out_ref[ri] = value.reshape(rows, planes, width)
            squares = squares + jnp.sum((value * value).reshape(rows, planes, width), axis=0)
        squares_ref[...] += squares

        @pl.when(group == pl.num_programs(0) - 1)
        def _():
            total = jnp.sum(squares_ref[...], keepdims=True)
            norm_ref[...] = jnp.broadcast_to(total, norm_ref.shape)

    if depth_pairs == 1:
        combine(back)
    else:
        sum_ref = scratch[0]

        @pl.when(pair == 0)
        def _():
            sum_ref[...] = back

        @pl.when(pair > 0)
        def _():
            sum_ref[...] += back

        @pl.when(pair == depth_pairs - 1)
        def _():
            combine(sum_ref[...])


def finish(me, sums, mine, got, sens, direction, residual, matrix, planes, slabs_group):
    _, coils, rows, total, width = sens.shape
    pairs, double, wide = mine.shape
    groups, deep = total // planes, slabs_group // 2

    def place(i, me):
        return lax.bitwise_xor(i * slabs_group, me[0]) // slabs_group

    row_block = pl.BlockSpec((1, double, wide), lambda i, j, me: (i * deep + j, 0, 0))
    image = pl.BlockSpec((2, rows, planes, width), lambda i, j, me: (0, 0, place(i, me), 0))
    return pl.pallas_call(
        lambda *refs: finish_kernel(planes, deep, *refs),
        grid_spec=pltpu.PrefetchScalarGridSpec(
            num_scalar_prefetch=1,
            grid=(groups, deep),
            in_specs=[
                pl.BlockSpec(sums.shape, lambda i, j, me: (0, 0)),
                row_block,
                row_block,
                pl.BlockSpec(
                    (2, coils, rows, planes, width), lambda i, j, me: (0, 0, 0, place(i, me), 0)
                ),
                image,
                image,
                pl.BlockSpec((1,) + matrix.shape[1:], lambda i, j, me: (i * deep + j, 0, 0, 0)),
            ],
            out_specs=[image, pl.BlockSpec(sums.shape, lambda i, j, me: (0, 0))],
            scratch_shapes=[pltpu.VMEM((planes, width), F32)]
            + ([pltpu.VMEM((2 * rows * planes, wide), F32)] if deep > 1 else []),
        ),
        out_shape=[
            jax.ShapeDtypeStruct(residual.shape, F32),
            jax.ShapeDtypeStruct(sums.shape, F32),
        ],
        compiler_params=params(56),
        name="finish",
    )(me, sums, mine, got, sens, direction, residual, matrix)


def swap(value, bit, slabs):
    return lax.ppermute(value, "slab", [(i, i ^ bit) for i in range(slabs)])


def sum_scatter(keep, send, bits, slabs):
    dims = keep.shape[1:]
    left = sorted(bits, reverse=True)
    for number, bit in enumerate(bits):
        axis = left.index(bit)
        left.pop(axis)
        if number > 0:
            value = (keep + got).reshape((2,) * (len(left) + 1) + dims)
            keep = lax.index_in_dim(value, 0, axis, keepdims=False)
            send = lax.index_in_dim(value, 1, axis, keepdims=False)
        got = swap(send, bit, slabs)
    return keep, got


def gather(value, bits, slabs):
    have = []
    for bit in bits:
        other = swap(value, bit, slabs)
        value = jnp.stack([value, other], axis=sum(1 for b in have if b > bit))
        have.append(bit)
    return value


def body(x_image, residual, direction, sensitivity, tile_block, tile_count, tile_weight):
    _, coils, rows, plane_count, ny = sensitivity.shape
    tiles, _, cells = tile_weight.shape
    slabs = lax.axis_size("slab")
    me = lax.axis_index("slab")
    lines = plane_count * GY // slabs
    segment = min(lines, GY)
    per_gx = lines // segment
    unit = math.gcd(cells, segment)
    segments = -(-(segment - unit + cells) // segment)
    planes = 8 if rows % 2 == 0 else 16
    slabs_group = planes * GY // lines
    pairs = slabs // 2
    bits = [1 << i for i in range(slabs.bit_length() - 1)]

    first = tile_block * cells
    start = first % segment
    base = (me * lines) % GY
    info = []
    for k in range(segments):
        row = jnp.minimum(first // segment + k, GX * per_gx - 1)
        plane = (me * lines + (row % per_gx) * segment) // GY
        turn = (base + start - segment * k) % GY // unit
        fields = [row // per_gx, plane % planes, turn, segment * k - start]
        info.append(jnp.stack(fields + [jnp.zeros_like(row)] * (FIELDS - len(fields)), axis=1))
    info = jnp.concatenate(info, axis=0)

    fillers = [lambda: squares(residual), lambda: squares(direction)]
    norms, have = [], []
    for number, bit in enumerate(reversed(bits)):
        other = swap(info, bit, slabs)
        if number < len(fillers):
            norms.append(fillers[number]())
        info = jnp.stack([info, other], axis=sum(1 for b in have if b > bit))
        have.append(bit)
        info, *norms = lax.optimization_barrier((info, *norms))
    info = info.reshape(pairs, 2, segments * tiles, FIELDS)

    x_cos, x_sin = dft(np.arange(GX), np.repeat(np.arange(rows), planes), GX)
    angle = (jnp.arange(GX, dtype=jnp.int32) * (me * rows) % GX).astype(F32) * (2 * math.pi / GX)
    turn_cos, turn_sin = jnp.cos(angle)[:, None], jnp.sin(angle)[:, None]
    x_upper = jnp.asarray(np.hstack([x_cos, x_sin]).astype(np.float32))
    x_lower = jnp.asarray(np.hstack([-x_sin, x_cos]).astype(np.float32))
    x_table = jnp.stack(
        [x_upper * turn_cos + x_lower * turn_sin, x_lower * turn_cos - x_upper * turn_sin]
    )
    x_parts = []
    for _ in range(3):
        part = lax.reduce_precision(x_table, 8, 7)
        x_parts.append(part.astype(BF16))
        x_table = x_table - part
    x_table = jnp.stack(x_parts)
    y_cos, y_sin = dft(np.arange(ny), np.arange(cells), GY)
    y_forward = jnp.asarray(table_parts(np.vstack([y_cos, y_sin]), 3))
    y_back = jnp.asarray(table_parts(np.vstack([y_cos.T, y_sin.T]), 2))
    start_table = np.hstack(dft(np.arange(GY // unit) * unit, np.arange(ny), GY, False))
    start_table = np.pad(start_table, ((0, -start_table.shape[0] % 8), (0, 0)))
    start_table = jnp.asarray(start_table.astype(np.float32))
    me_array = me.astype(jnp.int32)[None]

    keep, send, x_matrix = partial_rows(
        me_array, info, sensitivity, direction, x_table, planes, slabs_group
    )
    got = swap(send, 1, slabs)
    chunk = min(pairs, 4)
    grid = row_cells(
        keep, got, info, start_table, y_forward, tiles, segment, coils, chunk
    )
    high_bits = bits[1:]
    *grid, x_matrix = lax.optimization_barrier((*grid, x_matrix))
    x_matrix = transposed(x_matrix)
    orders = [high_bits[c % 2 :] + high_bits[: c % 2] for c in range(coils)]
    grid = [
        value
        for c, order in enumerate(orders)
        for value in sum_scatter(grid[2 * c], grid[2 * c + 1], order, slabs)
    ]

    *grid, x_matrix = lax.optimization_barrier((*grid, x_matrix))
    spread, sums = run_tiles(tile_count, norms, grid, tile_weight)

    dims = spread[0].shape
    had, have = [[] for _ in spread], [[] for _ in spread]
    for number, bit in enumerate(high_bits):
        sums = sums + swap(sums, bit, slabs)
        for c, order in enumerate(orders):
            way = order[len(order) - 1 - number]
            other = swap(spread[c], way, slabs)
            if number == len(order) - 1:
                had[c] = [spread[c].reshape((-1,) + dims), other.reshape((-1,) + dims)]
            else:
                axis = sum(1 for b in have[c] if b > way)
                spread[c] = jnp.stack([spread[c], other], axis=axis)
                have[c].append(way)
        if number < len(high_bits) - 1:
            sums, *spread = lax.optimization_barrier((sums, *spread))
    sums, *had = lax.optimization_barrier((sums, *had))
    mine = adjoint_rows(had[0] + had[1], info, start_table, y_back, segment, chunk)
    other = swap(mine, 1, slabs)
    sums, mine = lax.optimization_barrier((sums, mine))
    sums = sums + swap(sums, 1, slabs)
    residual_next, norm = finish(
        me_array, sums, mine, other, sensitivity, direction, residual, x_matrix, planes, slabs_group
    )

    pieces = 3
    x_next = None
    for number, bit in enumerate(reversed(bits)):
        norm, x_image = lax.optimization_barrier((norm, x_image))
        other = swap(norm, bit, slabs)
        if number < pieces:
            x_next = x_update(sums, x_image, direction, number, pieces, x_next)
            x_next, x_image = lax.optimization_barrier((x_next, x_image))
        if bit > 1:
            norm, x_next = lax.optimization_barrier((norm + other, x_next))
    direction_next = direction_update(sums, norm, other, residual_next, direction)
    return (x_next, residual_next, direction_next)


def solution(mesh):
    image = P(None, "slab", "frames", None)
    placed = (image, image, image, P(None, None, "slab", None, None)) + (
        P("slab"),
        P("slab"),
        P("slab", None, None),
    )
    return jax.shard_map(
        body, mesh=mesh, in_specs=placed, out_specs=(image, image, image), check_vma=False
    )
```

```python
import math

import jax
import jax.numpy as jnp
import ml_dtypes
import numpy as np
from jax import lax
from jax.experimental import pallas as pl
from jax.experimental.pallas import tpu as pltpu
from jax.sharding import PartitionSpec as P

GX = 480
GY = 480
DAMPING = 0.1
HIGHEST = lax.Precision.HIGHEST
F32 = jnp.float32
BF16 = jnp.bfloat16
MIB = 1024 * 1024
FIELDS = 8


def dft(out_index, in_index, size, scaled=True):
    angle = (out_index[:, None] * in_index[None, :] % size) * (2.0 * math.pi / size)
    scale = 1.0 / math.sqrt(size) if scaled else 1.0
    return np.cos(angle) * scale, np.sin(angle) * scale


def table_parts(table, count):
    parts = []
    for _ in range(count):
        part = table.astype(ml_dtypes.bfloat16)
        parts.append(part)
        table = table - part.astype(np.float64)
    return np.stack(parts)


def split(value, count):
    parts = []
    for step in range(count):
        part = value.astype(BF16)
        parts.append(part)
        if step + 1 < count:
            value = value - part.astype(F32)
    return parts


def dot(a, b):
    return lax.dot_general(a, b, (((1,), (0,)), ((), ())), preferred_element_type=F32)


def six_products(lhs, rhs):
    rows = lhs[0].shape[0]
    first = dot(jnp.concatenate(lhs, axis=0), rhs[0])
    second = dot(jnp.concatenate(lhs[:2], axis=0), rhs[1])
    third = dot(lhs[0], rhs[2])
    small = first[2 * rows :] + second[rows:] + third
    return first[:rows] + (first[rows : 2 * rows] + second[:rows] + small)


def params(mib):
    return pltpu.CompilerParams(vmem_limit_bytes=mib * MIB)


def resident():
    return pl.BlockSpec(memory_space=pltpu.VMEM)


def in_hbm():
    return pl.BlockSpec(memory_space=pltpu.HBM)


def scalars():
    return pl.BlockSpec(memory_space=pltpu.SMEM)


def blocks(shape, index, steps):
    return resident() if steps == 1 else pl.BlockSpec(shape, index)


def load_kernel(from_hbm, out_ref, sem):
    copies = [
        pltpu.make_async_copy(from_hbm.at[piece], out_ref.at[piece], sem.at[piece])
        for piece in range(out_ref.shape[0])
    ]
    for copy in copies:
        copy.start()
    for copy in copies:
        copy.wait()


def load(value):
    flat = (-1,) + value.shape[-3:]
    out = pltpu.with_memory_space_constraint(value.reshape(flat), pltpu.HBM)
    out = pl.pallas_call(
        load_kernel,
        in_specs=[in_hbm()],
        out_specs=resident(),
        out_shape=jax.ShapeDtypeStruct(out.shape, F32),
        scratch_shapes=[pltpu.SemaphoreType.DMA((out.shape[0],))],
        compiler_params=params(2),
        name="load",
    )(out)
    return out.reshape(value.shape)


def squares_kernel(res_ref, norm_ref):
    rows = res_ref.shape[1]

    def step(row, total):
        return total + res_ref[0, row] * res_ref[0, row] + res_ref[1, row] * res_ref[1, row]

    total = lax.fori_loop(0, rows, step, jnp.zeros(res_ref.shape[2:], F32))
    total = jnp.sum(total, keepdims=True)
    first = lax.broadcasted_iota(jnp.int32, norm_ref.shape, 0) == 0
    norm_ref[...] = jnp.where(first, total, 0.0)


def squares(residual):
    return pl.pallas_call(
        squares_kernel,
        in_specs=[resident()],
        out_specs=resident(),
        out_shape=jax.ShapeDtypeStruct((8, 128), F32),
        compiler_params=params(8),
        name="squares",
    )(residual)


def x_kernel(first, sums_ref, x_ref, dir_ref, *refs):
    rows = x_ref.shape[0]
    step = sums_ref[0:1, 0:1] / sums_ref[1:2, 0:1]
    at = pl.ds(first + pl.program_id(0) * rows, rows)
    refs[-1][...] = x_ref[...] + step * dir_ref[at]


def x_update(sums, x_image, direction, piece, pieces, before):
    dims = x_image.shape
    flat = (-1,) + dims[2:]
    rows = dims[0] * dims[1] // pieces
    step = rows // 2
    given = [] if before is None else [before.reshape(flat)]
    block = pl.BlockSpec((step,) + dims[2:], lambda i: (2 * piece + i, 0, 0))
    out = pl.pallas_call(
        lambda *refs: x_kernel(piece * rows, *refs),
        grid=(2,),
        in_specs=[resident(), block, resident()] + [in_hbm()] * len(given),
        out_specs=block,
        out_shape=jax.ShapeDtypeStruct((dims[0] * dims[1],) + dims[2:], F32),
        input_output_aliases={3: 0} if given else {},
        compiler_params=params(16),
        name="x_update",
    )(sums, x_image.reshape(flat), direction.reshape(flat), *given)
    return out.reshape(dims)


def direction_kernel(sums_ref, one_ref, two_ref, res_ref, dir_ref, out_ref):
    rows = out_ref.shape[0]
    ratio = (one_ref[0:1, 0:1] + two_ref[0:1, 0:1]) / sums_ref[0:1, 0:1]
    at = pl.ds(pl.program_id(0) * rows, rows)
    out_ref[...] = res_ref[at] + ratio * dir_ref[at]


def direction_update(sums, one, two, residual, direction):
    dims = residual.shape
    flat = (-1,) + dims[2:]
    rows = dims[0] * dims[1]
    steps = 3
    out = pl.pallas_call(
        direction_kernel,
        grid=(steps,),
        in_specs=[resident()] * 5,
        out_specs=pl.BlockSpec((rows // steps,) + dims[2:], lambda i: (i, 0, 0)),
        out_shape=jax.ShapeDtypeStruct((rows,) + dims[2:], F32),
        compiler_params=params(16),
        name="direction_update",
    )(sums, one, two, residual.reshape(flat), direction.reshape(flat))
    return out.reshape(dims)


def row_matrix(info, table_ref, planes, parts):
    pairs, count, _ = info.shape
    half = count // 2
    info = info.reshape(pairs * count, FIELDS)
    depth = table_ref.shape[3]
    hot = lax.broadcasted_iota(jnp.int32, (pairs * count, GX), 1) == info[:, 0:1]
    hot = jnp.where(hot, 1.0, 0.0).astype(BF16)
    live = lax.broadcasted_iota(jnp.int32, (pairs * count, depth), 1) % planes == info[:, 1:2]
    matrix = []
    for part in range(parts):
        sides = [
            jnp.where(live, dot(hot, table_ref[part, side]), 0.0)
            .astype(BF16)
            .reshape(pairs, 2, 1, half, depth)
            for side in range(2)
        ]
        matrix.append(jnp.concatenate(sides, axis=2).reshape(pairs, 2 * count, depth))
    return matrix


def coil_parts(start, planes, sens_ref, dir_ref, out_ref):
    _, coils, rows, _, width = sens_ref.shape
    half = rows * planes
    chunk = max(16 // planes, 1)
    plane = pl.ds(start, planes)
    squares = jnp.zeros((planes, width), F32)
    for index in range(0, rows, chunk):
        at = slice(index, index + chunk)
        to = index * planes
        d_re, d_im = dir_ref[0, at, plane], dir_ref[1, at, plane]
        squares += jnp.sum(d_re * d_re + d_im * d_im, axis=0)
        for coil in range(coils):
            s_re, s_im = sens_ref[0, coil, at, plane], sens_ref[1, coil, at, plane]
            pair = (s_re * d_re - s_im * d_im, s_re * d_im + s_im * d_re)
            for ri, value in enumerate(pair):
                value = value.reshape(chunk * planes, width)
                where = slice(ri * half + to, ri * half + to + chunk * planes)
                for number, part in enumerate(split(value, 3)):
                    out_ref[number, where, coil * width : (coil + 1) * width] = part
    return squares


def rows_kernel(
    planes, slabs_group, steps, me_ref, info_ref, sens_hbm, dir_hbm, table_ref, *refs
):
    pairs, _, count, _ = info_ref.shape
    coils, _, total, width = sens_hbm.shape[1:]
    keep_refs, send_refs = refs[:coils], refs[coils : 2 * coils]
    matrix_ref, norm_ref, one_ref, two_ref, sens_ref, dir_ref, sem = refs[2 * coils :]
    groups = total // planes

    def copies(group):
        at = pl.ds(pl.multiple_of(group * planes, planes), planes)
        return (
            pltpu.make_async_copy(sens_hbm.at[:, :, :, at], sens_ref.at[:, :, :, at], sem.at[group, 0]),
            pltpu.make_async_copy(dir_hbm.at[:, :, at], dir_ref.at[:, :, at], sem.at[group, 1]),
        )

    def start_copies():
        for group in range(groups):
            for copy in copies(group):
                copy.start()

    def wait_copies(group):
        for copy in copies(group):
            copy.wait()

    if steps == 1:
        start_copies()
    else:
        pl.when(pl.program_id(0) == 0)(start_copies)
    info = info_ref[...].reshape(pairs, 2 * count, FIELDS)
    for part, value in enumerate(row_matrix(info, table_ref, planes, 3)):
        matrix_ref[:, part] = value

    def coil_images(group, ref):
        start = pl.multiple_of(group * planes, planes)
        return coil_parts(start, planes, sens_ref, dir_ref, ref)

    def products(pair, image_ref):
        matrix = [matrix_ref[pair, part] for part in range(3)]
        out = six_products(matrix, [image_ref[part] for part in range(3)])
        for coil in range(coils):
            mine = out[:, coil * width : (coil + 1) * width]
            keep_refs[coil][pair] = mine[: 2 * count]
            send_refs[coil][pair] = mine[2 * count :]

    squares = jnp.zeros((planes, width), F32)
    if slabs_group == 2:
        high = me_ref[0] // 2

        def step(index, squares):
            group = 2 * index
            wait_copies(group + 1)
            squares += coil_images(group + 1, two_ref)
            products(lax.bitwise_xor(group, high), one_ref)
            wait_copies(group + 2)
            squares += coil_images(group + 2, one_ref)
            products(lax.bitwise_xor(group + 1, high), two_ref)
            return squares

        wait_copies(0)
        squares = coil_images(0, one_ref)
        squares = lax.fori_loop(0, groups // 2 - 1, step, squares)
        wait_copies(groups - 1)
        squares += coil_images(groups - 1, two_ref)
        products(lax.bitwise_xor(groups - 2, high), one_ref)
        products(lax.bitwise_xor(groups - 1, high), two_ref)
    else:
        first = pl.program_id(0) * pairs

        @pl.when(first == 0)
        def _():
            for group in range(groups):
                wait_copies(group)

        group = lax.bitwise_xor(2 * first, me_ref[0]) // slabs_group
        fresh = coil_images(group, one_ref)
        squares = jnp.where(2 * first % slabs_group == 0, fresh, 0.0)
        for pair in range(pairs):
            products(pair, one_ref)
    amount = DAMPING * jnp.sum(squares, keepdims=True)
    at = lax.broadcasted_iota(jnp.int32, norm_ref.shape, 0)
    amount = jnp.where(at == 0, 0.0, amount)
    if steps == 1:
        norm_ref[...] = amount
    else:

        @pl.when(pl.program_id(0) == 0)
        def _():
            norm_ref[...] = jnp.zeros(norm_ref.shape, F32)

        norm_ref[...] += amount


def partial_rows(me, info, sens, direction, table, planes, slabs_group):
    pairs, _, count, _ = info.shape
    _, coils, rows, total, width = sens.shape
    depth = 2 * rows * planes
    step = min(pairs, 512 // (2 * count))
    steps = pairs // step
    shape = (2 * count, width)
    kept = jax.ShapeDtypeStruct((pairs,) + shape, F32)
    kept_block = blocks((step,) + shape, lambda i: (i, 0, 0), steps)
    shape = (3, 4 * count, depth)
    *values, matrix, norm = pl.pallas_call(
        lambda *refs: rows_kernel(planes, slabs_group, steps, *refs),
        grid=() if steps == 1 else (steps,),
        in_specs=[
            scalars(),
            blocks((step, 2, count, FIELDS), lambda i: (i, 0, 0, 0), steps),
            in_hbm(),
            in_hbm(),
            resident(),
        ],
        out_specs=[kept_block] * (2 * coils)
        + [
            blocks((step,) + shape, lambda i: (i, 0, 0, 0), steps),
            blocks((8, 128), lambda i: (0, 0), steps),
        ],
        out_shape=[kept] * (2 * coils)
        + [
            jax.ShapeDtypeStruct((pairs,) + shape, BF16),
            jax.ShapeDtypeStruct((8, 128), F32),
        ],
        scratch_shapes=[pltpu.VMEM((3, depth, coils * width), BF16)] * 2
        + [
            pltpu.VMEM(sens.shape, F32),
            pltpu.VMEM(direction.shape, F32),
            pltpu.SemaphoreType.DMA((total // planes, 2)),
        ],
        compiler_params=params(40),
        name="partial_rows",
    )(
        me,
        info,
        pltpu.with_memory_space_constraint(sens, pltpu.HBM),
        pltpu.with_memory_space_constraint(direction, pltpu.HBM),
        table,
    )
    return values[:coils], values[coils:], matrix, norm


def start_turn(info_ref, start_ref):
    chunk, _, count, _ = info_ref.shape
    info = info_ref[:, 0].reshape(chunk * count, FIELDS)
    starts = start_ref.shape[0]
    hot = lax.broadcasted_iota(jnp.int32, (chunk * count, starts), 1) == info[:, 2:3]
    turn = jnp.dot(
        jnp.where(hot, 1.0, 0.0), start_ref[...], precision=HIGHEST, preferred_element_type=F32
    )
    width = turn.shape[1] // 2
    return info, turn[:, :width], turn[:, width:]


def segment_mask(info, cells, segment):
    at = lax.broadcasted_iota(jnp.int32, (info.shape[0], cells), 1)
    return (at >= info[:, 3:4]) & (at < info[:, 3:4] + segment)


def side_of(value, bit):
    step = 2**bit
    return value // step % 2, value // (2 * step) * step + value % step


def cells_kernel(tiles, segment, bit, keep_ref, got_ref, info_ref, start_ref, table_ref, *out_refs):
    pairs, count, width = keep_ref.shape
    count = count // 2
    cells = table_ref.shape[2]
    info, cos, sin = start_turn(info_ref, start_ref)
    both = keep_ref[...] + got_ref[...]
    re = both[:, :count].reshape(pairs * count, width)
    im = both[:, count:].reshape(pairs * count, width)
    re, im = cos * re + sin * im, cos * im - sin * re
    value = [jnp.concatenate([re, im], axis=1), jnp.concatenate([im, -re], axis=1)]
    value = split(jnp.concatenate(value, axis=0), 3)
    out = six_products(value, [table_ref[part] for part in range(3)])
    mask = segment_mask(info, cells, segment)
    for ri in range(2):
        mine = out[ri * pairs * count : (ri + 1) * pairs * count]
        mine = jnp.where(mask, mine, 0.0).reshape(pairs, count // tiles, tiles, cells)
        mine = jnp.sum(mine, axis=1)
        for pair in range(pairs):
            side, place = side_of(pair, bit)
            out_refs[side][place, :, ri * cells : (ri + 1) * cells] = mine[pair]


def row_cells(keep, got, info, start, table, tiles, segment, bit):
    pairs, double, width = keep.shape
    lines = 2 * table.shape[2]
    chunk = pairs if pairs <= 8 else 4
    steps = pairs // chunk
    rows = blocks((chunk, double, width), lambda i: (i, 0, 0), steps)
    half = jax.ShapeDtypeStruct((pairs // 2, tiles, lines), F32)
    return pl.pallas_call(
        lambda *refs: cells_kernel(tiles, segment, bit, *refs),
        grid=() if steps == 1 else (steps,),
        in_specs=[
            rows,
            rows,
            blocks((chunk, 1, double // 2, FIELDS), lambda i: (i, 0, 0, 0), steps),
            resident(),
            resident(),
        ],
        out_specs=[blocks((chunk // 2, tiles, lines), lambda i: (i, 0, 0), steps)] * 2,
        out_shape=[half] * 2,
        compiler_params=params(24),
        name="row_cells",
    )(keep, got, info, start, table)


def adjoint_kernel(segment, bit, had_ref, got_ref, info_ref, start_ref, table_ref, out_ref):
    chunk, _, count, _ = info_ref.shape
    _, tiles, cells = had_ref.shape
    cells = cells // 2
    info, cos, sin = start_turn(info_ref, start_ref)
    mask = segment_mask(info, cells, segment)
    both = []
    for ri in range(2):
        wide = []
        for pair in range(chunk):
            side, place = side_of(pair, bit)
            value = (had_ref, got_ref)[side][place, :, ri * cells : (ri + 1) * cells]
            wide += [value] * (count // tiles)
        both.append(jnp.where(mask, jnp.concatenate(wide, axis=0), 0.0))
    re, im = both
    value = [jnp.concatenate([re, -im], axis=1), jnp.concatenate([im, re], axis=1)]
    high, low = split(jnp.concatenate(value, axis=0), 2)
    first = dot(jnp.concatenate([high, low], axis=0), table_ref[0])
    total, rows = high.shape[0], chunk * count
    out = first[:total] + (first[total:] + dot(high, table_ref[1]))
    re, im = out[:rows], out[rows:]
    out_ref[:, :count] = (cos * re - sin * im).reshape(chunk, count, -1)
    out_ref[:, count:] = (cos * im + sin * re).reshape(chunk, count, -1)


def adjoint_rows(had, got, info, start, table, segment, bit):
    half, tiles, lines = had.shape
    pairs, _, count, _ = info.shape
    width = table.shape[2]
    chunk = pairs if pairs <= 8 else 4
    steps = pairs // chunk
    cells = blocks((chunk // 2, tiles, lines), lambda i: (i, 0, 0), steps)
    return pl.pallas_call(
        lambda *refs: adjoint_kernel(segment, bit, *refs),
        grid=() if steps == 1 else (steps,),
        in_specs=[
            cells,
            cells,
            blocks((chunk, 1, count, FIELDS), lambda i: (i, 0, 0, 0), steps),
            resident(),
            resident(),
        ],
        out_specs=blocks((chunk, 2 * count, width), lambda i: (i, 0, 0), steps),
        out_shape=jax.ShapeDtypeStruct((pairs, 2 * count, width), F32),
        compiler_params=params(24),
        name="adjoint_rows",
    )(had, got, info, start, table)


def tiles_kernel(count_ref, norm_refs, keep_ref, got_ref, weight_ref, out_ref, sums_ref):
    tiles, _, cells = weight_ref.shape
    grid = keep_ref[...] + got_ref[...]
    rows = [grid[:, ri * cells : (ri + 1) * cells] for ri in range(2)]
    found = []
    for tile in range(tiles):
        both = jnp.concatenate([row[tile : tile + 1] for row in rows], axis=0).astype(BF16)
        found.append(
            lax.dot_general(
                both, weight_ref[tile], (((1,), (1,)), ((), ())), preferred_element_type=F32
            )
        )
    spread = []
    for tile in range(tiles):
        live = lax.broadcasted_iota(jnp.int32, found[tile].shape, 1) < count_ref[tile]
        spread.append(dot(jnp.where(live, found[tile], 0.0).astype(BF16), weight_ref[tile]))
    total = 0.0
    for ri, row in enumerate(rows):
        value = jnp.concatenate([piece[ri : ri + 1] for piece in spread], axis=0)
        total = total + row * value
        out_ref[:, ri * cells : (ri + 1) * cells] = value
    total = jnp.sum(total, keepdims=True)
    first = lax.broadcasted_iota(jnp.int32, sums_ref.shape, 0) == 0
    norm = norm_refs[0][...]
    for ref in norm_refs[1:]:
        norm = norm + ref[...]
    sums_ref[...] = norm + jnp.where(first, 0.0, total)


def run_tiles(count, norms, keep, got, weight):
    more = len(norms)
    return pl.pallas_call(
        lambda *refs: tiles_kernel(refs[0], refs[1 : 1 + more], *refs[1 + more :]),
        in_specs=[scalars()] + [resident()] * (more + 3),
        out_specs=[resident()] * 2,
        out_shape=[
            jax.ShapeDtypeStruct(keep.shape, F32),
            jax.ShapeDtypeStruct((8, 128), F32),
        ],
        compiler_params=params(8),
        name="tiles",
    )(count, *norms, keep, got, weight)


def turn_kernel(matrix_ref, out_ref):
    for pair in range(matrix_ref.shape[0]):
        for part in range(2):
            value = matrix_ref[pair, part].astype(F32)
            out_ref[pair, part] = jnp.transpose(value).astype(BF16)


def transposed(matrix):
    pairs, parts, rows, depth = matrix.shape
    step = min(pairs, 8)
    steps = pairs // step
    return pl.pallas_call(
        turn_kernel,
        grid=() if steps == 1 else (steps,),
        in_specs=[blocks((step, parts, rows, depth), lambda q: (q, 0, 0, 0), steps)],
        out_specs=blocks((step, 2, depth, rows), lambda q: (q, 0, 0, 0), steps),
        out_shape=jax.ShapeDtypeStruct((pairs, 2, depth, rows), BF16),
        compiler_params=params(12),
        name="transposed",
    )(matrix)


def back_rows(matrix, rows):
    value = [jnp.concatenate([mine, got], axis=0) for mine, got in zip(rows[::2], rows[1::2])]
    high, low = split(jnp.concatenate(value, axis=1), 2)
    left = jnp.concatenate([matrix[0], matrix[1], matrix[0]], axis=1)
    return dot(left, jnp.concatenate([high, high, low], axis=0))


def combine(back, plane, step, sens_ref, dir_ref, res_ref, out_ref):
    _, coils, rows, _, width = sens_ref.shape
    planes = plane.stop - plane.start
    half = rows * planes
    total = [DAMPING * dir_ref[ri, :, plane].reshape(half, width) for ri in range(2)]
    for coil in range(coils):
        lanes = slice(coil * width, (coil + 1) * width)
        v_re, v_im = back[:half, lanes], back[half:, lanes]
        s_re = sens_ref[0, coil, :, plane].reshape(half, width)
        s_im = sens_ref[1, coil, :, plane].reshape(half, width)
        total[0] += s_re * v_re + s_im * v_im
        total[1] += s_re * v_im - s_im * v_re
    squares = 0.0
    for ri in range(2):
        value = res_ref[ri, :, plane].reshape(half, width) - step * total[ri]
        value = value.reshape(rows, planes, width)
        out_ref[ri, :, plane] = value
        squares = squares + jnp.sum(value * value, axis=0)
    return squares


def finish_kernel(planes, me_ref, sums_ref, sens_ref, dir_ref, res_ref, matrix_ref, *refs):
    coils, rows, total, width = sens_ref.shape[1:]
    row_refs = refs[: 2 * coils]
    out_hbm, out_ref, norm_ref, sem = refs[2 * coils :]
    step = sums_ref[0:1, 0:1] / sums_ref[1:2, 0:1]
    squares = jnp.zeros((planes, width), F32)
    copies = []
    for group in range(total // planes):
        pair = lax.bitwise_xor(group, me_ref[0] // 2)
        back = back_rows(
            [matrix_ref[pair, part] for part in range(2)], [ref[pair] for ref in row_refs]
        )
        plane = slice(group * planes, (group + 1) * planes)
        squares += combine(back, plane, step, sens_ref, dir_ref, res_ref, out_ref)
        at = pl.ds(group * planes, planes)
        copies.append(
            pltpu.make_async_copy(out_ref.at[:, :, at], out_hbm.at[:, :, at], sem.at[group])
        )
        copies[-1].start()
    for copy in copies:
        copy.wait()
    norm_ref[...] = jnp.broadcast_to(jnp.sum(squares, keepdims=True), norm_ref.shape)


def finish(me, sums, rows, sens, direction, residual, matrix, planes):
    kept = jax.ShapeDtypeStruct(residual.shape, F32)
    return pl.pallas_call(
        lambda *refs: finish_kernel(planes, *refs),
        in_specs=[scalars()] + [resident()] * (5 + len(rows)),
        out_specs=[in_hbm(), resident(), resident()],
        out_shape=[kept, kept, jax.ShapeDtypeStruct(sums.shape, F32)],
        scratch_shapes=[pltpu.SemaphoreType.DMA((residual.shape[2] // planes,))],
        compiler_params=params(16),
        name="finish",
    )(me, sums, sens, direction, residual, matrix, *rows)


def finish_deep_kernel(planes, me_ref, sums_ref, sens_ref, dir_ref, res_ref, matrix_ref, *refs):
    coils = sens_ref.shape[1]
    row_refs = refs[: 2 * coils]
    out_ref, norm_ref, squares_ref, sum_ref = refs[2 * coils :]
    group, pair = pl.program_id(0), pl.program_id(1)
    back = back_rows([matrix_ref[0, part] for part in range(2)], [ref[0] for ref in row_refs])

    @pl.when((group == 0) & (pair == 0))
    def _():
        squares_ref[...] = jnp.zeros(squares_ref.shape, F32)

    @pl.when(pair == 0)
    def _():
        sum_ref[...] = back

    @pl.when(pair > 0)
    def _():
        sum_ref[...] += back

    @pl.when(pair == pl.num_programs(1) - 1)
    def _():
        step = sums_ref[0:1, 0:1] / sums_ref[1:2, 0:1]
        squares_ref[...] += combine(
            sum_ref[...], slice(0, planes), step, sens_ref, dir_ref, res_ref, out_ref
        )
        total = jnp.sum(squares_ref[...], keepdims=True)
        norm_ref[...] = jnp.broadcast_to(total, norm_ref.shape)


def finish_deep(me, sums, rows, sens, direction, residual, matrix, planes, slabs_group):
    _, coils, height, total, width = sens.shape
    double = rows[0].shape[1]
    groups, deep = total // planes, slabs_group // 2

    def pair(i, j, me):
        return lax.bitwise_xor(i, me[0] // slabs_group) * deep + j

    row_block = pl.BlockSpec((1, double, width), lambda i, j, me: (pair(i, j, me), 0, 0))
    image = pl.BlockSpec((2, height, planes, width), lambda i, j, me: (0, 0, i, 0))
    small = pl.BlockSpec(sums.shape, lambda i, j, me: (0, 0))
    out, norm = pl.pallas_call(
        lambda *refs: finish_deep_kernel(planes, *refs),
        grid_spec=pltpu.PrefetchScalarGridSpec(
            num_scalar_prefetch=1,
            grid=(groups, deep),
            in_specs=[
                small,
                pl.BlockSpec(
                    (2, coils, height, planes, width), lambda i, j, me: (0, 0, 0, i, 0)
                ),
                image,
                image,
                pl.BlockSpec((1,) + matrix.shape[1:], lambda i, j, me: (pair(i, j, me), 0, 0, 0)),
            ]
            + [row_block] * len(rows),
            out_specs=[image, small],
            scratch_shapes=[
                pltpu.VMEM((planes, width), F32),
                pltpu.VMEM((2 * height * planes, coils * width), F32),
            ],
        ),
        out_shape=[
            jax.ShapeDtypeStruct(residual.shape, F32),
            jax.ShapeDtypeStruct(sums.shape, F32),
        ],
        compiler_params=params(32),
        name="finish_deep",
    )(me, sums, sens, direction, residual, matrix, *rows)
    return out, out, norm


def swap(value, bit, slabs):
    return lax.ppermute(value, "slab", [(i, i ^ bit) for i in range(slabs)])


def sum_scatter(keep, send, bits, slabs):
    dims = keep.shape[1:]
    left = sorted(bits, reverse=True)
    for number, bit in enumerate(bits):
        axis = left.index(bit)
        left.pop(axis)
        if number > 0:
            value = (keep + got).reshape((2,) * (len(left) + 1) + dims)
            keep = lax.index_in_dim(value, 0, axis, keepdims=False)
            send = lax.index_in_dim(value, 1, axis, keepdims=False)
        got = swap(send, bit, slabs)
    return keep, got


def gather(value, bits, slabs):
    have = []
    for bit in bits:
        other = swap(value, bit, slabs)
        value = jnp.stack([value, other], axis=sum(1 for b in have if b > bit))
        have.append(bit)
    return value


def body(x_image, residual, direction, sensitivity, tile_block, tile_count, tile_weight):
    _, coils, rows, plane_count, ny = sensitivity.shape
    tiles, _, cells = tile_weight.shape
    slabs = lax.axis_size("slab")
    me = lax.axis_index("slab")
    lines = plane_count * GY // slabs
    segment = min(lines, GY)
    per_gx = lines // segment
    unit = math.gcd(cells, segment)
    segments = -(-(segment - unit + cells) // segment)
    planes = 8 if rows % 2 == 0 else 16
    slabs_group = planes * GY // lines
    pairs = slabs // 2
    bits = [1 << i for i in range(slabs.bit_length() - 1)]

    first = tile_block * cells
    start = first % segment
    base = (me * lines) % GY
    info = []
    for k in range(segments):
        row = jnp.minimum(first // segment + k, GX * per_gx - 1)
        plane = (me * lines + (row % per_gx) * segment) // GY
        turn = (base + start - segment * k) % GY // unit
        fields = [row // per_gx, plane % planes, turn, segment * k - start]
        info.append(jnp.stack(fields + [jnp.zeros_like(row)] * (FIELDS - len(fields)), axis=1))
    info = jnp.concatenate(info, axis=0)

    norms, have = [], []
    for number, bit in enumerate(reversed(bits)):
        other = swap(info, bit, slabs)
        if number == 0:
            norms.append(squares(residual))
        info = jnp.stack([info, other], axis=sum(1 for b in have if b > bit))
        have.append(bit)
        info, *norms = lax.optimization_barrier((info, *norms))
    info = info.reshape(pairs, 2, segments * tiles, FIELDS)

    x_cos, x_sin = dft(np.arange(GX), np.repeat(np.arange(rows), planes), GX)
    angle = (jnp.arange(GX, dtype=jnp.int32) * (me * rows) % GX).astype(F32) * (2 * math.pi / GX)
    turn_cos, turn_sin = jnp.cos(angle)[:, None], jnp.sin(angle)[:, None]
    x_upper = jnp.asarray(np.hstack([x_cos, x_sin]).astype(np.float32))
    x_lower = jnp.asarray(np.hstack([-x_sin, x_cos]).astype(np.float32))
    x_table = jnp.stack(
        [x_upper * turn_cos + x_lower * turn_sin, x_lower * turn_cos - x_upper * turn_sin]
    )
    x_parts = []
    for _ in range(3):
        part = lax.reduce_precision(x_table, 8, 7)
        x_parts.append(part.astype(BF16))
        x_table = x_table - part
    x_table = jnp.stack(x_parts)
    y_cos, y_sin = dft(np.arange(ny), np.arange(cells), GY)
    y_forward = jnp.asarray(table_parts(np.vstack([y_cos, y_sin]), 3))
    y_back = jnp.asarray(table_parts(np.vstack([y_cos.T, y_sin.T]), 2))
    start_table = np.hstack(dft(np.arange(GY // unit) * unit, np.arange(ny), GY, False))
    start_table = np.pad(start_table, ((0, -start_table.shape[0] % 8), (0, 0)))
    start_table = jnp.asarray(start_table.astype(np.float32))
    me_array = me.astype(jnp.int32)[None]

    keep, send, x_matrix, norm = partial_rows(
        me_array, info, sensitivity, direction, x_table, planes, slabs_group
    )
    norms.append(norm)
    got = [swap(value, 1, slabs) for value in send]
    grid = [
        row_cells(keep[c], got[c], info, start_table, y_forward, tiles, segment, c % 2)
        for c in range(coils)
    ]
    grid[-1], x_matrix = lax.optimization_barrier((grid[-1], x_matrix))
    x_matrix = transposed(x_matrix)
    high_bits = bits[1:]
    orders = [high_bits[c % 2 :] + high_bits[: c % 2] for c in range(coils)]
    grid = [sum_scatter(*value, order, slabs) for value, order in zip(grid, orders)]
    grid[-1], x_matrix = lax.optimization_barrier((grid[-1], x_matrix))

    rows_back, loaded = [], []
    for c, order in enumerate(orders):
        spread, sums = run_tiles(tile_count, norms, *grid[c], tile_weight)
        norms = [sums]
        dims = spread.shape
        have = []
        for number, bit in enumerate(order[::-1]):
            if c == coils - 1:
                sums = sums + swap(sums, high_bits[-1 - number], slabs)
            other = swap(spread, bit, slabs)
            if c == coils - 1 and number < 3:
                loaded.append(load((sensitivity, direction, residual)[number]))
            if bit != order[0]:
                spread = jnp.stack([spread, other], axis=sum(1 for b in have if b > bit))
                have.append(bit)
                if c == coils - 1:
                    sums, spread, sensitivity, direction, residual, *loaded = lax.optimization_barrier(
                        (sums, spread, sensitivity, direction, residual, *loaded)
                    )
        spread, other = spread.reshape((-1,) + dims), other.reshape((-1,) + dims)
        if c == coils - 1:
            sums, spread, other, *loaded = lax.optimization_barrier((sums, spread, other, *loaded))
        mine = adjoint_rows(spread, other, info, start_table, y_back, segment, c % 2)
        rows_back += [mine, swap(mine, 1, slabs)]
    sums = sums + swap(sums, 1, slabs)
    sens, move, residual = loaded
    if slabs_group == 2:
        residual_next, res, norm = finish(
            me_array, sums, rows_back, sens, move, residual, x_matrix, planes
        )
    else:
        residual_next, res, norm = finish_deep(
            me_array, sums, rows_back, sens, move, residual, x_matrix, planes, slabs_group
        )

    pieces = 3
    x_next = None
    for number, bit in enumerate(reversed(bits)):
        norm, x_image = lax.optimization_barrier((norm, x_image))
        other = swap(norm, bit, slabs)
        if number < pieces:
            x_next = x_update(sums, x_image, move, number, pieces, x_next)
            x_next, x_image = lax.optimization_barrier((x_next, x_image))
        if bit > 1:
            norm, x_next = lax.optimization_barrier((norm + other, x_next))
    direction_next = direction_update(sums, norm, other, res, move)
    return (x_next, residual_next, direction_next)


def solution(mesh):
    image = P(None, "slab", "frames", None)
    placed = (image, image, image, P(None, None, "slab", None, None)) + (
        P("slab"),
        P("slab"),
        P("slab", None, None),
    )
    return jax.shard_map(
        body, mesh=mesh, in_specs=placed, out_specs=(image, image, image), check_vma=False
    )
```

```python
import math

import jax
import jax.numpy as jnp
import ml_dtypes
import numpy as np
from jax import lax
from jax.experimental import pallas as pl
from jax.experimental.pallas import tpu as pltpu
from jax.sharding import PartitionSpec as P

GX = 480
GY = 480
DAMPING = 0.1
HIGHEST = lax.Precision.HIGHEST
F32 = jnp.float32
BF16 = jnp.bfloat16
MIB = 1024 * 1024
FIELDS = 8


def dft(out_index, in_index, size, scaled=True):
    angle = (out_index[:, None] * in_index[None, :] % size) * (2.0 * math.pi / size)
    scale = 1.0 / math.sqrt(size) if scaled else 1.0
    return np.cos(angle) * scale, np.sin(angle) * scale


def table_parts(table, count):
    parts = []
    for _ in range(count):
        part = table.astype(ml_dtypes.bfloat16)
        parts.append(part)
        table = table - part.astype(np.float64)
    return np.stack(parts)


def split(value, count):
    parts = []
    for step in range(count):
        part = value.astype(BF16)
        parts.append(part)
        if step + 1 < count:
            value = value - part.astype(F32)
    return parts


def dot(a, b):
    return lax.dot_general(a, b, (((1,), (0,)), ((), ())), preferred_element_type=F32)


def six_products(lhs, rhs):
    rows = lhs[0].shape[0]
    first = dot(jnp.concatenate(lhs, axis=0), rhs[0])
    second = dot(jnp.concatenate(lhs[:2], axis=0), rhs[1])
    third = dot(lhs[0], rhs[2])
    small = first[2 * rows :] + second[rows:] + third
    return first[:rows] + (first[rows : 2 * rows] + second[:rows] + small)


def params(mib):
    return pltpu.CompilerParams(vmem_limit_bytes=mib * MIB)


def resident():
    return pl.BlockSpec(memory_space=pltpu.VMEM)


def in_hbm():
    return pl.BlockSpec(memory_space=pltpu.HBM)


def scalars():
    return pl.BlockSpec(memory_space=pltpu.SMEM)


def blocks(shape, index, steps):
    return resident() if steps == 1 else pl.BlockSpec(shape, index)


def load_kernel(from_hbm, out_ref, sem):
    copies = [
        pltpu.make_async_copy(from_hbm.at[piece], out_ref.at[piece], sem.at[piece])
        for piece in range(out_ref.shape[0])
    ]
    for copy in copies:
        copy.start()
    for copy in copies:
        copy.wait()


def load(value):
    flat = (-1,) + value.shape[-3:]
    out = pltpu.with_memory_space_constraint(value.reshape(flat), pltpu.HBM)
    out = pl.pallas_call(
        load_kernel,
        in_specs=[in_hbm()],
        out_specs=resident(),
        out_shape=jax.ShapeDtypeStruct(out.shape, F32),
        scratch_shapes=[pltpu.SemaphoreType.DMA((out.shape[0],))],
        compiler_params=params(2),
        name="load",
    )(out)
    return out.reshape(value.shape)


def squares_kernel(res_ref, norm_ref):
    rows = res_ref.shape[1]

    def step(row, total):
        return total + res_ref[0, row] * res_ref[0, row] + res_ref[1, row] * res_ref[1, row]

    total = lax.fori_loop(0, rows, step, jnp.zeros(res_ref.shape[2:], F32))
    total = jnp.sum(total, keepdims=True)
    first = lax.broadcasted_iota(jnp.int32, norm_ref.shape, 0) == 0
    norm_ref[...] = jnp.where(first, total, 0.0)


def squares(residual):
    return pl.pallas_call(
        squares_kernel,
        in_specs=[resident()],
        out_specs=resident(),
        out_shape=jax.ShapeDtypeStruct((8, 128), F32),
        compiler_params=params(8),
        name="squares",
    )(residual)


def x_kernel(first, sums_ref, x_ref, dir_ref, *refs):
    rows = x_ref.shape[0]
    step = sums_ref[0:1, 0:1] / sums_ref[1:2, 0:1]
    at = pl.ds(first + pl.program_id(0) * rows, rows)
    refs[-1][...] = x_ref[...] + step * dir_ref[at]


def x_update(sums, x_image, direction, piece, pieces, before):
    dims = x_image.shape
    flat = (-1,) + dims[2:]
    rows = dims[0] * dims[1] // pieces
    step = rows // 2
    given = [] if before is None else [before.reshape(flat)]
    block = pl.BlockSpec((step,) + dims[2:], lambda i: (2 * piece + i, 0, 0))
    out = pl.pallas_call(
        lambda *refs: x_kernel(piece * rows, *refs),
        grid=(2,),
        in_specs=[resident(), block, resident()] + [in_hbm()] * len(given),
        out_specs=block,
        out_shape=jax.ShapeDtypeStruct((dims[0] * dims[1],) + dims[2:], F32),
        input_output_aliases={3: 0} if given else {},
        compiler_params=params(16),
        name="x_update",
    )(sums, x_image.reshape(flat), direction.reshape(flat), *given)
    return out.reshape(dims)


def direction_kernel(sums_ref, one_ref, two_ref, res_ref, dir_ref, out_hbm, out_ref, sem):
    pieces = sem.shape[0]
    rows = out_ref.shape[0] // pieces
    ratio = (one_ref[0:1, 0:1] + two_ref[0:1, 0:1]) / sums_ref[0:1, 0:1]
    copies = []
    for piece in range(pieces):
        at = pl.ds(piece * rows, rows)
        out_ref[at] = res_ref[at] + ratio * dir_ref[at]
        copies.append(pltpu.make_async_copy(out_ref.at[at], out_hbm.at[at], sem.at[piece]))
        copies[-1].start()
    for copy in copies:
        copy.wait()


def direction_update(sums, one, two, residual, direction):
    dims = residual.shape
    flat = (-1,) + dims[2:]
    shape = (dims[0] * dims[1],) + dims[2:]
    out = pl.pallas_call(
        direction_kernel,
        in_specs=[resident()] * 5,
        out_specs=in_hbm(),
        out_shape=jax.ShapeDtypeStruct(shape, F32),
        scratch_shapes=[pltpu.VMEM(shape, F32), pltpu.SemaphoreType.DMA((6,))],
        compiler_params=params(16),
        name="direction_update",
    )(sums, one, two, residual.reshape(flat), direction.reshape(flat))
    return out.reshape(dims)


def row_matrix(info, table_ref, planes, parts):
    pairs, count, _ = info.shape
    half = count // 2
    info = info.reshape(pairs * count, FIELDS)
    depth = table_ref.shape[3]
    hot = lax.broadcasted_iota(jnp.int32, (pairs * count, GX), 1) == info[:, 0:1]
    hot = jnp.where(hot, 1.0, 0.0).astype(BF16)
    live = lax.broadcasted_iota(jnp.int32, (pairs * count, depth), 1) % planes == info[:, 1:2]
    matrix = []
    for part in range(parts):
        sides = [
            jnp.where(live, dot(hot, table_ref[part, side]), 0.0)
            .astype(BF16)
            .reshape(pairs, 2, 1, half, depth)
            for side in range(2)
        ]
        matrix.append(jnp.concatenate(sides, axis=2).reshape(pairs, 2 * count, depth))
    return matrix


def half_turn(value):
    return pltpu.roll(value, 4, 1)


def low_half(shape):
    return lax.broadcasted_iota(jnp.int32, shape, 1) < 4


def coil_parts(start, planes, sens_ref, dir_ref, out_ref):
    _, coils, rows, _, width = sens_ref.shape
    sides = out_ref.shape[0]
    own = planes // sides
    half = rows * own
    chunk = max(16 // own, 1)
    plane = pl.ds(start, planes)
    squares = jnp.zeros((planes, width), F32)
    for index in range(0, rows, chunk):
        at = slice(index, index + chunk)
        to = index * own
        d_re, d_im = dir_ref[0, at, plane], dir_ref[1, at, plane]
        squares += jnp.sum(d_re * d_re + d_im * d_im, axis=0)
        for coil in range(coils):
            s_re, s_im = sens_ref[0, coil, at, plane], sens_ref[1, coil, at, plane]
            pair = (s_re * d_re - s_im * d_im, s_re * d_im + s_im * d_re)
            for ri, value in enumerate(pair):
                if sides == 2:
                    value = value.reshape(chunk // 2, 2, planes, width)
                    one, two = value[:, 0], value[:, 1]
                    low = low_half(one.shape)
                    values = [jnp.where(low, one, half_turn(two)), jnp.where(low, half_turn(one), two)]
                else:
                    values = [value]
                where = slice(ri * half + to, ri * half + to + chunk * own)
                for side, value in enumerate(values):
                    value = value.reshape(chunk * own, width)
                    for number, part in enumerate(split(value, 3)):
                        out_ref[side, number, where, coil * width : (coil + 1) * width] = part
    return squares


def rows_kernel(
    planes, slabs_group, steps, me_ref, info_ref, sens_hbm, dir_hbm, table_ref, *refs
):
    pairs, _, count, _ = info_ref.shape
    coils, _, total, width = sens_hbm.shape[1:]
    keep_refs, send_refs = refs[:coils], refs[coils : 2 * coils]
    matrix_ref, norm_ref, one_ref, two_ref, sens_ref, dir_ref, sem = refs[2 * coils :]
    groups = total // planes

    def copies(group):
        at = pl.ds(pl.multiple_of(group * planes, planes), planes)
        return (
            pltpu.make_async_copy(sens_hbm.at[:, :, :, at], sens_ref.at[:, :, :, at], sem.at[group, 0]),
            pltpu.make_async_copy(dir_hbm.at[:, :, at], dir_ref.at[:, :, at], sem.at[group, 1]),
        )

    def start_copies():
        for group in range(groups):
            for copy in copies(group):
                copy.start()

    def wait_copies(group):
        for copy in copies(group):
            copy.wait()

    if steps == 1:
        start_copies()
    else:
        pl.when(pl.program_id(0) == 0)(start_copies)
    info = info_ref[...].reshape(pairs, 2 * count, FIELDS)
    own = planes // one_ref.shape[0]
    for part, value in enumerate(row_matrix(info, table_ref, own, 3)):
        matrix_ref[:, part] = value

    def coil_images(group, ref):
        start = pl.multiple_of(group * planes, planes)
        return coil_parts(start, planes, sens_ref, dir_ref, ref)

    def products(pair, image_ref):
        for side, out_refs in enumerate((keep_refs, send_refs)):
            rows = slice(2 * side * count, 2 * (side + 1) * count)
            matrix = [matrix_ref[pair, part, rows] for part in range(3)]
            slab = lax.rem(me_ref[0] + side, 2) if slabs_group == 2 else 0
            out = six_products(matrix, [image_ref[slab, part] for part in range(3)])
            for coil in range(coils):
                out_refs[coil][pair] = out[:, coil * width : (coil + 1) * width]

    squares = jnp.zeros((planes, width), F32)
    if slabs_group == 2:
        high = me_ref[0] // 2

        def step(index, squares):
            group = 2 * index
            wait_copies(group + 1)
            squares += coil_images(group + 1, two_ref)
            products(lax.bitwise_xor(group, high), one_ref)
            wait_copies(group + 2)
            squares += coil_images(group + 2, one_ref)
            products(lax.bitwise_xor(group + 1, high), two_ref)
            return squares

        wait_copies(0)
        squares = coil_images(0, one_ref)
        squares = lax.fori_loop(0, groups // 2 - 1, step, squares)
        wait_copies(groups - 1)
        squares += coil_images(groups - 1, two_ref)
        products(lax.bitwise_xor(groups - 2, high), one_ref)
        products(lax.bitwise_xor(groups - 1, high), two_ref)
    else:
        first = pl.program_id(0) * pairs

        @pl.when(first == 0)
        def _():
            for group in range(groups):
                wait_copies(group)

        group = lax.bitwise_xor(2 * first, me_ref[0]) // slabs_group
        fresh = coil_images(group, one_ref)
        squares = jnp.where(2 * first % slabs_group == 0, fresh, 0.0)
        for pair in range(pairs):
            products(pair, one_ref)
    amount = DAMPING * jnp.sum(squares, keepdims=True)
    at = lax.broadcasted_iota(jnp.int32, norm_ref.shape, 0)
    amount = jnp.where(at == 0, 0.0, amount)
    if steps == 1:
        norm_ref[...] = amount
    else:

        @pl.when(pl.program_id(0) == 0)
        def _():
            norm_ref[...] = jnp.zeros(norm_ref.shape, F32)

        norm_ref[...] += amount


def partial_rows(me, info, sens, direction, table, planes, slabs_group):
    pairs, _, count, _ = info.shape
    _, coils, rows, total, width = sens.shape
    depth = table.shape[3]
    step = min(pairs, 512 // (2 * count))
    steps = pairs // step
    shape = (2 * count, width)
    kept = jax.ShapeDtypeStruct((pairs,) + shape, F32)
    kept_block = blocks((step,) + shape, lambda i: (i, 0, 0), steps)
    shape = (3, 4 * count, depth)
    *values, matrix, norm = pl.pallas_call(
        lambda *refs: rows_kernel(planes, slabs_group, steps, *refs),
        grid=() if steps == 1 else (steps,),
        in_specs=[
            scalars(),
            blocks((step, 2, count, FIELDS), lambda i: (i, 0, 0, 0), steps),
            in_hbm(),
            in_hbm(),
            resident(),
        ],
        out_specs=[kept_block] * (2 * coils)
        + [
            blocks((step,) + shape, lambda i: (i, 0, 0, 0), steps),
            blocks((8, 128), lambda i: (0, 0), steps),
        ],
        out_shape=[kept] * (2 * coils)
        + [
            jax.ShapeDtypeStruct((pairs,) + shape, BF16),
            jax.ShapeDtypeStruct((8, 128), F32),
        ],
        scratch_shapes=[pltpu.VMEM((2 if slabs_group == 2 else 1, 3, depth, coils * width), BF16)] * 2
        + [
            pltpu.VMEM(sens.shape, F32),
            pltpu.VMEM(direction.shape, F32),
            pltpu.SemaphoreType.DMA((total // planes, 2)),
        ],
        compiler_params=params(40),
        name="partial_rows",
    )(
        me,
        info,
        pltpu.with_memory_space_constraint(sens, pltpu.HBM),
        pltpu.with_memory_space_constraint(direction, pltpu.HBM),
        table,
    )
    return values[:coils], values[coils:], matrix, norm


def start_turn(info_ref, start_ref):
    chunk, _, count, _ = info_ref.shape
    info = info_ref[:, 0].reshape(chunk * count, FIELDS)
    starts = start_ref.shape[0]
    hot = lax.broadcasted_iota(jnp.int32, (chunk * count, starts), 1) == info[:, 2:3]
    turn = jnp.dot(
        jnp.where(hot, 1.0, 0.0), start_ref[...], precision=HIGHEST, preferred_element_type=F32
    )
    width = turn.shape[1] // 2
    return info, turn[:, :width], turn[:, width:]


def segment_mask(info, cells, segment):
    at = lax.broadcasted_iota(jnp.int32, (info.shape[0], cells), 1)
    return (at >= info[:, 3:4]) & (at < info[:, 3:4] + segment)


def side_of(value, bit):
    step = 2**bit
    return value // step % 2, value // (2 * step) * step + value % step


def cells_kernel(tiles, segment, bit, keep_ref, got_ref, info_ref, start_ref, table_ref, *out_refs):
    pairs, count, width = keep_ref.shape
    count = count // 2
    cells = table_ref.shape[2]
    info, cos, sin = start_turn(info_ref, start_ref)
    both = keep_ref[...] + got_ref[...]
    re = both[:, :count].reshape(pairs * count, width)
    im = both[:, count:].reshape(pairs * count, width)
    re, im = cos * re + sin * im, cos * im - sin * re
    value = [jnp.concatenate([re, im], axis=1), jnp.concatenate([im, -re], axis=1)]
    value = split(jnp.concatenate(value, axis=0), 3)
    out = six_products(value, [table_ref[part] for part in range(3)])
    mask = segment_mask(info, cells, segment)
    for ri in range(2):
        mine = out[ri * pairs * count : (ri + 1) * pairs * count]
        mine = jnp.where(mask, mine, 0.0).reshape(pairs, count // tiles, tiles, cells)
        mine = jnp.sum(mine, axis=1)
        for pair in range(pairs):
            side, place = side_of(pair, bit)
            out_refs[side][place, :, ri * cells : (ri + 1) * cells] = mine[pair]


def row_cells(keep, got, info, start, table, tiles, segment, bit):
    pairs, double, width = keep.shape
    lines = 2 * table.shape[2]
    chunk = pairs if pairs <= 8 else 4
    steps = pairs // chunk
    rows = blocks((chunk, double, width), lambda i: (i, 0, 0), steps)
    half = jax.ShapeDtypeStruct((pairs // 2, tiles, lines), F32)
    return pl.pallas_call(
        lambda *refs: cells_kernel(tiles, segment, bit, *refs),
        grid=() if steps == 1 else (steps,),
        in_specs=[
            rows,
            rows,
            blocks((chunk, 1, double // 2, FIELDS), lambda i: (i, 0, 0, 0), steps),
            resident(),
            resident(),
        ],
        out_specs=[blocks((chunk // 2, tiles, lines), lambda i: (i, 0, 0), steps)] * 2,
        out_shape=[half] * 2,
        compiler_params=params(24),
        name="row_cells",
    )(keep, got, info, start, table)


def adjoint_kernel(segment, bit, had_ref, got_ref, info_ref, start_ref, table_ref, out_ref):
    chunk, _, count, _ = info_ref.shape
    _, tiles, cells = had_ref.shape
    cells = cells // 2
    info, cos, sin = start_turn(info_ref, start_ref)
    mask = segment_mask(info, cells, segment)
    both = []
    for ri in range(2):
        wide = []
        for pair in range(chunk):
            side, place = side_of(pair, bit)
            value = (had_ref, got_ref)[side][place, :, ri * cells : (ri + 1) * cells]
            wide += [value] * (count // tiles)
        both.append(jnp.where(mask, jnp.concatenate(wide, axis=0), 0.0))
    re, im = both
    value = [jnp.concatenate([re, -im], axis=1), jnp.concatenate([im, re], axis=1)]
    high, low = split(jnp.concatenate(value, axis=0), 2)
    first = dot(jnp.concatenate([high, low], axis=0), table_ref[0])
    total, rows = high.shape[0], chunk * count
    out = first[:total] + (first[total:] + dot(high, table_ref[1]))
    re, im = out[:rows], out[rows:]
    out_ref[:, :count] = (cos * re - sin * im).reshape(chunk, count, -1)
    out_ref[:, count:] = (cos * im + sin * re).reshape(chunk, count, -1)


def adjoint_rows(had, got, info, start, table, segment, bit):
    half, tiles, lines = had.shape
    pairs, _, count, _ = info.shape
    width = table.shape[2]
    chunk = pairs if pairs <= 8 else 4
    steps = pairs // chunk
    cells = blocks((chunk // 2, tiles, lines), lambda i: (i, 0, 0), steps)
    return pl.pallas_call(
        lambda *refs: adjoint_kernel(segment, bit, *refs),
        grid=() if steps == 1 else (steps,),
        in_specs=[
            cells,
            cells,
            blocks((chunk, 1, count, FIELDS), lambda i: (i, 0, 0, 0), steps),
            resident(),
            resident(),
        ],
        out_specs=blocks((chunk, 2 * count, width), lambda i: (i, 0, 0), steps),
        out_shape=jax.ShapeDtypeStruct((pairs, 2 * count, width), F32),
        compiler_params=params(24),
        name="adjoint_rows",
    )(had, got, info, start, table)


def tiles_kernel(count_ref, norm_refs, keep_ref, got_ref, weight_ref, out_ref, sums_ref):
    tiles, _, cells = weight_ref.shape
    grid = keep_ref[...] + got_ref[...]
    rows = [grid[:, ri * cells : (ri + 1) * cells] for ri in range(2)]
    found = []
    for tile in range(tiles):
        both = jnp.concatenate([row[tile : tile + 1] for row in rows], axis=0).astype(BF16)
        found.append(
            lax.dot_general(
                both, weight_ref[tile], (((1,), (1,)), ((), ())), preferred_element_type=F32
            )
        )
    spread = []
    for tile in range(tiles):
        live = lax.broadcasted_iota(jnp.int32, found[tile].shape, 1) < count_ref[tile]
        spread.append(dot(jnp.where(live, found[tile], 0.0).astype(BF16), weight_ref[tile]))
    total = 0.0
    for ri, row in enumerate(rows):
        value = jnp.concatenate([piece[ri : ri + 1] for piece in spread], axis=0)
        total = total + row * value
        out_ref[:, ri * cells : (ri + 1) * cells] = value
    total = jnp.sum(total, keepdims=True)
    first = lax.broadcasted_iota(jnp.int32, sums_ref.shape, 0) == 0
    norm = norm_refs[0][...]
    for ref in norm_refs[1:]:
        norm = norm + ref[...]
    sums_ref[...] = norm + jnp.where(first, 0.0, total)


def run_tiles(count, norms, keep, got, weight):
    more = len(norms)
    return pl.pallas_call(
        lambda *refs: tiles_kernel(refs[0], refs[1 : 1 + more], *refs[1 + more :]),
        in_specs=[scalars()] + [resident()] * (more + 3),
        out_specs=[resident()] * 2,
        out_shape=[
            jax.ShapeDtypeStruct(keep.shape, F32),
            jax.ShapeDtypeStruct((8, 128), F32),
        ],
        compiler_params=params(8),
        name="tiles",
    )(count, *norms, keep, got, weight)


def turn_kernel(matrix_ref, out_ref):
    sides = out_ref.shape[1]
    rows = matrix_ref.shape[2] // sides
    for pair in range(matrix_ref.shape[0]):
        for side in range(sides):
            high, low = [
                matrix_ref[pair, part, side * rows : (side + 1) * rows].astype(F32) for part in range(2)
            ]
            value = jnp.concatenate([high, low, high], axis=0)
            out_ref[pair, side] = jnp.transpose(value).astype(BF16)


def transposed(matrix, sides):
    pairs, parts, rows, depth = matrix.shape
    step = min(pairs, 8)
    steps = pairs // step
    shape = (sides, depth, 3 * rows // sides)
    return pl.pallas_call(
        turn_kernel,
        grid=() if steps == 1 else (steps,),
        in_specs=[blocks((step, parts, rows, depth), lambda q: (q, 0, 0, 0), steps)],
        out_specs=blocks((step,) + shape, lambda q: (q, 0, 0, 0), steps),
        out_shape=jax.ShapeDtypeStruct((pairs,) + shape, BF16),
        compiler_params=params(12),
        name="transposed",
    )(matrix)


def back_rows(matrix, rows):
    high, low = split(rows, 2)
    return dot(matrix, jnp.concatenate([high, high, low], axis=0))


def back_group(odd, matrix, mine, got):
    first = back_rows(matrix(odd), jnp.where(odd == 0, mine, got))
    second = back_rows(matrix(1 - odd), jnp.where(odd == 0, got, mine))
    shape = (first.shape[0] // 8, 8, first.shape[1])
    first, second = first.reshape(shape), second.reshape(shape)
    low = low_half(shape)
    one = jnp.where(low, first, half_turn(second))
    two = jnp.where(low, half_turn(first), second)
    value = jnp.concatenate([one[:, None], two[:, None]], axis=1)
    return value.reshape(16 * shape[0], shape[2])


def combine(back, plane, step, sens_ref, dir_ref, res_ref, out_ref):
    _, coils, rows, _, width = sens_ref.shape
    planes = plane.stop - plane.start
    half = rows * planes
    total = [DAMPING * dir_ref[ri, :, plane].reshape(half, width) for ri in range(2)]
    for coil in range(coils):
        lanes = slice(coil * width, (coil + 1) * width)
        v_re, v_im = back[:half, lanes], back[half:, lanes]
        s_re = sens_ref[0, coil, :, plane].reshape(half, width)
        s_im = sens_ref[1, coil, :, plane].reshape(half, width)
        total[0] += s_re * v_re + s_im * v_im
        total[1] += s_re * v_im - s_im * v_re
    squares = 0.0
    for ri in range(2):
        value = res_ref[ri, :, plane].reshape(half, width) - step * total[ri]
        value = value.reshape(rows, planes, width)
        out_ref[ri, :, plane] = value
        squares = squares + jnp.sum(value * value, axis=0)
    return squares


def finish_kernel(planes, me_ref, sums_ref, sens_ref, dir_ref, res_ref, matrix_ref, *refs):
    coils, rows, total, width = sens_ref.shape[1:]
    row_refs = refs[: 2 * coils]
    out_hbm, out_ref, norm_ref, sem = refs[2 * coils :]
    step = sums_ref[0:1, 0:1] / sums_ref[1:2, 0:1]
    squares = jnp.zeros((planes, width), F32)
    copies = []
    for group in range(total // planes):
        pair, odd = lax.bitwise_xor(group, me_ref[0] // 2), lax.rem(me_ref[0], 2)
        mine = jnp.concatenate([ref[pair] for ref in row_refs[::2]], axis=1)
        got = jnp.concatenate([ref[pair] for ref in row_refs[1::2]], axis=1)
        back = back_group(odd, lambda side: matrix_ref[pair, side], mine, got)
        plane = slice(group * planes, (group + 1) * planes)
        squares += combine(back, plane, step, sens_ref, dir_ref, res_ref, out_ref)
        at = pl.ds(group * planes, planes)
        copies.append(
            pltpu.make_async_copy(out_ref.at[:, :, at], out_hbm.at[:, :, at], sem.at[group])
        )
        copies[-1].start()
    for copy in copies:
        copy.wait()
    norm_ref[...] = jnp.broadcast_to(jnp.sum(squares, keepdims=True), norm_ref.shape)


def finish(me, sums, rows, sens, direction, residual, matrix, planes):
    kept = jax.ShapeDtypeStruct(residual.shape, F32)
    return pl.pallas_call(
        lambda *refs: finish_kernel(planes, *refs),
        in_specs=[scalars()] + [resident()] * (5 + len(rows)),
        out_specs=[in_hbm(), resident(), resident()],
        out_shape=[kept, kept, jax.ShapeDtypeStruct(sums.shape, F32)],
        scratch_shapes=[pltpu.SemaphoreType.DMA((residual.shape[2] // planes,))],
        compiler_params=params(16),
        name="finish",
    )(me, sums, sens, direction, residual, matrix, *rows)


def finish_deep_kernel(planes, me_ref, sums_ref, sens_ref, dir_ref, res_ref, matrix_ref, *refs):
    coils = sens_ref.shape[1]
    row_refs = refs[: 2 * coils]
    out_ref, norm_ref, squares_ref, sum_ref = refs[2 * coils :]
    group, pair = pl.program_id(0), pl.program_id(1)
    rows = [jnp.concatenate([ref[0] for ref in row_refs[k::2]], axis=1) for k in range(2)]
    back = back_rows(matrix_ref[0, 0], jnp.concatenate(rows, axis=0))

    @pl.when((group == 0) & (pair == 0))
    def _():
        squares_ref[...] = jnp.zeros(squares_ref.shape, F32)

    @pl.when(pair == 0)
    def _():
        sum_ref[...] = back

    @pl.when(pair > 0)
    def _():
        sum_ref[...] += back

    @pl.when(pair == pl.num_programs(1) - 1)
    def _():
        step = sums_ref[0:1, 0:1] / sums_ref[1:2, 0:1]
        squares_ref[...] += combine(
            sum_ref[...], slice(0, planes), step, sens_ref, dir_ref, res_ref, out_ref
        )
        total = jnp.sum(squares_ref[...], keepdims=True)
        norm_ref[...] = jnp.broadcast_to(total, norm_ref.shape)


def finish_deep(me, sums, rows, sens, direction, residual, matrix, planes, slabs_group):
    _, coils, height, total, width = sens.shape
    double = rows[0].shape[1]
    groups, deep = total // planes, slabs_group // 2

    def pair(i, j, me):
        return lax.bitwise_xor(i, me[0] // slabs_group) * deep + j

    row_block = pl.BlockSpec((1, double, width), lambda i, j, me: (pair(i, j, me), 0, 0))
    image = pl.BlockSpec((2, height, planes, width), lambda i, j, me: (0, 0, i, 0))
    small = pl.BlockSpec(sums.shape, lambda i, j, me: (0, 0))
    out, norm = pl.pallas_call(
        lambda *refs: finish_deep_kernel(planes, *refs),
        grid_spec=pltpu.PrefetchScalarGridSpec(
            num_scalar_prefetch=1,
            grid=(groups, deep),
            in_specs=[
                small,
                pl.BlockSpec(
                    (2, coils, height, planes, width), lambda i, j, me: (0, 0, 0, i, 0)
                ),
                image,
                image,
                pl.BlockSpec((1,) + matrix.shape[1:], lambda i, j, me: (pair(i, j, me), 0, 0, 0)),
            ]
            + [row_block] * len(rows),
            out_specs=[image, small],
            scratch_shapes=[
                pltpu.VMEM((planes, width), F32),
                pltpu.VMEM((2 * height * planes, coils * width), F32),
            ],
        ),
        out_shape=[
            jax.ShapeDtypeStruct(residual.shape, F32),
            jax.ShapeDtypeStruct(sums.shape, F32),
        ],
        compiler_params=params(32),
        name="finish_deep",
    )(me, sums, sens, direction, residual, matrix, *rows)
    return out, out, norm


def swap(value, bit, slabs):
    return lax.ppermute(value, "slab", [(i, i ^ bit) for i in range(slabs)])


def sum_scatter(keep, send, bits, slabs):
    dims = keep.shape[1:]
    left = sorted(bits, reverse=True)
    for number, bit in enumerate(bits):
        axis = left.index(bit)
        left.pop(axis)
        if number > 0:
            value = (keep + got).reshape((2,) * (len(left) + 1) + dims)
            keep = lax.index_in_dim(value, 0, axis, keepdims=False)
            send = lax.index_in_dim(value, 1, axis, keepdims=False)
        got = swap(send, bit, slabs)
    return keep, got


def gather(value, bits, slabs):
    have = []
    for bit in bits:
        other = swap(value, bit, slabs)
        value = jnp.stack([value, other], axis=sum(1 for b in have if b > bit))
        have.append(bit)
    return value


def body(x_image, residual, direction, sensitivity, tile_block, tile_count, tile_weight):
    _, coils, rows, plane_count, ny = sensitivity.shape
    tiles, _, cells = tile_weight.shape
    slabs = lax.axis_size("slab")
    me = lax.axis_index("slab")
    lines = plane_count * GY // slabs
    segment = min(lines, GY)
    per_gx = lines // segment
    unit = math.gcd(cells, segment)
    segments = -(-(segment - unit + cells) // segment)
    planes = 8 if rows % 2 == 0 else 16
    slabs_group = planes * GY // lines
    own = planes // 2 if slabs_group == 2 else planes
    pairs = slabs // 2
    bits = [1 << i for i in range(slabs.bit_length() - 1)]

    first = tile_block * cells
    start = first % segment
    base = (me * lines) % GY
    info = []
    for k in range(segments):
        row = jnp.minimum(first // segment + k, GX * per_gx - 1)
        plane = (me * lines + (row % per_gx) * segment) // GY
        turn = (base + start - segment * k) % GY // unit
        fields = [row // per_gx, plane % own, turn, segment * k - start]
        info.append(jnp.stack(fields + [jnp.zeros_like(row)] * (FIELDS - len(fields)), axis=1))
    info = jnp.concatenate(info, axis=0)

    have = []
    for number, bit in enumerate(reversed(bits)):
        other = swap(info, bit, slabs)
        info = jnp.stack([info, other], axis=sum(1 for b in have if b > bit))
        have.append(bit)
    info = info.reshape(pairs, 2, segments * tiles, FIELDS)

    x_cos, x_sin = dft(np.arange(GX), np.repeat(np.arange(rows), own), GX)
    angle = (jnp.arange(GX, dtype=jnp.int32) * (me * rows) % GX).astype(F32) * (2 * math.pi / GX)
    turn_cos, turn_sin = jnp.cos(angle)[:, None], jnp.sin(angle)[:, None]
    x_upper = jnp.asarray(np.hstack([x_cos, x_sin]).astype(np.float32))
    x_lower = jnp.asarray(np.hstack([-x_sin, x_cos]).astype(np.float32))
    x_table = jnp.stack(
        [x_upper * turn_cos + x_lower * turn_sin, x_lower * turn_cos - x_upper * turn_sin]
    )
    x_parts = []
    for _ in range(3):
        part = lax.reduce_precision(x_table, 8, 7)
        x_parts.append(part.astype(BF16))
        x_table = x_table - part
    x_table = jnp.stack(x_parts)
    y_cos, y_sin = dft(np.arange(ny), np.arange(cells), GY)
    y_forward = jnp.asarray(table_parts(np.vstack([y_cos, y_sin]), 3))
    y_back = jnp.asarray(table_parts(np.vstack([y_cos.T, y_sin.T]), 2))
    start_table = np.hstack(dft(np.arange(GY // unit) * unit, np.arange(ny), GY, False))
    start_table = np.pad(start_table, ((0, -start_table.shape[0] % 8), (0, 0)))
    start_table = jnp.asarray(start_table.astype(np.float32))
    me_array = me.astype(jnp.int32)[None]

    keep, send, x_matrix, norm = partial_rows(
        me_array, info, sensitivity, direction, x_table, planes, slabs_group
    )
    got = [swap(value, 1, slabs) for value in send]
    grid = [
        row_cells(keep[c], got[c], info, start_table, y_forward, tiles, segment, c % 2)
        for c in range(coils)
    ]
    grid[-1], x_matrix, residual = lax.optimization_barrier((grid[-1], x_matrix, residual))
    x_matrix = transposed(x_matrix, planes // own)
    norms = [norm, squares(residual)]
    high_bits = bits[1:]
    orders = [high_bits[c % 2 :] + high_bits[: c % 2] for c in range(coils)]
    ways = [high_bits[c % 2 :] + high_bits[: c % 2] for c in range(coils)]
    grid = [sum_scatter(*value, ways[c % 2], slabs) for c, value in enumerate(grid)]
    grid[-1], x_matrix, norms = lax.optimization_barrier((grid[-1], x_matrix, norms))

    rows_back, loaded = [], []
    for c, order in enumerate(orders):
        spread, sums = run_tiles(tile_count, norms, *grid[c], tile_weight)
        norms = [sums]
        dims = spread.shape
        have = []
        for number, bit in enumerate(order[::-1]):
            if c == coils - 1:
                sums = sums + swap(sums, high_bits[-1 - number], slabs)
            other = swap(spread, bit, slabs)
            if c == coils - 1 and number < 3:
                loaded.append(load((sensitivity, direction, residual)[number]))
            if bit != order[0]:
                spread = jnp.stack([spread, other], axis=sum(1 for b in have if b > bit))
                have.append(bit)
                if c == coils - 1:
                    sums, spread, sensitivity, direction, residual, *loaded = lax.optimization_barrier(
                        (sums, spread, sensitivity, direction, residual, *loaded)
                    )
        spread, other = spread.reshape((-1,) + dims), other.reshape((-1,) + dims)
        if c == coils - 1:
            sums, spread, other, *loaded = lax.optimization_barrier((sums, spread, other, *loaded))
        mine = adjoint_rows(spread, other, info, start_table, y_back, segment, c % 2)
        rows_back += [mine, swap(mine, 1, slabs)]
    sums = sums + swap(sums, 1, slabs)
    sens, move, residual = loaded
    if slabs_group == 2:
        residual_next, res, norm = finish(
            me_array, sums, rows_back, sens, move, residual, x_matrix, planes
        )
    else:
        residual_next, res, norm = finish_deep(
            me_array, sums, rows_back, sens, move, residual, x_matrix, planes, slabs_group
        )

    pieces = 3
    x_next = None
    for number, bit in enumerate(reversed(bits)):
        norm, x_image = lax.optimization_barrier((norm, x_image))
        other = swap(norm, bit, slabs)
        if number < pieces:
            x_next = x_update(sums, x_image, move, number, pieces, x_next)
            x_next, x_image = lax.optimization_barrier((x_next, x_image))
        if bit > 1:
            norm, x_next = lax.optimization_barrier((norm + other, x_next))
    direction_next = direction_update(sums, norm, other, res, move)
    return (x_next, residual_next, direction_next)


def solution(mesh):
    image = P(None, "slab", "frames", None)
    placed = (image, image, image, P(None, None, "slab", None, None)) + (
        P("slab"),
        P("slab"),
        P("slab", None, None),
    )
    return jax.shard_map(
        body, mesh=mesh, in_specs=placed, out_specs=(image, image, image), check_vma=False
    )
```

```python
import math

import jax
import jax.numpy as jnp
import ml_dtypes
import numpy as np
from jax import lax
from jax.experimental import pallas as pl
from jax.experimental.pallas import tpu as pltpu
from jax.sharding import PartitionSpec as P

GX = 480
GY = 480
DAMPING = 0.1
HIGHEST = lax.Precision.HIGHEST
F32 = jnp.float32
BF16 = jnp.bfloat16
MIB = 1024 * 1024
FIELDS = 8


def dft(out_index, in_index, size, scaled=True):
    angle = (out_index[:, None] * in_index[None, :] % size) * (2.0 * math.pi / size)
    scale = 1.0 / math.sqrt(size) if scaled else 1.0
    return np.cos(angle) * scale, np.sin(angle) * scale


def table_parts(table, count):
    parts = []
    for _ in range(count):
        part = table.astype(ml_dtypes.bfloat16)
        parts.append(part)
        table = table - part.astype(np.float64)
    return np.stack(parts)


def split(value, count):
    parts = []
    for step in range(count):
        part = value.astype(BF16)
        parts.append(part)
        if step + 1 < count:
            value = value - part.astype(F32)
    return parts


def dot(a, b):
    return lax.dot_general(a, b, (((1,), (0,)), ((), ())), preferred_element_type=F32)


def six_products(lhs, rhs):
    rows = lhs[0].shape[0]
    first = dot(jnp.concatenate(lhs, axis=0), rhs[0])
    second = dot(jnp.concatenate(lhs[:2], axis=0), rhs[1])
    third = dot(lhs[0], rhs[2])
    small = first[2 * rows :] + second[rows:] + third
    return first[:rows] + (first[rows : 2 * rows] + second[:rows] + small)


def params(mib):
    return pltpu.CompilerParams(vmem_limit_bytes=mib * MIB)


def resident():
    return pl.BlockSpec(memory_space=pltpu.VMEM)


def in_hbm():
    return pl.BlockSpec(memory_space=pltpu.HBM)


def scalars():
    return pl.BlockSpec(memory_space=pltpu.SMEM)


def blocks(shape, index, steps):
    return resident() if steps == 1 else pl.BlockSpec(shape, index)


def load_kernel(from_hbm, out_ref, sem):
    copies = [
        pltpu.make_async_copy(from_hbm.at[piece], out_ref.at[piece], sem.at[piece])
        for piece in range(out_ref.shape[0])
    ]
    for copy in copies:
        copy.start()
    for copy in copies:
        copy.wait()


def load(value):
    return pl.pallas_call(
        load_kernel,
        in_specs=[in_hbm()],
        out_specs=resident(),
        out_shape=jax.ShapeDtypeStruct(value.shape, F32),
        scratch_shapes=[pltpu.SemaphoreType.DMA((value.shape[0],))],
        compiler_params=params(2),
        name="load",
    )(pltpu.with_memory_space_constraint(value, pltpu.HBM))


def squares_kernel(res_ref, norm_ref):
    rows = res_ref.shape[1]

    def step(row, total):
        return total + res_ref[0, row] * res_ref[0, row] + res_ref[1, row] * res_ref[1, row]

    total = lax.fori_loop(0, rows, step, jnp.zeros(res_ref.shape[2:], F32))
    total = jnp.sum(total, keepdims=True)
    first = lax.broadcasted_iota(jnp.int32, norm_ref.shape, 0) == 0
    norm_ref[...] = jnp.where(first, total, 0.0)


def squares(residual):
    return pl.pallas_call(
        squares_kernel,
        in_specs=[resident()],
        out_specs=resident(),
        out_shape=jax.ShapeDtypeStruct((8, 128), F32),
        compiler_params=params(8),
        name="squares",
    )(residual)


def x_kernel(first, sums_ref, x_ref, dir_ref, *refs):
    rows = x_ref.shape[0]
    step = sums_ref[0:1, 0:1] / sums_ref[1:2, 0:1]
    at = pl.ds(first + pl.program_id(0) * rows, rows)
    refs[-1][...] = x_ref[...] + step * dir_ref[at]


def x_update(sums, x_image, direction, piece, pieces, before):
    dims = x_image.shape
    flat = (-1,) + dims[2:]
    rows = dims[0] * dims[1] // pieces
    step = rows // 2
    given = [] if before is None else [before.reshape(flat)]
    block = pl.BlockSpec((step,) + dims[2:], lambda i: (2 * piece + i, 0, 0))
    out = pl.pallas_call(
        lambda *refs: x_kernel(piece * rows, *refs),
        grid=(2,),
        in_specs=[resident(), block, resident()] + [in_hbm()] * len(given),
        out_specs=block,
        out_shape=jax.ShapeDtypeStruct((dims[0] * dims[1],) + dims[2:], F32),
        input_output_aliases={3: 0} if given else {},
        compiler_params=params(16),
        name="x_update",
    )(sums, x_image.reshape(flat), direction.reshape(flat), *given)
    return out.reshape(dims)


def direction_kernel(sums_ref, one_ref, two_ref, res_ref, dir_ref, out_hbm, out_ref, sem):
    pieces = sem.shape[0]
    rows = out_ref.shape[0] // pieces
    ratio = (one_ref[0:1, 0:1] + two_ref[0:1, 0:1]) / sums_ref[0:1, 0:1]
    copies = []
    for piece in range(pieces):
        at = pl.ds(piece * rows, rows)
        out_ref[at] = res_ref[at] + ratio * dir_ref[at]
        copies.append(pltpu.make_async_copy(out_ref.at[at], out_hbm.at[at], sem.at[piece]))
        copies[-1].start()
    for copy in copies:
        copy.wait()


def direction_update(sums, one, two, residual, direction):
    dims = residual.shape
    flat = (-1,) + dims[2:]
    shape = (dims[0] * dims[1],) + dims[2:]
    out = pl.pallas_call(
        direction_kernel,
        in_specs=[resident()] * 5,
        out_specs=in_hbm(),
        out_shape=jax.ShapeDtypeStruct(shape, F32),
        scratch_shapes=[pltpu.VMEM(shape, F32), pltpu.SemaphoreType.DMA((6,))],
        compiler_params=params(16),
        name="direction_update",
    )(sums, one, two, residual.reshape(flat), direction.reshape(flat))
    return out.reshape(dims)


def row_matrix(info, table_ref, planes, parts):
    pairs, count, _ = info.shape
    half = count // 2
    info = info.reshape(pairs * count, FIELDS)
    depth = table_ref.shape[3]
    hot = lax.broadcasted_iota(jnp.int32, (pairs * count, GX), 1) == info[:, 0:1]
    hot = jnp.where(hot, 1.0, 0.0).astype(BF16)
    live = lax.broadcasted_iota(jnp.int32, (pairs * count, depth), 1) % planes == info[:, 1:2]
    matrix = []
    for part in range(parts):
        sides = [
            jnp.where(live, dot(hot, table_ref[part, side]), 0.0)
            .astype(BF16)
            .reshape(pairs, 2, 1, half, depth)
            for side in range(2)
        ]
        matrix.append(jnp.concatenate(sides, axis=2).reshape(pairs, 2 * count, depth))
    return matrix


def half_turn(value):
    return pltpu.roll(value, 4, 1)


def low_half(shape):
    return lax.broadcasted_iota(jnp.int32, shape, 1) < 4


def coil_parts(start, planes, sens_ref, dir_ref, out_ref):
    _, coils, rows, _, width = sens_ref.shape
    sides = out_ref.shape[0]
    own = planes // sides
    half = rows * own
    chunk = max(16 // own, 1)
    plane = pl.ds(start, planes)
    squares = jnp.zeros((planes, width), F32)
    for index in range(0, rows, chunk):
        at = slice(index, index + chunk)
        to = index * own
        d_re, d_im = dir_ref[0, at, plane], dir_ref[1, at, plane]
        squares += jnp.sum(d_re * d_re + d_im * d_im, axis=0)
        for coil in range(coils):
            s_re, s_im = sens_ref[0, coil, at, plane], sens_ref[1, coil, at, plane]
            pair = (s_re * d_re - s_im * d_im, s_re * d_im + s_im * d_re)
            for ri, value in enumerate(pair):
                if sides == 2:
                    value = value.reshape(chunk // 2, 2, planes, width)
                    one, two = value[:, 0], value[:, 1]
                    low = low_half(one.shape)
                    values = [jnp.where(low, one, half_turn(two)), jnp.where(low, half_turn(one), two)]
                else:
                    values = [value]
                where = slice(ri * half + to, ri * half + to + chunk * own)
                for side, value in enumerate(values):
                    value = value.reshape(chunk * own, width)
                    for number, part in enumerate(split(value, 3)):
                        out_ref[side, number, where, coil * width : (coil + 1) * width] = part
    return squares


def rows_kernel(
    planes, slabs_group, steps, me_ref, info_ref, sens_hbm, dir_hbm, table_ref, *refs
):
    pairs, _, count, _ = info_ref.shape
    coils, _, total, width = sens_hbm.shape[1:]
    keep_refs, send_refs = refs[:coils], refs[coils : 2 * coils]
    matrix_ref, norm_ref, one_ref, two_ref, sens_ref, dir_ref, sem = refs[2 * coils :]
    groups = total // planes

    def copies(group):
        at = pl.ds(pl.multiple_of(group * planes, planes), planes)
        return (
            pltpu.make_async_copy(sens_hbm.at[:, :, :, at], sens_ref.at[:, :, :, at], sem.at[group, 0]),
            pltpu.make_async_copy(dir_hbm.at[:, :, at], dir_ref.at[:, :, at], sem.at[group, 1]),
        )

    def start_copies():
        for group in range(groups):
            for copy in copies(group):
                copy.start()

    def wait_copies(group):
        for copy in copies(group):
            copy.wait()

    if steps == 1:
        start_copies()
    else:
        pl.when(pl.program_id(0) == 0)(start_copies)
    info = info_ref[...].reshape(pairs, 2 * count, FIELDS)
    own = planes // one_ref.shape[0]
    for part, value in enumerate(row_matrix(info, table_ref, own, 3)):
        matrix_ref[:, part] = value

    def coil_images(group, ref):
        start = pl.multiple_of(group * planes, planes)
        return coil_parts(start, planes, sens_ref, dir_ref, ref)

    def products(pair, image_ref):
        for side, out_refs in enumerate((keep_refs, send_refs)):
            rows = slice(2 * side * count, 2 * (side + 1) * count)
            matrix = [matrix_ref[pair, part, rows] for part in range(3)]
            slab = lax.rem(me_ref[0] + side, 2) if slabs_group == 2 else 0
            out = six_products(matrix, [image_ref[slab, part] for part in range(3)])
            for coil in range(coils):
                out_refs[coil][pair] = out[:, coil * width : (coil + 1) * width]

    squares = jnp.zeros((planes, width), F32)
    if slabs_group == 2:
        high = me_ref[0] // 2

        def step(index, squares):
            group = 2 * index
            wait_copies(group + 1)
            squares += coil_images(group + 1, two_ref)
            products(lax.bitwise_xor(group, high), one_ref)
            wait_copies(group + 2)
            squares += coil_images(group + 2, one_ref)
            products(lax.bitwise_xor(group + 1, high), two_ref)
            return squares

        wait_copies(0)
        squares = coil_images(0, one_ref)
        squares = lax.fori_loop(0, groups // 2 - 1, step, squares)
        wait_copies(groups - 1)
        squares += coil_images(groups - 1, two_ref)
        products(lax.bitwise_xor(groups - 2, high), one_ref)
        products(lax.bitwise_xor(groups - 1, high), two_ref)
    else:
        first = pl.program_id(0) * pairs

        @pl.when(first == 0)
        def _():
            for group in range(groups):
                wait_copies(group)

        group = lax.bitwise_xor(2 * first, me_ref[0]) // slabs_group
        fresh = coil_images(group, one_ref)
        squares = jnp.where(2 * first % slabs_group == 0, fresh, 0.0)
        for pair in range(pairs):
            products(pair, one_ref)
    amount = DAMPING * jnp.sum(squares, keepdims=True)
    at = lax.broadcasted_iota(jnp.int32, norm_ref.shape, 0)
    amount = jnp.where(at == 0, 0.0, amount)
    if steps == 1:
        norm_ref[...] = amount
    else:

        @pl.when(pl.program_id(0) == 0)
        def _():
            norm_ref[...] = jnp.zeros(norm_ref.shape, F32)

        norm_ref[...] += amount


def partial_rows(me, info, sens, direction, table, planes, slabs_group):
    pairs, _, count, _ = info.shape
    _, coils, rows, total, width = sens.shape
    depth = table.shape[3]
    step = min(pairs, 512 // (2 * count))
    steps = pairs // step
    shape = (2 * count, width)
    kept = jax.ShapeDtypeStruct((pairs,) + shape, F32)
    kept_block = blocks((step,) + shape, lambda i: (i, 0, 0), steps)
    shape = (3, 4 * count, depth)
    *values, matrix, norm = pl.pallas_call(
        lambda *refs: rows_kernel(planes, slabs_group, steps, *refs),
        grid=() if steps == 1 else (steps,),
        in_specs=[
            scalars(),
            blocks((step, 2, count, FIELDS), lambda i: (i, 0, 0, 0), steps),
            in_hbm(),
            in_hbm(),
            resident(),
        ],
        out_specs=[kept_block] * (2 * coils)
        + [
            blocks((step,) + shape, lambda i: (i, 0, 0, 0), steps),
            blocks((8, 128), lambda i: (0, 0), steps),
        ],
        out_shape=[kept] * (2 * coils)
        + [
            jax.ShapeDtypeStruct((pairs,) + shape, BF16),
            jax.ShapeDtypeStruct((8, 128), F32),
        ],
        scratch_shapes=[pltpu.VMEM((2 if slabs_group == 2 else 1, 3, depth, coils * width), BF16)] * 2
        + [
            pltpu.VMEM(sens.shape, F32),
            pltpu.VMEM(direction.shape, F32),
            pltpu.SemaphoreType.DMA((total // planes, 2)),
        ],
        compiler_params=params(40),
        name="partial_rows",
    )(
        me,
        info,
        pltpu.with_memory_space_constraint(sens, pltpu.HBM),
        pltpu.with_memory_space_constraint(direction, pltpu.HBM),
        table,
    )
    return values[:coils], values[coils:], matrix, norm


def side_of(pair, bit):
    return (pair >> bit) & 1, ((pair >> (bit + 1)) << bit) | (pair & ((1 << bit) - 1))


def of_side(pairs, bit, side):
    return [pair for pair in range(pairs) if side_of(pair, bit)[0] == side]


def start_turn(pairs, info_ref, start_ref):
    info = jnp.concatenate([info_ref[pair, 0] for pair in pairs], axis=0)
    starts = start_ref.shape[0]
    hot = lax.broadcasted_iota(jnp.int32, (info.shape[0], starts), 1) == info[:, 2:3]
    turn = jnp.dot(
        jnp.where(hot, 1.0, 0.0), start_ref[...], precision=HIGHEST, preferred_element_type=F32
    )
    width = turn.shape[1] // 2
    return info, turn[:, :width], turn[:, width:]


def segment_mask(info, cells, segment):
    at = lax.broadcasted_iota(jnp.int32, (info.shape[0], cells), 1)
    return (at >= info[:, 3:4]) & (at < info[:, 3:4] + segment)


def cells_kernel(
    tiles, segment, bit, side, keep_ref, got_ref, info_ref, start_ref, table_ref, out_ref
):
    chosen = of_side(keep_ref.shape[0], bit, side)
    pairs, count = len(chosen), keep_ref.shape[1] // 2
    cells = table_ref.shape[2]
    info, cos, sin = start_turn(chosen, info_ref, start_ref)
    both = [keep_ref[pair] + got_ref[pair] for pair in chosen]
    re = jnp.concatenate([value[:count] for value in both], axis=0)
    im = jnp.concatenate([value[count:] for value in both], axis=0)
    re, im = cos * re + sin * im, cos * im - sin * re
    value = [jnp.concatenate([re, im], axis=1), jnp.concatenate([im, -re], axis=1)]
    value = split(jnp.concatenate(value, axis=0), 3)
    out = six_products(value, [table_ref[part] for part in range(3)])
    mask = segment_mask(info, cells, segment)
    for ri in range(2):
        mine = out[ri * pairs * count : (ri + 1) * pairs * count]
        mine = jnp.where(mask, mine, 0.0).reshape(pairs, count // tiles, tiles, cells)
        out_ref[:, :, ri * cells : (ri + 1) * cells] = jnp.sum(mine, axis=1)


def row_cells(keep, got, info, start, table, tiles, segment, bit, side):
    pairs, double, width = keep.shape
    lines = 2 * table.shape[2]
    chunk = pairs if pairs <= 8 else 4
    steps = pairs // chunk
    rows = blocks((chunk, double, width), lambda i: (i, 0, 0), steps)
    return pl.pallas_call(
        lambda *refs: cells_kernel(tiles, segment, bit, side, *refs),
        grid=() if steps == 1 else (steps,),
        in_specs=[
            rows,
            rows,
            blocks((chunk, 1, double // 2, FIELDS), lambda i: (i, 0, 0, 0), steps),
            resident(),
            resident(),
        ],
        out_specs=blocks((chunk // 2, tiles, lines), lambda i: (i, 0, 0), steps),
        out_shape=jax.ShapeDtypeStruct((pairs // 2, tiles, lines), F32),
        compiler_params=params(24),
        name="row_cells",
    )(keep, got, info, start, table)


def adjoint_kernel(
    segment, bit, side, part, steps, cell_ref, info_ref, start_ref, table_ref, *refs
):
    out_ref = refs[-3] if part is not None else refs[0]
    if part is not None:
        from_hbm, to_ref, sem = refs[0], refs[-2], refs[-1]
        copies = [
            pltpu.make_async_copy(from_hbm.at[part, piece], to_ref.at[piece], sem.at[piece])
            for piece in range(to_ref.shape[0])
        ]

        def start_copies():
            for copy in copies:
                copy.start()

        def wait_copies():
            for copy in copies:
                copy.wait()

        if steps == 1:
            start_copies()
        else:
            pl.when(pl.program_id(0) == 0)(start_copies)
    chosen = of_side(info_ref.shape[0], bit, side)
    chunk, count = len(chosen), info_ref.shape[2]
    tiles = cell_ref.shape[1]
    cells = table_ref.shape[1] // 2
    info, cos, sin = start_turn(chosen, info_ref, start_ref)
    mask = segment_mask(info, cells, segment)
    both = []
    for ri in range(2):
        wide = []
        for place in range(chunk):
            wide += [cell_ref[place, :, ri * cells : (ri + 1) * cells]] * (count // tiles)
        both.append(jnp.where(mask, jnp.concatenate(wide, axis=0), 0.0))
    re, im = both
    value = [jnp.concatenate([re, -im], axis=1), jnp.concatenate([im, re], axis=1)]
    high, low = split(jnp.concatenate(value, axis=0), 2)
    first = dot(jnp.concatenate([high, low], axis=0), table_ref[0])
    total, rows = high.shape[0], chunk * count
    out = first[:total] + (first[total:] + dot(high, table_ref[1]))
    re, im = out[:rows], out[rows:]
    out_ref[:, :count] = (cos * re - sin * im).reshape(chunk, count, -1)
    out_ref[:, count:] = (cos * im + sin * re).reshape(chunk, count, -1)
    if part is not None:
        if steps == 1:
            wait_copies()
        else:
            pl.when(pl.program_id(0) == steps - 1)(wait_copies)


def adjoint_rows(value, info, start, table, segment, bit, side, large=None, part=None):
    half, tiles, lines = value.shape
    pairs, _, count, _ = info.shape
    width = table.shape[2]
    chunk = pairs if pairs <= 8 else 4
    steps = pairs // chunk
    more = large is not None
    return pl.pallas_call(
        lambda *refs: adjoint_kernel(segment, bit, side, part, steps, *refs),
        grid=() if steps == 1 else (steps,),
        in_specs=[
            blocks((chunk // 2, tiles, lines), lambda i: (i, 0, 0), steps),
            blocks((chunk, 1, count, FIELDS), lambda i: (i, 0, 0, 0), steps),
            resident(),
            resident(),
        ]
        + [in_hbm()] * more,
        out_specs=[blocks((chunk // 2, 2 * count, width), lambda i: (i, 0, 0), steps)]
        + [resident()] * more,
        out_shape=[jax.ShapeDtypeStruct((half, 2 * count, width), F32)]
        + ([jax.ShapeDtypeStruct(large.shape[1:], F32)] if more else []),
        scratch_shapes=[pltpu.SemaphoreType.DMA((large.shape[1],))] if more else [],
        compiler_params=params(24),
        name="adjoint_rows",
    )(
        value,
        info,
        start,
        table,
        *([pltpu.with_memory_space_constraint(large, pltpu.HBM)] if more else []),
    )


def tiles_kernel(coils, count_ref, norm_refs, weight_ref, *refs):
    tiles, _, cells = weight_ref.shape
    cell_refs, out_refs, sums_refs = refs[: 2 * coils], refs[2 * coils : 3 * coils], refs[3 * coils :]
    rows = []
    for keep, got in zip(cell_refs[::2], cell_refs[1::2]):
        grid = keep[...] + got[...]
        rows += [grid[:, ri * cells : (ri + 1) * cells] for ri in range(2)]
    found = []
    for tile in range(tiles):
        grid = jnp.concatenate([row[tile : tile + 1] for row in rows], axis=0).astype(BF16)
        found.append(
            lax.dot_general(
                grid, weight_ref[tile], (((1,), (1,)), ((), ())), preferred_element_type=F32
            )
        )
    spread = []
    for tile in range(tiles):
        live = lax.broadcasted_iota(jnp.int32, found[tile].shape, 1) < count_ref[tile]
        spread.append(dot(jnp.where(live, found[tile], 0.0).astype(BF16), weight_ref[tile]))
    total = 0.0
    for number, row in enumerate(rows):
        value = jnp.concatenate([piece[number : number + 1] for piece in spread], axis=0)
        total = total + row * value
        ri = number % 2
        out_refs[number // 2][:, ri * cells : (ri + 1) * cells] = value
    total = jnp.sum(total, keepdims=True)
    norm = norm_refs[0][...] + norm_refs[1][...]
    first = lax.broadcasted_iota(jnp.int32, norm.shape, 0) == 0
    norm = norm + jnp.where(first, 0.0, total)
    if sums_refs:
        sums_refs[0][...] = norm
    else:
        out_refs[-1][:, 2 * cells :] = jnp.concatenate([norm] * (tiles // norm.shape[0]), axis=0)


def run_tiles(count, norms, cells, weight, carry):
    coils = len(cells)
    tiles, lines = cells[0][0].shape
    shapes = [(tiles, lines + 128 * (carry and c == coils - 1)) for c in range(coils)]
    if not carry:
        shapes.append((8, 128))
    out = pl.pallas_call(
        lambda *refs: tiles_kernel(coils, refs[0], refs[1:3], *refs[3:]),
        in_specs=[scalars()] + [resident()] * (2 * coils + 3),
        out_specs=[resident()] * len(shapes),
        out_shape=[jax.ShapeDtypeStruct(shape, F32) for shape in shapes],
        compiler_params=params(8),
        name="tiles",
    )(count, *norms, weight, *[value for pair in cells for value in pair])
    return list(out[:coils]), list(out[coils:])


def turn_kernel(matrix_ref, out_ref):
    sides = out_ref.shape[1]
    rows = matrix_ref.shape[2] // sides
    for pair in range(matrix_ref.shape[0]):
        for side in range(sides):
            high, low = [
                matrix_ref[pair, part, side * rows : (side + 1) * rows].astype(F32) for part in range(2)
            ]
            value = jnp.concatenate([high, low, high], axis=0)
            out_ref[pair, side] = jnp.transpose(value).astype(BF16)


def transposed(matrix, sides):
    pairs, parts, rows, depth = matrix.shape
    step = min(pairs, 8)
    steps = pairs // step
    shape = (sides, depth, 3 * rows // sides)
    return pl.pallas_call(
        turn_kernel,
        grid=() if steps == 1 else (steps,),
        in_specs=[blocks((step, parts, rows, depth), lambda q: (q, 0, 0, 0), steps)],
        out_specs=blocks((step,) + shape, lambda q: (q, 0, 0, 0), steps),
        out_shape=jax.ShapeDtypeStruct((pairs,) + shape, BF16),
        compiler_params=params(12),
        name="transposed",
    )(matrix)


def back_rows(matrix, rows):
    high, low = split(rows, 2)
    return dot(matrix, jnp.concatenate([high, high, low], axis=0))


def back_group(odd, matrix, mine, got):
    first = back_rows(matrix(odd), jnp.where(odd == 0, mine, got))
    second = back_rows(matrix(1 - odd), jnp.where(odd == 0, got, mine))
    shape = (first.shape[0] // 8, 8, first.shape[1])
    first, second = first.reshape(shape), second.reshape(shape)
    low = low_half(shape)
    one = jnp.where(low, first, half_turn(second))
    two = jnp.where(low, half_turn(first), second)
    value = jnp.concatenate([one[:, None], two[:, None]], axis=1)
    return value.reshape(16 * shape[0], shape[2])


def combine(back, plane, step, sens_refs, dir_ref, res_ref, out_ref):
    coils, rows, _, width = sens_refs[0].shape
    planes = plane.stop - plane.start
    half = rows * planes
    total = [DAMPING * dir_ref[ri, :, plane].reshape(half, width) for ri in range(2)]
    for coil in range(coils):
        lanes = slice(coil * width, (coil + 1) * width)
        v_re, v_im = back[:half, lanes], back[half:, lanes]
        s_re, s_im = [ref[coil, :, plane].reshape(half, width) for ref in sens_refs]
        total[0] += s_re * v_re + s_im * v_im
        total[1] += s_re * v_im - s_im * v_re
    squares = 0.0
    for ri in range(2):
        value = res_ref[ri, :, plane].reshape(half, width) - step * total[ri]
        value = value.reshape(rows, planes, width)
        out_ref[ri, :, plane] = value
        squares = squares + jnp.sum(value * value, axis=0)
    return squares


def finish_kernel(planes, me_ref, sums_ref, re_ref, im_ref, dir_ref, res_ref, matrix_ref, *refs):
    coils, rows, total, width = re_ref.shape
    row_refs = refs[: 4 * coils]
    out_hbm, out_ref, norm_ref, sem = refs[4 * coils :]
    step = sums_ref[0:1, 0:1] / sums_ref[1:2, 0:1]
    squares = jnp.zeros((planes, width), F32)
    copies = []
    for group in range(total // planes):
        pair, odd = lax.bitwise_xor(group, me_ref[0] // 2), lax.rem(me_ref[0], 2)
        values = []
        for coil in range(coils):
            side, place = side_of(pair, coil % 2)
            for k in range(2):
                one, two = row_refs[4 * coil + k], row_refs[4 * coil + 2 + k]
                values.append(jnp.where(side == 0, one[place], two[place]))
        mine = jnp.concatenate(values[::2], axis=1)
        got = jnp.concatenate(values[1::2], axis=1)
        back = back_group(odd, lambda side: matrix_ref[pair, side], mine, got)
        plane = slice(group * planes, (group + 1) * planes)
        squares += combine(back, plane, step, (re_ref, im_ref), dir_ref, res_ref, out_ref)
        at = pl.ds(group * planes, planes)
        copies.append(
            pltpu.make_async_copy(out_ref.at[:, :, at], out_hbm.at[:, :, at], sem.at[group])
        )
        copies[-1].start()
    for copy in copies:
        copy.wait()
    norm_ref[...] = jnp.broadcast_to(jnp.sum(squares, keepdims=True), norm_ref.shape)


def finish(me, sums, rows, sens, direction, residual, matrix, planes):
    kept = jax.ShapeDtypeStruct(residual.shape, F32)
    return pl.pallas_call(
        lambda *refs: finish_kernel(planes, *refs),
        in_specs=[scalars()] + [resident()] * (6 + len(rows)),
        out_specs=[in_hbm(), resident(), resident()],
        out_shape=[kept, kept, jax.ShapeDtypeStruct(sums.shape, F32)],
        scratch_shapes=[pltpu.SemaphoreType.DMA((residual.shape[2] // planes,))],
        compiler_params=params(16),
        name="finish",
    )(me, sums, *sens, direction, residual, matrix, *rows)


def finish_deep_kernel(
    planes, me_ref, sums_ref, re_ref, im_ref, dir_ref, res_ref, matrix_ref, *refs
):
    coils = re_ref.shape[0]
    row_refs = refs[: 2 * coils]
    out_ref, norm_ref, squares_ref, sum_ref = refs[2 * coils :]
    group, pair = pl.program_id(0), pl.program_id(1)
    rows = [jnp.concatenate([ref[0] for ref in row_refs[k::2]], axis=1) for k in range(2)]
    back = back_rows(matrix_ref[0, 0], jnp.concatenate(rows, axis=0))

    @pl.when((group == 0) & (pair == 0))
    def _():
        squares_ref[...] = jnp.zeros(squares_ref.shape, F32)

    @pl.when(pair == 0)
    def _():
        sum_ref[...] = back

    @pl.when(pair > 0)
    def _():
        sum_ref[...] += back

    @pl.when(pair == pl.num_programs(1) - 1)
    def _():
        step = sums_ref[0:1, 0:1] / sums_ref[1:2, 0:1]
        squares_ref[...] += combine(
            sum_ref[...], slice(0, planes), step, (re_ref, im_ref), dir_ref, res_ref, out_ref
        )
        total = jnp.sum(squares_ref[...], keepdims=True)
        norm_ref[...] = jnp.broadcast_to(total, norm_ref.shape)


def finish_deep(me, sums, rows, sens, direction, residual, matrix, planes, slabs_group):
    coils, height, total, width = sens[0].shape
    double = rows[0].shape[1]
    groups, deep = total // planes, slabs_group // 2

    def pair(i, j, me):
        return lax.bitwise_xor(i, me[0] // slabs_group) * deep + j

    row_block = pl.BlockSpec((1, double, width), lambda i, j, me: (pair(i, j, me), 0, 0))
    image = pl.BlockSpec((2, height, planes, width), lambda i, j, me: (0, 0, i, 0))
    small = pl.BlockSpec(sums.shape, lambda i, j, me: (0, 0))
    out, norm = pl.pallas_call(
        lambda *refs: finish_deep_kernel(planes, *refs),
        grid_spec=pltpu.PrefetchScalarGridSpec(
            num_scalar_prefetch=1,
            grid=(groups, deep),
            in_specs=[
                small,
                pl.BlockSpec((coils, height, planes, width), lambda i, j, me: (0, 0, i, 0)),
                pl.BlockSpec((coils, height, planes, width), lambda i, j, me: (0, 0, i, 0)),
                image,
                image,
                pl.BlockSpec((1,) + matrix.shape[1:], lambda i, j, me: (pair(i, j, me), 0, 0, 0)),
            ]
            + [row_block] * len(rows),
            out_specs=[image, small],
            scratch_shapes=[
                pltpu.VMEM((planes, width), F32),
                pltpu.VMEM((2 * height * planes, coils * width), F32),
            ],
        ),
        out_shape=[
            jax.ShapeDtypeStruct(residual.shape, F32),
            jax.ShapeDtypeStruct(sums.shape, F32),
        ],
        compiler_params=params(32),
        name="finish_deep",
    )(me, sums, *sens, direction, residual, matrix, *rows)
    return out, out, norm


def swap(value, bit, slabs):
    return lax.ppermute(value, "slab", [(i, i ^ bit) for i in range(slabs)])


def sum_scatter(keep, send, bits, slabs):
    dims = keep.shape[1:]
    left = sorted(bits, reverse=True)
    for number, bit in enumerate(bits):
        axis = left.index(bit)
        left.pop(axis)
        if number > 0:
            value = (keep + got).reshape((2,) * (len(left) + 1) + dims)
            keep = lax.index_in_dim(value, 0, axis, keepdims=False)
            send = lax.index_in_dim(value, 1, axis, keepdims=False)
        got = swap(send, bit, slabs)
    return keep, got


def gather(value, bits, slabs):
    have = []
    for bit in bits:
        other = swap(value, bit, slabs)
        value = jnp.stack([value, other], axis=sum(1 for b in have if b > bit))
        have.append(bit)
    return value


def body(x_image, residual, direction, sensitivity, tile_block, tile_count, tile_weight):
    _, coils, rows, plane_count, ny = sensitivity.shape
    tiles, _, cells = tile_weight.shape
    slabs = lax.axis_size("slab")
    me = lax.axis_index("slab")
    lines = plane_count * GY // slabs
    segment = min(lines, GY)
    per_gx = lines // segment
    unit = math.gcd(cells, segment)
    segments = -(-(segment - unit + cells) // segment)
    planes = 8 if rows % 2 == 0 else 16
    slabs_group = planes * GY // lines
    own = planes // 2 if slabs_group == 2 else planes
    pairs = slabs // 2
    bits = [1 << i for i in range(slabs.bit_length() - 1)]

    first = tile_block * cells
    start = first % segment
    base = (me * lines) % GY
    info = []
    for k in range(segments):
        row = jnp.minimum(first // segment + k, GX * per_gx - 1)
        plane = (me * lines + (row % per_gx) * segment) // GY
        turn = (base + start - segment * k) % GY // unit
        fields = [row // per_gx, plane % own, turn, segment * k - start]
        info.append(jnp.stack(fields + [jnp.zeros_like(row)] * (FIELDS - len(fields)), axis=1))
    info = jnp.concatenate(info, axis=0)

    have = []
    for number, bit in enumerate(reversed(bits)):
        other = swap(info, bit, slabs)
        info = jnp.stack([info, other], axis=sum(1 for b in have if b > bit))
        have.append(bit)
    info = info.reshape(pairs, 2, segments * tiles, FIELDS)

    x_cos, x_sin = dft(np.arange(GX), np.repeat(np.arange(rows), own), GX)
    angle = (jnp.arange(GX, dtype=jnp.int32) * (me * rows) % GX).astype(F32) * (2 * math.pi / GX)
    turn_cos, turn_sin = jnp.cos(angle)[:, None], jnp.sin(angle)[:, None]
    x_upper = jnp.asarray(np.hstack([x_cos, x_sin]).astype(np.float32))
    x_lower = jnp.asarray(np.hstack([-x_sin, x_cos]).astype(np.float32))
    x_table = jnp.stack(
        [x_upper * turn_cos + x_lower * turn_sin, x_lower * turn_cos - x_upper * turn_sin]
    )
    x_parts = []
    for _ in range(3):
        part = lax.reduce_precision(x_table, 8, 7)
        x_parts.append(part.astype(BF16))
        x_table = x_table - part
    x_table = jnp.stack(x_parts)
    y_cos, y_sin = dft(np.arange(ny), np.arange(cells), GY)
    y_forward = jnp.asarray(table_parts(np.vstack([y_cos, y_sin]), 3))
    y_back = jnp.asarray(table_parts(np.vstack([y_cos.T, y_sin.T]), 2))
    start_table = np.hstack(dft(np.arange(GY // unit) * unit, np.arange(ny), GY, False))
    start_table = np.pad(start_table, ((0, -start_table.shape[0] % 8), (0, 0)))
    start_table = jnp.asarray(start_table.astype(np.float32))
    me_array = me.astype(jnp.int32)[None]

    keep, send, x_matrix, norm = partial_rows(
        me_array, info, sensitivity, direction, x_table, planes, slabs_group
    )
    got = [swap(value, 1, slabs) for value in send]
    grid = []
    for c in range(coils):
        send, stay = [
            row_cells(keep[c], got[c], info, start_table, y_forward, tiles, segment, c % 2, side)
            for side in (1, 0)
        ]
        grid.append([stay, send])
    grid[-1][0], x_matrix, residual = lax.optimization_barrier((grid[-1][0], x_matrix, residual))
    x_matrix = transposed(x_matrix, planes // own)
    norms = [norm, squares(residual)]
    high_bits = bits[1:]
    orders = [high_bits[c % 2 :] + high_bits[: c % 2] for c in range(coils)]
    grid = [sum_scatter(*value, order, slabs) for value, order in zip(grid, orders)]
    grid[-1], x_matrix, norms = lax.optimization_barrier((grid[-1], x_matrix, norms))

    spread, sums = run_tiles(tile_count, norms, grid, tile_weight, False)
    rows_back, sens, loaded, inputs = [], [], [], [direction, residual]
    dims = [value.shape for value in spread]
    orders = [high_bits[c % 2 :] + high_bits[: c % 2] for c in range(coils)]
    have = [[] for _ in range(coils)]
    for number in range(len(high_bits)):
        ways = [order[-1 - number] for order in orders]
        other = [swap(value, bit, slabs) for value, bit in zip(spread, ways)]
        if not False:
            sums = [sums[0] + swap(sums[0], high_bits[-1 - number], slabs)]
        if 1 <= number < 1 + 2:
            loaded.append(load(inputs[number - 1]))
        if number == len(high_bits) - 1:
            for c in range(coils):
                had = spread[c].reshape((-1,) + dims[c])
                mine, part = adjoint_rows(
                    had, info, start_table, y_back, segment, c % 2, 0, sensitivity, c
                )
                sens.append(part)
                rows_back.append([mine, swap(mine, 1, slabs)])
        else:
            for c in range(coils):
                axis = sum(1 for b in have[c] if b > ways[c])
                spread[c] = jnp.stack([spread[c], other[c]], axis=axis)
                have[c].append(ways[c])
        spread, other, sums, loaded, inputs = lax.optimization_barrier((spread, other, sums, loaded, inputs))
    for c in range(coils):
        got = other[c].reshape((-1,) + dims[c])
        (mine,) = adjoint_rows(got, info, start_table, y_back, segment, c % 2, 1)
        rows_back[c] += [mine, swap(mine, 1, slabs)]
    sums = sums[0] + swap(sums[0], 1, slabs)
    move, residual = loaded
    if slabs_group == 2:
        rows_back = [value for values in rows_back for value in values]
    else:
        both = []
        for c, (one, near_one, two, near_two) in enumerate(rows_back):
            shape = (pairs >> (c % 2 + 1), 1 << (c % 2)) + one.shape[1:]
            for had, got in ((one, two), (near_one, near_two)):
                value = jnp.stack([had.reshape(shape), got.reshape(shape)], axis=1)
                both.append(value.reshape((pairs,) + one.shape[1:]))
        rows_back = both
    if slabs_group == 2:
        residual_next, res, norm = finish(
            me_array, sums, rows_back, sens, move, residual, x_matrix, planes
        )
    else:
        residual_next, res, norm = finish_deep(
            me_array, sums, rows_back, sens, move, residual, x_matrix, planes, slabs_group
        )

    pieces = 3
    x_next = None
    for number, bit in enumerate(reversed(bits)):
        norm, x_image = lax.optimization_barrier((norm, x_image))
        other = swap(norm, bit, slabs)
        if number < pieces:
            x_next = x_update(sums, x_image, move, number, pieces, x_next)
            x_next, x_image = lax.optimization_barrier((x_next, x_image))
        if bit > 1:
            norm, x_next = lax.optimization_barrier((norm + other, x_next))
    direction_next = direction_update(sums, norm, other, res, move)
    return (x_next, residual_next, direction_next)


def solution(mesh):
    image = P(None, "slab", "frames", None)
    placed = (image, image, image, P(None, None, "slab", None, None)) + (
        P("slab"),
        P("slab"),
        P("slab", None, None),
    )
    return jax.shard_map(
        body, mesh=mesh, in_specs=placed, out_specs=(image, image, image), check_vma=False
    )
```

```python
import math

import jax
import jax.numpy as jnp
import ml_dtypes
import numpy as np
from jax import lax
from jax.experimental import pallas as pl
from jax.experimental.pallas import tpu as pltpu
from jax.sharding import PartitionSpec as P

GX = 480
GY = 480
DAMPING = 0.1
HIGHEST = lax.Precision.HIGHEST
F32 = jnp.float32
BF16 = jnp.bfloat16
MIB = 1024 * 1024
FIELDS = 8


def dft(out_index, in_index, size, scaled=True):
    angle = (out_index[:, None] * in_index[None, :] % size) * (2.0 * math.pi / size)
    scale = 1.0 / math.sqrt(size) if scaled else 1.0
    return np.cos(angle) * scale, np.sin(angle) * scale


def table_parts(table, count):
    parts = []
    for _ in range(count):
        part = table.astype(ml_dtypes.bfloat16)
        parts.append(part)
        table = table - part.astype(np.float64)
    return np.stack(parts)


def split(value, count):
    parts = []
    for step in range(count):
        part = value.astype(BF16)
        parts.append(part)
        if step + 1 < count:
            value = value - part.astype(F32)
    return parts


def dot(a, b):
    return lax.dot_general(a, b, (((1,), (0,)), ((), ())), preferred_element_type=F32)


def six_products(lhs, rhs):
    rows = lhs[0].shape[0]
    first = dot(jnp.concatenate(lhs, axis=0), rhs[0])
    second = dot(jnp.concatenate(lhs[:2], axis=0), rhs[1])
    third = dot(lhs[0], rhs[2])
    small = first[2 * rows :] + second[rows:] + third
    return first[:rows] + (first[rows : 2 * rows] + second[:rows] + small)


def params(mib):
    return pltpu.CompilerParams(vmem_limit_bytes=mib * MIB)


def resident():
    return pl.BlockSpec(memory_space=pltpu.VMEM)


def in_hbm():
    return pl.BlockSpec(memory_space=pltpu.HBM)


def scalars():
    return pl.BlockSpec(memory_space=pltpu.SMEM)


def blocks(shape, index, steps):
    return resident() if steps == 1 else pl.BlockSpec(shape, index)


def load_kernel(from_hbm, out_ref, sem):
    copies = [
        pltpu.make_async_copy(from_hbm.at[piece], out_ref.at[piece], sem.at[piece])
        for piece in range(out_ref.shape[0])
    ]
    for copy in copies:
        copy.start()
    for copy in copies:
        copy.wait()


def load(value):
    return pl.pallas_call(
        load_kernel,
        in_specs=[in_hbm()],
        out_specs=resident(),
        out_shape=jax.ShapeDtypeStruct(value.shape, F32),
        scratch_shapes=[pltpu.SemaphoreType.DMA((value.shape[0],))],
        compiler_params=params(2),
        name="load",
    )(pltpu.with_memory_space_constraint(value, pltpu.HBM))


def squares_kernel(res_ref, norm_ref):
    rows = res_ref.shape[1]

    def step(row, total):
        return total + res_ref[0, row] * res_ref[0, row] + res_ref[1, row] * res_ref[1, row]

    total = lax.fori_loop(0, rows, step, jnp.zeros(res_ref.shape[2:], F32))
    total = jnp.sum(total, keepdims=True)
    first = lax.broadcasted_iota(jnp.int32, norm_ref.shape, 0) == 0
    norm_ref[...] = jnp.where(first, total, 0.0)


def squares(residual):
    return pl.pallas_call(
        squares_kernel,
        in_specs=[resident()],
        out_specs=resident(),
        out_shape=jax.ShapeDtypeStruct((8, 128), F32),
        compiler_params=params(8),
        name="squares",
    )(residual)


def x_kernel(first, sums_ref, x_ref, dir_ref, *refs):
    rows = x_ref.shape[0]
    step = sums_ref[0:1, 0:1] / sums_ref[1:2, 0:1]
    at = pl.ds(first + pl.program_id(0) * rows, rows)
    refs[-1][...] = x_ref[...] + step * dir_ref[at]


def x_update(sums, x_image, direction, piece, pieces, before):
    dims = x_image.shape
    flat = (-1,) + dims[2:]
    rows = dims[0] * dims[1] // pieces
    step = rows // 2
    given = [] if before is None else [before.reshape(flat)]
    block = pl.BlockSpec((step,) + dims[2:], lambda i: (2 * piece + i, 0, 0))
    out = pl.pallas_call(
        lambda *refs: x_kernel(piece * rows, *refs),
        grid=(2,),
        in_specs=[resident(), block, resident()] + [in_hbm()] * len(given),
        out_specs=block,
        out_shape=jax.ShapeDtypeStruct((dims[0] * dims[1],) + dims[2:], F32),
        input_output_aliases={3: 0} if given else {},
        compiler_params=params(16),
        name="x_update",
    )(sums, x_image.reshape(flat), direction.reshape(flat), *given)
    return out.reshape(dims)


def direction_kernel(sums_ref, one_ref, two_ref, res_ref, dir_ref, out_hbm, out_ref, sem):
    pieces = sem.shape[0]
    rows = out_ref.shape[0] // pieces
    ratio = (one_ref[0:1, 0:1] + two_ref[0:1, 0:1]) / sums_ref[0:1, 0:1]
    copies = []
    for piece in range(pieces):
        at = pl.ds(piece * rows, rows)
        out_ref[at] = res_ref[at] + ratio * dir_ref[at]
        copies.append(pltpu.make_async_copy(out_ref.at[at], out_hbm.at[at], sem.at[piece]))
        copies[-1].start()
    for copy in copies:
        copy.wait()


def direction_update(sums, one, two, residual, direction):
    dims = residual.shape
    flat = (-1,) + dims[2:]
    shape = (dims[0] * dims[1],) + dims[2:]
    out = pl.pallas_call(
        direction_kernel,
        in_specs=[resident()] * 5,
        out_specs=in_hbm(),
        out_shape=jax.ShapeDtypeStruct(shape, F32),
        scratch_shapes=[pltpu.VMEM(shape, F32), pltpu.SemaphoreType.DMA((6,))],
        compiler_params=params(16),
        name="direction_update",
    )(sums, one, two, residual.reshape(flat), direction.reshape(flat))
    return out.reshape(dims)


def row_matrix(info, table_ref, planes, parts):
    pairs, count, _ = info.shape
    half = count // 2
    info = info.reshape(pairs * count, FIELDS)
    depth = table_ref.shape[3]
    hot = lax.broadcasted_iota(jnp.int32, (pairs * count, GX), 1) == info[:, 0:1]
    hot = jnp.where(hot, 1.0, 0.0).astype(BF16)
    live = lax.broadcasted_iota(jnp.int32, (pairs * count, depth), 1) % planes == info[:, 1:2]
    matrix = []
    for part in range(parts):
        sides = [
            jnp.where(live, dot(hot, table_ref[part, side]), 0.0)
            .astype(BF16)
            .reshape(pairs, 2, 1, half, depth)
            for side in range(2)
        ]
        matrix.append(jnp.concatenate(sides, axis=2).reshape(pairs, 2 * count, depth))
    return matrix


def half_turn(value):
    return pltpu.roll(value, 4, 1)


def low_half(shape):
    return lax.broadcasted_iota(jnp.int32, shape, 1) < 4


def coil_parts(start, planes, sens_ref, dir_ref, out_ref):
    _, coils, rows, _, width = sens_ref.shape
    sides = out_ref.shape[0]
    own = planes // sides
    half = rows * own
    chunk = max(16 // own, 1)
    plane = pl.ds(start, planes)
    squares = jnp.zeros((planes, width), F32)
    for index in range(0, rows, chunk):
        at = slice(index, index + chunk)
        to = index * own
        d_re, d_im = dir_ref[0, at, plane], dir_ref[1, at, plane]
        squares += jnp.sum(d_re * d_re + d_im * d_im, axis=0)
        for coil in range(coils):
            s_re, s_im = sens_ref[0, coil, at, plane], sens_ref[1, coil, at, plane]
            pair = (s_re * d_re - s_im * d_im, s_re * d_im + s_im * d_re)
            for ri, value in enumerate(pair):
                if sides == 2:
                    value = value.reshape(chunk // 2, 2, planes, width)
                    one, two = value[:, 0], value[:, 1]
                    low = low_half(one.shape)
                    values = [jnp.where(low, one, half_turn(two)), jnp.where(low, half_turn(one), two)]
                else:
                    values = [value]
                where = slice(ri * half + to, ri * half + to + chunk * own)
                for side, value in enumerate(values):
                    value = value.reshape(chunk * own, width)
                    for number, part in enumerate(split(value, 3)):
                        out_ref[side, number, where, coil * width : (coil + 1) * width] = part
    return squares


def rows_kernel(
    planes, slabs_group, steps, me_ref, info_ref, sens_hbm, dir_hbm, table_ref, *refs
):
    pairs, _, count, _ = info_ref.shape
    coils, _, total, width = sens_hbm.shape[1:]
    keep_refs, send_refs = refs[:coils], refs[coils : 2 * coils]
    matrix_ref, norm_ref, one_ref, two_ref, sens_ref, dir_ref, sem = refs[2 * coils :]
    groups = total // planes

    def copies(group):
        at = pl.ds(pl.multiple_of(group * planes, planes), planes)
        return (
            pltpu.make_async_copy(sens_hbm.at[:, :, :, at], sens_ref.at[:, :, :, at], sem.at[group, 0]),
            pltpu.make_async_copy(dir_hbm.at[:, :, at], dir_ref.at[:, :, at], sem.at[group, 1]),
        )

    def start_copies():
        for group in range(groups):
            for copy in copies(group):
                copy.start()

    def wait_copies(group):
        for copy in copies(group):
            copy.wait()

    if steps == 1:
        start_copies()
    else:
        pl.when(pl.program_id(0) == 0)(start_copies)
    info = info_ref[...].reshape(pairs, 2 * count, FIELDS)
    own = planes // one_ref.shape[0]
    for part, value in enumerate(row_matrix(info, table_ref, own, 3)):
        matrix_ref[:, part] = value

    def coil_images(group, ref):
        start = pl.multiple_of(group * planes, planes)
        return coil_parts(start, planes, sens_ref, dir_ref, ref)

    def products(pair, image_ref):
        for side, out_refs in enumerate((keep_refs, send_refs)):
            rows = slice(2 * side * count, 2 * (side + 1) * count)
            matrix = [matrix_ref[pair, part, rows] for part in range(3)]
            slab = lax.rem(me_ref[0] + side, 2) if slabs_group == 2 else 0
            out = six_products(matrix, [image_ref[slab, part] for part in range(3)])
            for coil in range(coils):
                out_refs[coil][pair] = out[:, coil * width : (coil + 1) * width]

    squares = jnp.zeros((planes, width), F32)
    if slabs_group == 2:
        high = me_ref[0] // 2

        def step(index, squares):
            group = 2 * index
            wait_copies(group + 1)
            squares += coil_images(group + 1, two_ref)
            products(lax.bitwise_xor(group, high), one_ref)
            wait_copies(group + 2)
            squares += coil_images(group + 2, one_ref)
            products(lax.bitwise_xor(group + 1, high), two_ref)
            return squares

        wait_copies(0)
        squares = coil_images(0, one_ref)
        squares = lax.fori_loop(0, groups // 2 - 1, step, squares)
        wait_copies(groups - 1)
        squares += coil_images(groups - 1, two_ref)
        products(lax.bitwise_xor(groups - 2, high), one_ref)
        products(lax.bitwise_xor(groups - 1, high), two_ref)
    else:
        first = pl.program_id(0) * pairs

        @pl.when(first == 0)
        def _():
            for group in range(groups):
                wait_copies(group)

        group = lax.bitwise_xor(2 * first, me_ref[0]) // slabs_group
        fresh = coil_images(group, one_ref)
        squares = jnp.where(2 * first % slabs_group == 0, fresh, 0.0)
        for pair in range(pairs):
            products(pair, one_ref)
    amount = DAMPING * jnp.sum(squares, keepdims=True)
    at = lax.broadcasted_iota(jnp.int32, norm_ref.shape, 0)
    amount = jnp.where(at == 0, 0.0, amount)
    if steps == 1:
        norm_ref[...] = amount
    else:

        @pl.when(pl.program_id(0) == 0)
        def _():
            norm_ref[...] = jnp.zeros(norm_ref.shape, F32)

        norm_ref[...] += amount


def partial_rows(me, info, sens, direction, table, planes, slabs_group):
    pairs, _, count, _ = info.shape
    _, coils, rows, total, width = sens.shape
    depth = table.shape[3]
    step = min(pairs, 512 // (2 * count))
    steps = pairs // step
    shape = (2 * count, width)
    kept = jax.ShapeDtypeStruct((pairs,) + shape, F32)
    kept_block = blocks((step,) + shape, lambda i: (i, 0, 0), steps)
    shape = (3, 4 * count, depth)
    *values, matrix, norm = pl.pallas_call(
        lambda *refs: rows_kernel(planes, slabs_group, steps, *refs),
        grid=() if steps == 1 else (steps,),
        in_specs=[
            scalars(),
            blocks((step, 2, count, FIELDS), lambda i: (i, 0, 0, 0), steps),
            in_hbm(),
            in_hbm(),
            resident(),
        ],
        out_specs=[kept_block] * (2 * coils)
        + [
            blocks((step,) + shape, lambda i: (i, 0, 0, 0), steps),
            blocks((8, 128), lambda i: (0, 0), steps),
        ],
        out_shape=[kept] * (2 * coils)
        + [
            jax.ShapeDtypeStruct((pairs,) + shape, BF16),
            jax.ShapeDtypeStruct((8, 128), F32),
        ],
        scratch_shapes=[pltpu.VMEM((2 if slabs_group == 2 else 1, 3, depth, coils * width), BF16)] * 2
        + [
            pltpu.VMEM(sens.shape, F32),
            pltpu.VMEM(direction.shape, F32),
            pltpu.SemaphoreType.DMA((total // planes, 2)),
        ],
        compiler_params=params(40),
        name="partial_rows",
    )(
        me,
        info,
        pltpu.with_memory_space_constraint(sens, pltpu.HBM),
        pltpu.with_memory_space_constraint(direction, pltpu.HBM),
        table,
    )
    return values[:coils], values[coils:], matrix, norm


def side_of(pair, bit):
    return (pair >> bit) & 1, ((pair >> (bit + 1)) << bit) | (pair & ((1 << bit) - 1))


def of_side(pairs, bit, side):
    return [pair for pair in range(pairs) if side_of(pair, bit)[0] == side]


def start_turn(pairs, info_ref, start_ref):
    info = jnp.concatenate([info_ref[pair, 0] for pair in pairs], axis=0)
    starts = start_ref.shape[0]
    hot = lax.broadcasted_iota(jnp.int32, (info.shape[0], starts), 1) == info[:, 2:3]
    turn = jnp.dot(
        jnp.where(hot, 1.0, 0.0), start_ref[...], precision=HIGHEST, preferred_element_type=F32
    )
    width = turn.shape[1] // 2
    return info, turn[:, :width], turn[:, width:]


def segment_mask(info, cells, segment):
    at = lax.broadcasted_iota(jnp.int32, (info.shape[0], cells), 1)
    return (at >= info[:, 3:4]) & (at < info[:, 3:4] + segment)


def cells_kernel(
    tiles, segment, bit, side, keep_ref, got_ref, info_ref, start_ref, table_ref, out_ref
):
    chosen = of_side(keep_ref.shape[0], bit, side)
    pairs, count = len(chosen), keep_ref.shape[1] // 2
    cells = table_ref.shape[2]
    info, cos, sin = start_turn(chosen, info_ref, start_ref)
    both = [keep_ref[pair] + got_ref[pair] for pair in chosen]
    re = jnp.concatenate([value[:count] for value in both], axis=0)
    im = jnp.concatenate([value[count:] for value in both], axis=0)
    re, im = cos * re + sin * im, cos * im - sin * re
    value = [jnp.concatenate([re, im], axis=1), jnp.concatenate([im, -re], axis=1)]
    value = split(jnp.concatenate(value, axis=0), 3)
    out = six_products(value, [table_ref[part] for part in range(3)])
    mask = segment_mask(info, cells, segment)
    for ri in range(2):
        mine = out[ri * pairs * count : (ri + 1) * pairs * count]
        mine = jnp.where(mask, mine, 0.0).reshape(pairs, count // tiles, tiles, cells)
        out_ref[:, :, ri * cells : (ri + 1) * cells] = jnp.sum(mine, axis=1)


def row_cells(keep, got, info, start, table, tiles, segment, bit, side):
    pairs, double, width = keep.shape
    lines = 2 * table.shape[2]
    chunk = pairs if pairs <= 8 else 4
    steps = pairs // chunk
    rows = blocks((chunk, double, width), lambda i: (i, 0, 0), steps)
    return pl.pallas_call(
        lambda *refs: cells_kernel(tiles, segment, bit, side, *refs),
        grid=() if steps == 1 else (steps,),
        in_specs=[
            rows,
            rows,
            blocks((chunk, 1, double // 2, FIELDS), lambda i: (i, 0, 0, 0), steps),
            resident(),
            resident(),
        ],
        out_specs=blocks((chunk // 2, tiles, lines), lambda i: (i, 0, 0), steps),
        out_shape=jax.ShapeDtypeStruct((pairs // 2, tiles, lines), F32),
        compiler_params=params(24),
        name="row_cells",
    )(keep, got, info, start, table)


def adjoint_kernel(
    segment, bit, side, part, steps, cell_ref, info_ref, start_ref, table_ref, *refs
):
    out_ref = refs[-3] if part is not None else refs[0]
    if part is not None:
        from_hbm, to_ref, sem = refs[0], refs[-2], refs[-1]
        copies = [
            pltpu.make_async_copy(from_hbm.at[part, piece], to_ref.at[piece], sem.at[piece])
            for piece in range(to_ref.shape[0])
        ]

        def start_copies():
            for copy in copies:
                copy.start()

        def wait_copies():
            for copy in copies:
                copy.wait()

        if steps == 1:
            start_copies()
        else:
            pl.when(pl.program_id(0) == 0)(start_copies)
    chosen = of_side(info_ref.shape[0], bit, side)
    chunk, count = len(chosen), info_ref.shape[2]
    tiles = cell_ref.shape[1]
    cells = table_ref.shape[1] // 2
    info, cos, sin = start_turn(chosen, info_ref, start_ref)
    mask = segment_mask(info, cells, segment)
    both = []
    for ri in range(2):
        wide = []
        for place in range(chunk):
            wide += [cell_ref[place, :, ri * cells : (ri + 1) * cells]] * (count // tiles)
        both.append(jnp.where(mask, jnp.concatenate(wide, axis=0), 0.0))
    re, im = both
    value = [jnp.concatenate([re, -im], axis=1), jnp.concatenate([im, re], axis=1)]
    high, low = split(jnp.concatenate(value, axis=0), 2)
    first = dot(jnp.concatenate([high, low], axis=0), table_ref[0])
    total, rows = high.shape[0], chunk * count
    out = first[:total] + (first[total:] + dot(high, table_ref[1]))
    re, im = out[:rows], out[rows:]
    out_ref[:, :count] = (cos * re - sin * im).reshape(chunk, count, -1)
    out_ref[:, count:] = (cos * im + sin * re).reshape(chunk, count, -1)
    if part is not None:
        if steps == 1:
            wait_copies()
        else:
            pl.when(pl.program_id(0) == steps - 1)(wait_copies)


def adjoint_rows(value, info, start, table, segment, bit, side, large=None, part=None):
    half, tiles, lines = value.shape
    pairs, _, count, _ = info.shape
    width = table.shape[2]
    chunk = pairs if pairs <= 8 else 4
    steps = pairs // chunk
    more = large is not None
    return pl.pallas_call(
        lambda *refs: adjoint_kernel(segment, bit, side, part, steps, *refs),
        grid=() if steps == 1 else (steps,),
        in_specs=[
            blocks((chunk // 2, tiles, lines), lambda i: (i, 0, 0), steps),
            blocks((chunk, 1, count, FIELDS), lambda i: (i, 0, 0, 0), steps),
            resident(),
            resident(),
        ]
        + [in_hbm()] * more,
        out_specs=[blocks((chunk // 2, 2 * count, width), lambda i: (i, 0, 0), steps)]
        + [resident()] * more,
        out_shape=[jax.ShapeDtypeStruct((half, 2 * count, width), F32)]
        + ([jax.ShapeDtypeStruct(large.shape[1:], F32)] if more else []),
        scratch_shapes=[pltpu.SemaphoreType.DMA((large.shape[1],))] if more else [],
        compiler_params=params(24),
        name="adjoint_rows",
    )(
        value,
        info,
        start,
        table,
        *([pltpu.with_memory_space_constraint(large, pltpu.HBM)] if more else []),
    )


def tiles_kernel(coils, count_ref, norm_refs, weight_ref, *refs):
    tiles, _, cells = weight_ref.shape
    cell_refs, out_refs, sums_refs = refs[: 2 * coils], refs[2 * coils : 3 * coils], refs[3 * coils :]
    rows = []
    for keep, got in zip(cell_refs[::2], cell_refs[1::2]):
        grid = keep[...] + got[...]
        rows += [grid[:, ri * cells : (ri + 1) * cells] for ri in range(2)]
    found = []
    for tile in range(tiles):
        grid = jnp.concatenate([row[tile : tile + 1] for row in rows], axis=0).astype(BF16)
        found.append(
            lax.dot_general(
                grid, weight_ref[tile], (((1,), (1,)), ((), ())), preferred_element_type=F32
            )
        )
    spread = []
    for tile in range(tiles):
        live = lax.broadcasted_iota(jnp.int32, found[tile].shape, 1) < count_ref[tile]
        spread.append(dot(jnp.where(live, found[tile], 0.0).astype(BF16), weight_ref[tile]))
    total = 0.0
    for number, row in enumerate(rows):
        value = jnp.concatenate([piece[number : number + 1] for piece in spread], axis=0)
        total = total + row * value
        ri = number % 2
        out_refs[number // 2][:, ri * cells : (ri + 1) * cells] = value
    total = jnp.sum(total, keepdims=True)
    norm = norm_refs[0][...] + norm_refs[1][...]
    first = lax.broadcasted_iota(jnp.int32, norm.shape, 0) == 0
    norm = norm + jnp.where(first, 0.0, total)
    if sums_refs:
        sums_refs[0][...] = norm
    else:
        out_refs[-1][:, 2 * cells :] = jnp.concatenate([norm] * (tiles // norm.shape[0]), axis=0)


def run_tiles(count, norms, cells, weight, carry):
    coils = len(cells)
    tiles, lines = cells[0][0].shape
    shapes = [(tiles, lines + 128 * (carry and c == coils - 1)) for c in range(coils)]
    if not carry:
        shapes.append((8, 128))
    out = pl.pallas_call(
        lambda *refs: tiles_kernel(coils, refs[0], refs[1:3], *refs[3:]),
        in_specs=[scalars()] + [resident()] * (2 * coils + 3),
        out_specs=[resident()] * len(shapes),
        out_shape=[jax.ShapeDtypeStruct(shape, F32) for shape in shapes],
        compiler_params=params(8),
        name="tiles",
    )(count, *norms, weight, *[value for pair in cells for value in pair])
    return list(out[:coils]), list(out[coils:])


def turn_kernel(matrix_ref, out_ref):
    sides = out_ref.shape[1]
    rows = matrix_ref.shape[2] // sides
    for pair in range(matrix_ref.shape[0]):
        for side in range(sides):
            high, low = [
                matrix_ref[pair, part, side * rows : (side + 1) * rows].astype(F32) for part in range(2)
            ]
            value = jnp.concatenate([high, low, high], axis=0)
            out_ref[pair, side] = jnp.transpose(value).astype(BF16)


def transposed(matrix, sides):
    pairs, parts, rows, depth = matrix.shape
    step = min(pairs, 8)
    steps = pairs // step
    shape = (sides, depth, 3 * rows // sides)
    return pl.pallas_call(
        turn_kernel,
        grid=() if steps == 1 else (steps,),
        in_specs=[blocks((step, parts, rows, depth), lambda q: (q, 0, 0, 0), steps)],
        out_specs=blocks((step,) + shape, lambda q: (q, 0, 0, 0), steps),
        out_shape=jax.ShapeDtypeStruct((pairs,) + shape, BF16),
        compiler_params=params(12),
        name="transposed",
    )(matrix)


def back_rows(matrix, rows):
    high, low = split(rows, 2)
    return dot(matrix, jnp.concatenate([high, high, low], axis=0))


def back_group(odd, matrix, mine, got):
    first = back_rows(matrix(odd), jnp.where(odd == 0, mine, got))
    second = back_rows(matrix(1 - odd), jnp.where(odd == 0, got, mine))
    shape = (first.shape[0] // 8, 8, first.shape[1])
    first, second = first.reshape(shape), second.reshape(shape)
    low = low_half(shape)
    one = jnp.where(low, first, half_turn(second))
    two = jnp.where(low, half_turn(first), second)
    value = jnp.concatenate([one[:, None], two[:, None]], axis=1)
    return value.reshape(16 * shape[0], shape[2])


def combine(back, plane, step, sens_refs, dir_ref, res_ref, out_ref):
    coils, rows, _, width = sens_refs[0].shape
    planes = plane.stop - plane.start
    half = rows * planes
    total = [DAMPING * dir_ref[ri, :, plane].reshape(half, width) for ri in range(2)]
    for coil in range(coils):
        lanes = slice(coil * width, (coil + 1) * width)
        v_re, v_im = back[:half, lanes], back[half:, lanes]
        s_re, s_im = [ref[coil, :, plane].reshape(half, width) for ref in sens_refs]
        total[0] += s_re * v_re + s_im * v_im
        total[1] += s_re * v_im - s_im * v_re
    squares = 0.0
    for ri in range(2):
        value = res_ref[ri, :, plane].reshape(half, width) - step * total[ri]
        value = value.reshape(rows, planes, width)
        out_ref[ri, :, plane] = value
        squares = squares + jnp.sum(value * value, axis=0)
    return squares


def finish_kernel(planes, me_ref, sums_ref, re_ref, im_ref, dir_ref, res_ref, matrix_ref, *refs):
    coils, rows, total, width = re_ref.shape
    row_refs = refs[: 4 * coils]
    out_hbm, out_ref, norm_ref, sem = refs[4 * coils :]
    step = sums_ref[0:1, 0:1] / sums_ref[1:2, 0:1]
    squares = jnp.zeros((planes, width), F32)
    copies = []
    for group in range(total // planes):
        pair, odd = lax.bitwise_xor(group, me_ref[0] // 2), lax.rem(me_ref[0], 2)
        values = []
        for coil in range(coils):
            side, place = side_of(pair, coil % 2)
            for k in range(2):
                one, two = row_refs[4 * coil + k], row_refs[4 * coil + 2 + k]
                values.append(jnp.where(side == 0, one[place], two[place]))
        mine = jnp.concatenate(values[::2], axis=1)
        got = jnp.concatenate(values[1::2], axis=1)
        back = back_group(odd, lambda side: matrix_ref[pair, side], mine, got)
        plane = slice(group * planes, (group + 1) * planes)
        squares += combine(back, plane, step, (re_ref, im_ref), dir_ref, res_ref, out_ref)
        at = pl.ds(group * planes, planes)
        copies.append(
            pltpu.make_async_copy(out_ref.at[:, :, at], out_hbm.at[:, :, at], sem.at[group])
        )
        copies[-1].start()
    for copy in copies:
        copy.wait()
    norm_ref[...] = jnp.broadcast_to(jnp.sum(squares, keepdims=True), norm_ref.shape)


def finish(me, sums, rows, sens, direction, residual, matrix, planes):
    kept = jax.ShapeDtypeStruct(residual.shape, F32)
    return pl.pallas_call(
        lambda *refs: finish_kernel(planes, *refs),
        in_specs=[scalars()] + [resident()] * (6 + len(rows)),
        out_specs=[in_hbm(), resident(), resident()],
        out_shape=[kept, kept, jax.ShapeDtypeStruct(sums.shape, F32)],
        scratch_shapes=[pltpu.SemaphoreType.DMA((residual.shape[2] // planes,))],
        compiler_params=params(16),
        name="finish",
    )(me, sums, *sens, direction, residual, matrix, *rows)


def finish_deep_kernel(
    planes, me_ref, sums_ref, re_ref, im_ref, dir_ref, res_ref, matrix_ref, *refs
):
    coils = re_ref.shape[0]
    row_refs = refs[: 2 * coils]
    out_ref, norm_ref, squares_ref, sum_ref = refs[2 * coils :]
    group, pair = pl.program_id(0), pl.program_id(1)
    rows = [jnp.concatenate([ref[0] for ref in row_refs[k::2]], axis=1) for k in range(2)]
    back = back_rows(matrix_ref[0, 0], jnp.concatenate(rows, axis=0))

    @pl.when((group == 0) & (pair == 0))
    def _():
        squares_ref[...] = jnp.zeros(squares_ref.shape, F32)

    @pl.when(pair == 0)
    def _():
        sum_ref[...] = back

    @pl.when(pair > 0)
    def _():
        sum_ref[...] += back

    @pl.when(pair == pl.num_programs(1) - 1)
    def _():
        step = sums_ref[0:1, 0:1] / sums_ref[1:2, 0:1]
        squares_ref[...] += combine(
            sum_ref[...], slice(0, planes), step, (re_ref, im_ref), dir_ref, res_ref, out_ref
        )
        total = jnp.sum(squares_ref[...], keepdims=True)
        norm_ref[...] = jnp.broadcast_to(total, norm_ref.shape)


def finish_deep(me, sums, rows, sens, direction, residual, matrix, planes, slabs_group):
    coils, height, total, width = sens[0].shape
    double = rows[0].shape[1]
    groups, deep = total // planes, slabs_group // 2

    def pair(i, j, me):
        return lax.bitwise_xor(i, me[0] // slabs_group) * deep + j

    row_block = pl.BlockSpec((1, double, width), lambda i, j, me: (pair(i, j, me), 0, 0))
    image = pl.BlockSpec((2, height, planes, width), lambda i, j, me: (0, 0, i, 0))
    small = pl.BlockSpec(sums.shape, lambda i, j, me: (0, 0))
    out, norm = pl.pallas_call(
        lambda *refs: finish_deep_kernel(planes, *refs),
        grid_spec=pltpu.PrefetchScalarGridSpec(
            num_scalar_prefetch=1,
            grid=(groups, deep),
            in_specs=[
                small,
                pl.BlockSpec((coils, height, planes, width), lambda i, j, me: (0, 0, i, 0)),
                pl.BlockSpec((coils, height, planes, width), lambda i, j, me: (0, 0, i, 0)),
                image,
                image,
                pl.BlockSpec((1,) + matrix.shape[1:], lambda i, j, me: (pair(i, j, me), 0, 0, 0)),
            ]
            + [row_block] * len(rows),
            out_specs=[image, small],
            scratch_shapes=[
                pltpu.VMEM((planes, width), F32),
                pltpu.VMEM((2 * height * planes, coils * width), F32),
            ],
        ),
        out_shape=[
            jax.ShapeDtypeStruct(residual.shape, F32),
            jax.ShapeDtypeStruct(sums.shape, F32),
        ],
        compiler_params=params(32),
        name="finish_deep",
    )(me, sums, *sens, direction, residual, matrix, *rows)
    return out, out, norm


def swap(value, bit, slabs):
    return lax.ppermute(value, "slab", [(i, i ^ bit) for i in range(slabs)])


def sum_scatter(keep, send, bits, slabs):
    dims = keep.shape[1:]
    left = sorted(bits, reverse=True)
    for number, bit in enumerate(bits):
        axis = left.index(bit)
        left.pop(axis)
        if number > 0:
            value = (keep + got).reshape((2,) * (len(left) + 1) + dims)
            keep = lax.index_in_dim(value, 0, axis, keepdims=False)
            send = lax.index_in_dim(value, 1, axis, keepdims=False)
        got = swap(send, bit, slabs)
    return keep, got


def gather(value, bits, slabs):
    have = []
    for bit in bits:
        other = swap(value, bit, slabs)
        value = jnp.stack([value, other], axis=sum(1 for b in have if b > bit))
        have.append(bit)
    return value


def body(x_image, residual, direction, sensitivity, tile_block, tile_count, tile_weight):
    _, coils, rows, plane_count, ny = sensitivity.shape
    tiles, _, cells = tile_weight.shape
    slabs = lax.axis_size("slab")
    me = lax.axis_index("slab")
    lines = plane_count * GY // slabs
    segment = min(lines, GY)
    per_gx = lines // segment
    unit = math.gcd(cells, segment)
    segments = -(-(segment - unit + cells) // segment)
    planes = 8 if rows % 2 == 0 else 16
    slabs_group = planes * GY // lines
    own = planes // 2 if slabs_group == 2 else planes
    pairs = slabs // 2
    bits = [1 << i for i in range(slabs.bit_length() - 1)]

    first = tile_block * cells
    start = first % segment
    base = (me * lines) % GY
    info = []
    for k in range(segments):
        row = jnp.minimum(first // segment + k, GX * per_gx - 1)
        plane = (me * lines + (row % per_gx) * segment) // GY
        turn = (base + start - segment * k) % GY // unit
        fields = [row // per_gx, plane % own, turn, segment * k - start]
        info.append(jnp.stack(fields + [jnp.zeros_like(row)] * (FIELDS - len(fields)), axis=1))
    info = jnp.concatenate(info, axis=0)

    have = []
    for number, bit in enumerate(reversed(bits)):
        other = swap(info, bit, slabs)
        info = jnp.stack([info, other], axis=sum(1 for b in have if b > bit))
        have.append(bit)
    info = info.reshape(pairs, 2, segments * tiles, FIELDS)

    x_cos, x_sin = dft(np.arange(GX), np.repeat(np.arange(rows), own), GX)
    angle = (jnp.arange(GX, dtype=jnp.int32) * (me * rows) % GX).astype(F32) * (2 * math.pi / GX)
    turn_cos, turn_sin = jnp.cos(angle)[:, None], jnp.sin(angle)[:, None]
    x_upper = jnp.asarray(np.hstack([x_cos, x_sin]).astype(np.float32))
    x_lower = jnp.asarray(np.hstack([-x_sin, x_cos]).astype(np.float32))
    x_table = jnp.stack(
        [x_upper * turn_cos + x_lower * turn_sin, x_lower * turn_cos - x_upper * turn_sin]
    )
    x_parts = []
    for _ in range(3):
        part = lax.reduce_precision(x_table, 8, 7)
        x_parts.append(part.astype(BF16))
        x_table = x_table - part
    x_table = jnp.stack(x_parts)
    y_cos, y_sin = dft(np.arange(ny), np.arange(cells), GY)
    y_forward = jnp.asarray(table_parts(np.vstack([y_cos, y_sin]), 3))
    y_back = jnp.asarray(table_parts(np.vstack([y_cos.T, y_sin.T]), 2))
    start_table = np.hstack(dft(np.arange(GY // unit) * unit, np.arange(ny), GY, False))
    start_table = np.pad(start_table, ((0, -start_table.shape[0] % 8), (0, 0)))
    start_table = jnp.asarray(start_table.astype(np.float32))
    me_array = me.astype(jnp.int32)[None]

    keep, send, x_matrix, norm = partial_rows(
        me_array, info, sensitivity, direction, x_table, planes, slabs_group
    )
    got = [swap(value, 1, slabs) for value in send]
    grid = []
    for c in range(coils):
        send, stay = [
            row_cells(keep[c], got[c], info, start_table, y_forward, tiles, segment, c % 2, side)
            for side in (1, 0)
        ]
        grid.append([stay, send])
    grid[-1][0], x_matrix, residual = lax.optimization_barrier((grid[-1][0], x_matrix, residual))
    x_matrix = transposed(x_matrix, planes // own)
    norms = [norm, squares(residual)]
    high_bits = bits[1:]
    orders = [high_bits[c % 2 :] + high_bits[: c % 2] for c in range(coils)]
    grid = [sum_scatter(*value, order, slabs) for value, order in zip(grid, orders)]
    grid[-1], x_matrix, norms = lax.optimization_barrier((grid[-1], x_matrix, norms))

    spread, sums = run_tiles(tile_count, norms, grid, tile_weight, False)
    rows_back, sens, loaded, inputs = [], [], [], [direction, residual]
    dims = [value.shape for value in spread]
    orders = [high_bits[c % 2 :] + high_bits[: c % 2] for c in range(coils)]
    have = [[] for _ in range(coils)]
    for number in range(len(high_bits)):
        ways = [order[-1 - number] for order in orders]
        other = [swap(value, bit, slabs) for value, bit in zip(spread, ways)]
        if not False:
            sums = [sums[0] + swap(sums[0], high_bits[-1 - number], slabs)]
        if number == 1:
            loaded += [load(value) for value in inputs]
        if number == len(high_bits) - 1:
            for c in range(coils):
                had = spread[c].reshape((-1,) + dims[c])
                mine, part = adjoint_rows(
                    had, info, start_table, y_back, segment, c % 2, 0, sensitivity, c
                )
                sens.append(part)
                rows_back.append([mine, swap(mine, 1, slabs)])
        else:
            for c in range(coils):
                axis = sum(1 for b in have[c] if b > ways[c])
                spread[c] = jnp.stack([spread[c], other[c]], axis=axis)
                have[c].append(ways[c])
        spread, other, sums, loaded, inputs = lax.optimization_barrier((spread, other, sums, loaded, inputs))
    for c in range(coils):
        got = other[c].reshape((-1,) + dims[c])
        (mine,) = adjoint_rows(got, info, start_table, y_back, segment, c % 2, 1)
        rows_back[c] += [mine, swap(mine, 1, slabs)]
    sums = sums[0] + swap(sums[0], 1, slabs)
    move, residual = loaded
    if slabs_group == 2:
        rows_back = [value for values in rows_back for value in values]
    else:
        both = []
        for c, (one, near_one, two, near_two) in enumerate(rows_back):
            shape = (pairs >> (c % 2 + 1), 1 << (c % 2)) + one.shape[1:]
            for had, got in ((one, two), (near_one, near_two)):
                value = jnp.stack([had.reshape(shape), got.reshape(shape)], axis=1)
                both.append(value.reshape((pairs,) + one.shape[1:]))
        rows_back = both
    if slabs_group == 2:
        residual_next, res, norm = finish(
            me_array, sums, rows_back, sens, move, residual, x_matrix, planes
        )
    else:
        residual_next, res, norm = finish_deep(
            me_array, sums, rows_back, sens, move, residual, x_matrix, planes, slabs_group
        )

    pieces = 3
    x_next = None
    for number, bit in enumerate(reversed(bits)):
        norm, x_image = lax.optimization_barrier((norm, x_image))
        other = swap(norm, bit, slabs)
        if number < pieces:
            x_next = x_update(sums, x_image, move, number, pieces, x_next)
            x_next, x_image = lax.optimization_barrier((x_next, x_image))
        if bit > 1:
            norm, x_next = lax.optimization_barrier((norm + other, x_next))
    direction_next = direction_update(sums, norm, other, res, move)
    return (x_next, residual_next, direction_next)


def solution(mesh):
    image = P(None, "slab", "frames", None)
    placed = (image, image, image, P(None, None, "slab", None, None)) + (
        P("slab"),
        P("slab"),
        P("slab", None, None),
    )
    return jax.shard_map(
        body, mesh=mesh, in_specs=placed, out_specs=(image, image, image), check_vma=False
    )
```
